128 devices in a mesh: seq: 32 (over z, x, y_hi), ffn: 4 (over y_lo, core).
Axes of the slice: x: 4, y: 4 (y_hi: 2, y_lo: 2; y = y_hi * 2 + y_lo), z: 4, core: 2. Of those that a mesh axis runs over, the one named last changes fastest.
Arguments:
- hidden_in: bfloat16 [4, 2048, 2048], P(None, 'seq'), may hold values from -6 to 6
- cotangent: bfloat16 [4, 2048, 2048], P(None, ('seq', 'ffn')), may hold values from -6 to 6
- doc_lengths: int32 [4, 8], replicated, may hold values from 0 to 2048, as said below
- inward: float32 [2048, 3, 2048], P('seq', None, 'ffn'), may hold values from -0.125 to 0.125
- inward_moment: float32 [2048, 3, 2048], P('seq', None, 'ffn'), may hold values from -0.00024414062 to 0.00024414062
- inward_squares: float32 [2048, 3, 2048], P('seq', None, 'ffn'), may hold values from 9.934108e-10 to 3.973643e-09
- outward: float32 [2048, 2048], P('ffn', 'seq'), may hold values from -0.125 to 0.125
- outward_moment: float32 [2048, 2048], P('ffn', 'seq'), may hold values from -0.00024414062 to 0.00024414062
- outward_squares: float32 [2048, 2048], P('ffn', 'seq'), may hold values from 9.934108e-10 to 3.973643e-09
- upward: float32 [2048, 4, 2048], P('seq', None, 'ffn'), may hold values from -0.125 to 0.125
- upward_moment: float32 [2048, 4, 2048], P('seq', None, 'ffn'), may hold values from -0.00024414062 to 0.00024414062
- upward_squares: float32 [2048, 4, 2048], P('seq', None, 'ffn'), may hold values from 9.934108e-10 to 3.973643e-09
- downward: float32 [4, 2048, 2048], P(None, 'ffn', 'seq'), may hold values from -0.0625 to 0.0625
- downward_moment: float32 [4, 2048, 2048], P(None, 'ffn', 'seq'), may hold values from -0.00024414062 to 0.00024414062
- downward_squares: float32 [4, 2048, 2048], P(None, 'ffn', 'seq'), may hold values from 9.934108e-10 to 3.973643e-09
- prenorm: float32 [4, 2048], replicated, may hold values from -0.9 to 2.5
- prenorm_moment: float32 [4, 2048], replicated, may hold values from -0.00024414062 to 0.00024414062
- prenorm_squares: float32 [4, 2048], replicated, may hold values from 9.934108e-10 to 3.973643e-09
- subnorm: float32 [2, 5, 2048], P(None, None, 'ffn'), may hold values from -0.9 to 2.5
- subnorm_moment: float32 [2, 5, 2048], P(None, None, 'ffn'), may hold values from -0.00024414062 to 0.00024414062
- subnorm_squares: float32 [2, 5, 2048], P(None, None, 'ffn'), may hold values from 9.934108e-10 to 3.973643e-09
Outputs:
- hidden_out: bfloat16 [4, 2048, 2048], P(None, ('seq', 'ffn'))
- input_grad: bfloat16 [4, 2048, 2048], P(None, 'seq')
- updated_inward: float32 [2048, 3, 2048], P('seq', None, 'ffn')
- moment_inward: float32 [2048, 3, 2048], P('seq', None, 'ffn')
- squares_inward: float32 [2048, 3, 2048], P('seq', None, 'ffn')
- updated_outward: float32 [2048, 2048], P('ffn', 'seq')
- moment_outward: float32 [2048, 2048], P('ffn', 'seq')
- squares_outward: float32 [2048, 2048], P('ffn', 'seq')
- updated_upward: float32 [2048, 4, 2048], P('seq', None, 'ffn')
- moment_upward: float32 [2048, 4, 2048], P('seq', None, 'ffn')
- squares_upward: float32 [2048, 4, 2048], P('seq', None, 'ffn')
- updated_downward: float32 [4, 2048, 2048], P(None, 'ffn', 'seq')
- moment_downward: float32 [4, 2048, 2048], P(None, 'ffn', 'seq')
- squares_downward: float32 [4, 2048, 2048], P(None, 'ffn', 'seq')
- updated_prenorm: float32 [4, 2048], replicated
- moment_prenorm: float32 [4, 2048], replicated
- squares_prenorm: float32 [4, 2048], replicated
- updated_subnorm: float32 [2, 5, 2048], P(None, None, 'ffn')
- moment_subnorm: float32 [2, 5, 2048], P(None, None, 'ffn')
- squares_subnorm: float32 [2, 5, 2048], P(None, None, 'ffn')
- grad_norm: float32 [], replicated
The draws below stay inside these ranges and needn't reach their ends.
Inputs may be any that keep to these rules, and one draw needn't show every extreme that they name: `doc_lengths`: each row holds whole documents from its first slot on, in order; a 0 marks an unused entry and all entries after it are 0; every other entry is at least 100; a row's lengths sum to at most 2048, the rest of the row being padding. In each micro-batch of 2 consecutive rows one row is a single document of 2048 tokens.
All inputs are finite; a program needn't handle non-finite values.
Results may differ from the reference program's by a relative error of at most 0.035.
Values may be sent and summed in bfloat16 or wider, within the bound.
No kernel may reach another device: no remote copies, remote signals or barrier semaphores. Data moves between devices by JAX's collectives and lax.ppermute only.
A program may use at most 256 MiB of HBM per device.

```python
import math
import jax
import jax.numpy as jnp
from jax import lax

D = 2048
HEADS = 32
HDIM = 64
FF = 8192
SLOTS = 2048
NDOC = 8
MINLEN = 100
RMB = 2
MB = 2
STEP = 10
ROWS = 4


def draw_doc_lengths(key, part):
    key = jax.random.fold_in(key, 11)
    key_level, key_extra, key_pick = jax.random.split(key, 3)
    levels = jax.random.randint(key_level, (ROWS, NDOC), 0, 6)
    span_top = jnp.maximum((SLOTS - MINLEN) // jnp.left_shift(1, levels), 1)
    extra_len = jax.random.randint(key_extra, (ROWS, NDOC), 0, span_top + 1)
    lengths = MINLEN + extra_len
    doc_ends = jnp.cumsum(lengths, axis=1)
    lengths = jnp.where(doc_ends <= SLOTS, lengths, 0)
    chosen = jax.random.randint(key_pick, (MB,), 0, RMB)
    whole_row = jnp.arange(ROWS) % RMB == jnp.repeat(chosen, RMB)
    single = jnp.zeros((NDOC,), jnp.int32).at[0].set(SLOTS)
    return jnp.where(whole_row[:, None], single[None, :], lengths).astype(jnp.int32)


def draw_prenorm(key, part):
    key = jax.random.fold_in(key, 21)
    key_gain, key_shift = jax.random.split(key)
    ramp_up = jnp.arange(D, dtype=jnp.float32) / (D - 1)
    gain_rows = 0.5 * (1.0 + 2.0 * ramp_up)[None, :] * jnp.exp(jax.random.uniform(key_gain, (2, D), jnp.float32, -0.22, 0.22))
    shift_rows = 0.3 * jnp.clip(jax.random.normal(key_shift, (2, D), jnp.float32), -3.0, 3.0)
    return jnp.stack([gain_rows[0], shift_rows[0], gain_rows[1], shift_rows[1]])


def draw_subnorm(key, part):
    key = jax.random.fold_in(key, 31)
    key_gain, key_shift = jax.random.split(key)
    ramp_up = jnp.arange(D, dtype=jnp.float32) / (D - 1)
    gain_rows = 0.5 * (1.0 + 2.0 * ramp_up)[None, :] * jnp.exp(jax.random.uniform(key_gain, (5, D), jnp.float32, -0.22, 0.22))
    shift_rows = 0.3 * jnp.clip(jax.random.normal(key_shift, (5, D), jnp.float32), -3.0, 3.0)
    return jnp.stack([gain_rows, shift_rows])


def level_of(key, shape, cuts, least, top_value):
    level, own = 1.0, jax.random.fold_in(key, 6)
    for position, parts in cuts:
        steps = jnp.exp(jax.random.uniform(jax.random.fold_in(own, position), (parts,), jnp.float32, least / len(cuts), top_value / len(cuts)))
        level = level * jnp.repeat(steps, shape[position] // parts).reshape([-1 if axis == position else 1 for axis in range(len(shape))])
    return level


def scatter_about(stream_key, dims, scale, limit, shards=(), kind=jnp.bfloat16):
    entries = scale * jax.random.normal(stream_key, dims, jnp.float32)
    if shards:
        entries = entries * level_of(stream_key, dims, shards, -0.22, 0.18)
    return jnp.clip(entries, -limit, limit).astype(kind)


def setup_inputs(seed: int = 0) -> dict:
    seeds = jax.random.split(jax.random.key(seed), 22)
    hidden_in = scatter_about(seeds[0], (ROWS, SLOTS, D), 1.0, 6.0, ((1, 32),))
    cotangent = scatter_about(seeds[1], (ROWS, SLOTS, D), 1.0, 6.0, ((1, 128),))
    doc_lengths = draw_doc_lengths(jax.random.fold_in(seeds[21], 71), 0)
    inward = scatter_about(seeds[3], (D, 3, D), D ** -0.5, 0.125, ((0, 32), (2, 4)), jnp.float32)
    inward_moment = scatter_about(seeds[4], (D, 3, D), (0.11 / (12 * D * D) ** 0.5), 0.00024414062, ((0, 32), (2, 4)), jnp.float32)
    inward_squares = jnp.clip(jnp.exp(math.log(3.973643192267673e-09) - 1.3862944 * jax.random.uniform(seeds[5], (D, 3, D), jnp.float32) ** level_of(seeds[5], (D, 3, D), ((0, 32), (2, 4)), -0.2, 0.2)), 9.934107980669182e-10, 3.973643192267673e-09)
    outward = scatter_about(seeds[6], (D, D), D ** -0.5, 0.125, ((0, 4), (1, 32)), jnp.float32)
    outward_moment = scatter_about(seeds[7], (D, D), (0.11 / (12 * D * D) ** 0.5), 0.00024414062, ((0, 4), (1, 32)), jnp.float32)
    outward_squares = jnp.clip(jnp.exp(math.log(3.973643192267673e-09) - 1.3862944 * jax.random.uniform(seeds[8], (D, D), jnp.float32) ** level_of(seeds[8], (D, D), ((0, 4), (1, 32)), -0.2, 0.2)), 9.934107980669182e-10, 3.973643192267673e-09)
    upward = scatter_about(seeds[9], (D, 4, D), D ** -0.5, 0.125, ((0, 32), (2, 4)), jnp.float32)
    upward_moment = scatter_about(seeds[10], (D, 4, D), (0.11 / (12 * D * D) ** 0.5), 0.00024414062, ((0, 32), (2, 4)), jnp.float32)
    upward_squares = jnp.clip(jnp.exp(math.log(3.973643192267673e-09) - 1.3862944 * jax.random.uniform(seeds[11], (D, 4, D), jnp.float32) ** level_of(seeds[11], (D, 4, D), ((0, 32), (2, 4)), -0.2, 0.2)), 9.934107980669182e-10, 3.973643192267673e-09)
    downward = scatter_about(seeds[12], (4, D, D), FF ** -0.5, 0.0625, ((1, 4), (2, 32)), jnp.float32)
    downward_moment = scatter_about(seeds[13], (4, D, D), (0.11 / (12 * D * D) ** 0.5), 0.00024414062, ((1, 4), (2, 32)), jnp.float32)
    downward_squares = jnp.clip(jnp.exp(math.log(3.973643192267673e-09) - 1.3862944 * jax.random.uniform(seeds[14], (4, D, D), jnp.float32) ** level_of(seeds[14], (4, D, D), ((1, 4), (2, 32)), -0.2, 0.2)), 9.934107980669182e-10, 3.973643192267673e-09)
    prenorm = draw_prenorm(jax.random.fold_in(seeds[21], 71), 0)
    prenorm_moment = scatter_about(seeds[16], (4, D), (0.11 / (12 * D * D) ** 0.5), 0.00024414062, (), jnp.float32)
    prenorm_squares = jnp.clip(jnp.exp(jax.random.uniform(seeds[17], (4, D), jnp.float32, math.log(9.934107980669182e-10), math.log(3.973643192267673e-09))), 9.934107980669182e-10, 3.973643192267673e-09)
    subnorm = draw_subnorm(jax.random.fold_in(seeds[21], 71), 0)
    subnorm_moment = scatter_about(seeds[19], (2, 5, D), (0.11 / (12 * D * D) ** 0.5), 0.00024414062, ((2, 4),), jnp.float32)
    subnorm_squares = jnp.clip(jnp.exp(math.log(3.973643192267673e-09) - 1.3862944 * jax.random.uniform(seeds[20], (2, 5, D), jnp.float32) ** level_of(seeds[20], (2, 5, D), ((2, 4),), -0.2, 0.2)), 9.934107980669182e-10, 3.973643192267673e-09)
    return dict(hidden_in=hidden_in, cotangent=cotangent, doc_lengths=doc_lengths, inward=inward, inward_moment=inward_moment, inward_squares=inward_squares, outward=outward, outward_moment=outward_moment, outward_squares=outward_squares, upward=upward, upward_moment=upward_moment, upward_squares=upward_squares, downward=downward, downward_moment=downward_moment, downward_squares=downward_squares, prenorm=prenorm, prenorm_moment=prenorm_moment, prenorm_squares=prenorm_squares, subnorm=subnorm, subnorm_moment=subnorm_moment, subnorm_squares=subnorm_squares)


@jax.custom_vjp
def low(v):
    return lax.optimization_barrier(v.astype(jnp.bfloat16)).astype(jnp.float32)

@jax.custom_vjp
def low_back(v):
    return v

def low_keep(v):
    return (low(v), None)

def low_pass(kept, grad):
    return (grad,)

def back_keep(v):
    return (v, None)

def back_low(kept, grad):
    return (low(grad),)
low.defvjp(low_keep, low_pass)
low_back.defvjp(back_keep, back_low)
norm_eps = 1e-05
rope_base = 10000.0
xpos_base = 512.0
clip_limit = 1.0
beta_first = 0.9
beta_second = 0.95
adam_eps = 1e-08
decay_rate = 0.1
matrix_rate = 0.04
norm_rate = 0.6
masked_score = -1e+30
highest = lax.Precision.HIGHEST

def layout_rows(doc_lengths, row_slots):
    doc_ends = jnp.cumsum(doc_lengths, axis=1)
    places = jnp.arange(row_slots, dtype=jnp.int32)
    segment = lax.optimization_barrier(jnp.sum((places[None, :, None] >= doc_ends[:, None, :]).astype(jnp.int32), axis=2))
    usable = (places[None, :] < doc_ends[:, -1:]).astype(jnp.float32)
    return (segment, usable)

def xpos_rotate(values, places, direction):
    head_dim = values.shape[-1]
    half_dim = head_dim // 2
    index_half = jnp.arange(half_dim, dtype=jnp.float32)
    inverse = jnp.power(rope_base, -2.0 * index_half / head_dim)
    angles = places[:, None] * inverse[None, :]
    zeta_base = (2.0 * index_half + 0.4 * head_dim) / (1.4 * head_dim)
    stretch = jnp.power(zeta_base[None, :], direction * places[:, None] / xpos_base)
    cosine = (jnp.cos(angles) * stretch)[:, None, :]
    sine_part = (jnp.sin(angles) * stretch)[:, None, :]
    front_half = values[..., :half_dim]
    back_part = values[..., half_dim:]
    return jnp.concatenate([front_half * cosine - back_part * sine_part, front_half * sine_part + back_part * cosine], axis=-1)

def plain_norm(values, norm_gain, norm_shift):
    center = lax.optimization_barrier(jnp.mean(values, axis=-1, keepdims=True))
    spread = lax.optimization_barrier(jnp.mean(jnp.square(values - center), axis=-1, keepdims=True))
    return (values - center) * lax.rsqrt(spread + norm_eps) * norm_gain + norm_shift

def adam_update(weight, moment, squares, gradient, factor, step_rate, decay_weight):
    clipped = gradient * factor
    moment_new = beta_first * moment + (1.0 - beta_first) * clipped
    squares_new = beta_second * squares + (1.0 - beta_second) * clipped * clipped
    moment_hat = moment_new / (1.0 - beta_first ** STEP)
    squares_hat = squares_new / (1.0 - beta_second ** STEP)
    updated = weight - step_rate * (moment_hat / (jnp.sqrt(squares_hat) + adam_eps) + decay_weight * weight)
    return (updated, moment_new, squares_new)

def reference(hidden_in, cotangent, doc_lengths, inward, inward_moment, inward_squares, outward, outward_moment, outward_squares, upward, upward_moment, upward_squares, downward, downward_moment, downward_squares, prenorm, prenorm_moment, prenorm_squares, subnorm, subnorm_moment, subnorm_squares):
    segment, usable = layout_rows(doc_lengths, SLOTS)
    places = jnp.arange(SLOTS, dtype=jnp.int32)
    offsets = (places - SLOTS // 2).astype(jnp.float32)
    block_rows = min(512, SLOTS)
    block_count = SLOTS // block_rows
    score_scale = 1.0 / math.sqrt(HDIM)

    def row_forward(params, row_hidden, row_segment, row_usable):
        inward_w, outward_w, upward_w, downward_w, prenorm_w, subnorm_w = params
        normed_one = low(plain_norm(row_hidden, prenorm_w[0], prenorm_w[1]))
        project = low_back(jnp.einsum('td,dke->tke', normed_one, low(inward_w), precision=highest))
        head_shape = (SLOTS, HEADS, HDIM)
        queries = low(xpos_rotate(project[:, 0].reshape(head_shape), offsets, 1.0))
        key_rows = low(xpos_rotate(project[:, 1].reshape(head_shape), offsets, -1.0))
        value_rows = low(project[:, 2].reshape(head_shape))

        def attend(bundle):
            block_query, block_segment, block_places = bundle
            scores = low_back(jnp.einsum('qhe,khe->hqk', block_query, key_rows, precision=highest) * score_scale)
            allowed = (places[None, :] <= block_places[:, None]) & (block_segment[:, None] == row_segment[None, :])
            scores = jnp.where(allowed[None], scores, masked_score)
            peak_score = lax.optimization_barrier(jnp.max(scores, axis=-1, keepdims=True))
            exponent = jnp.exp(scores - peak_score)
            chances = low(exponent / lax.optimization_barrier(jnp.sum(exponent, axis=-1, keepdims=True)))
            return jnp.einsum('hqk,khe->qhe', chances, value_rows, precision=highest)
        attended = lax.map(jax.checkpoint(attend), (queries.reshape(block_count, block_rows, HEADS, HDIM), row_segment.reshape(block_count, block_rows), places.reshape(block_count, block_rows)))
        attended = low_back(attended.reshape(SLOTS, HEADS * HDIM))
        mixed_low = low(plain_norm(attended, subnorm_w[0, 0], subnorm_w[1, 0]))
        branch = low_back(jnp.dot(mixed_low, low(outward_w), precision=highest))
        first_sum = row_hidden + row_usable[:, None] * branch
        middle = low(plain_norm(first_sum, prenorm_w[2], prenorm_w[3]))
        upper_proj = low_back(jnp.dot(middle, low(upward_w.reshape(D, FF)), precision=highest))
        activated = jax.nn.gelu(upper_proj, approximate=False)
        inner_low = low(plain_norm(activated, subnorm_w[0, 1:].reshape(FF), subnorm_w[1, 1:].reshape(FF)))
        lowered = low_back(jnp.dot(inner_low, low(downward_w.reshape(FF, D)), precision=highest))
        return first_sum + row_usable[:, None] * lowered

    def whole_layer(params, hidden):

        def row_step(bundle):
            return row_forward(params, bundle[0], bundle[1], bundle[2])
        return lax.map(jax.checkpoint(row_step), (hidden, segment, usable))
    params = (inward, outward, upward, downward, prenorm, subnorm)
    forward_out, pullback = jax.vjp(whole_layer, params, hidden_in.astype(jnp.float32))
    param_grads, grad_hidden = pullback(cotangent.astype(jnp.float32))
    squares_total = sum((jnp.sum(gradient * gradient) for gradient in param_grads))
    grad_norm = jnp.sqrt(squares_total)
    factor = jnp.minimum(1.0, clip_limit / (grad_norm + 1e-06))
    updated_inward, moment_inward, squares_inward = adam_update(inward, inward_moment, inward_squares, param_grads[0], factor, matrix_rate, decay_rate)
    updated_outward, moment_outward, squares_outward = adam_update(outward, outward_moment, outward_squares, param_grads[1], factor, matrix_rate, decay_rate)
    updated_upward, moment_upward, squares_upward = adam_update(upward, upward_moment, upward_squares, param_grads[2], factor, matrix_rate, decay_rate)
    updated_downward, moment_downward, squares_downward = adam_update(downward, downward_moment, downward_squares, param_grads[3], factor, matrix_rate, decay_rate)
    updated_prenorm, moment_prenorm, squares_prenorm = adam_update(prenorm, prenorm_moment, prenorm_squares, param_grads[4], factor, norm_rate, 0.0)
    updated_subnorm, moment_subnorm, squares_subnorm = adam_update(subnorm, subnorm_moment, subnorm_squares, param_grads[5], factor, norm_rate, 0.0)
    return (forward_out.astype(jnp.bfloat16), grad_hidden.astype(jnp.bfloat16), updated_inward, moment_inward, squares_inward, updated_outward, moment_outward, squares_outward, updated_upward, moment_upward, squares_upward, updated_downward, moment_downward, squares_downward, updated_prenorm, moment_prenorm, squares_prenorm, updated_subnorm, moment_subnorm, squares_subnorm, grad_norm)
```

```python
import functools
import math

import jax
import jax.numpy as jnp
import numpy as np
from jax import lax
from jax.experimental import pallas as pl
from jax.experimental.pallas import tpu as pltpu
from jax.sharding import Mesh
from jax.sharding import PartitionSpec as P

HDIM = 64
HALF = 32
FF = 8192
STEP = 10
Z, X, YH, YL, C = "seq_0", "seq_1", "seq_2", "ffn_0", "ffn_1"
FFN = (YL, C)
SEQ = (Z, X, YH)
SEQ_FFN = (Z, X, YH, YL, C)
ZX = (Z, X)
YY = (YH, YL)
EIGHT = (YH, YL, C)
TILE = 256

norm_eps = 1e-05
rope_base = 10000.0
xpos_base = 512.0
clip_limit = 1.0
beta_first = 0.9
beta_second = 0.95
adam_eps = 1e-08
decay_rate = 0.1
matrix_rate = 0.04
norm_rate = 0.6

F32 = jnp.float32
BF16 = jnp.bfloat16
SWAP = [(0, 1), (1, 0)]


def xor_pairs(count, k):
    return [(i, i ^ k) for i in range(count)]


def dot(a, b, da, db):
    return lax.dot_general(a, b, (((da,), (db,)), ((), ())), preferred_element_type=F32)


def eight_parts(own):
    lines = [own] + [lax.ppermute(own, YY, xor_pairs(4, k)) for k in (1, 2, 3)]
    parts = []
    for line in lines:
        parts += [line, lax.ppermute(line, C, SWAP)]
    return parts


def eight_gather(own):
    return jnp.concatenate(eight_parts(own), axis=0)


def eight_scatter(partial):
    tokens, width = partial.shape
    share = tokens // 8
    low = partial.astype(BF16).reshape(4, 2, share, width)
    got = lax.ppermute(low[:, 1], C, SWAP)
    both = partial.reshape(4, 2, share, width)[:, 0] + got.astype(F32)
    total = both[0]
    sent = both.astype(BF16)
    for k in (1, 2, 3):
        total = total + lax.ppermute(sent[k], YY, xor_pairs(4, k)).astype(F32)
    return total


def copies_of(shard, axis):
    copies = jnp.broadcast_to(shard, (lax.axis_size(axis), *shard.shape))
    return lax.all_to_all(copies, axis, split_axis=0, concat_axis=0, tiled=True)


def share_order(sums):
    shares = sums.reshape(sums.shape[0], 2, 2, 2, -1)
    for axis, name in ((1, YH), (2, YL), (3, C)):
        shares = jnp.where(lax.axis_index(name) == 0, shares, jnp.flip(shares, axis))
    return shares.reshape(sums.shape)


def eight_sum(sums):
    return share_order(jnp.sum(copies_of(share_order(sums), EIGHT), axis=0))


def turned(tile):
    return jnp.transpose(tile.astype(F32)).astype(BF16)


def forward_kernel(qkv_ref, start_ref, out_ref, top_ref, q_s, k_s, v_s, s_s):
    blocks = q_s.shape[0]
    pieces = TILE // 128
    for i in range(blocks):
        for j in range(pieces):
            part = slice(j * 128, (j + 1) * 128)
            q_s[i, :, part] = qkv_ref[i * pieces + j, 0]
            k_s[i, part, :] = turned(qkv_ref[i * pieces + j, 1])
            v_s[i, :, part] = qkv_ref[i * pieces + j, 2]
    factor = math.log2(math.e) / math.sqrt(HDIM)
    key_line = lax.broadcasted_iota(jnp.int32, (TILE, TILE), 0)
    query_line = lax.broadcasted_iota(jnp.int32, (TILE, TILE), 1)
    for i in range(blocks):
        query = q_s[i]
        begin = start_ref[:, i * TILE : (i + 1) * TILE]
        peak = None
        for b in range(i + 1):
            s = dot(k_s[b], query, 1, 0) * factor
            keep = key_line >= begin - b * TILE
            if b == i:
                keep = keep & (key_line <= query_line)
            s = jnp.where(keep, s, -1e30)
            s_s[b] = s
            high = jnp.max(s, axis=0, keepdims=True)
            peak = high if peak is None else jnp.maximum(peak, high)
        total = jnp.zeros((1, TILE), F32)
        acc = jnp.zeros((HDIM, TILE), F32)
        for b in range(i + 1):
            e = jnp.exp2(s_s[b] - peak)
            total = total + jnp.sum(e, axis=0, keepdims=True)
            acc = acc + dot(v_s[b], e.astype(BF16), 1, 0)
        out = acc / total
        for j in range(pieces):
            out_ref[i * pieces + j] = out[:, j * 128 : (j + 1) * 128]
        top_ref[:, i * TILE : (i + 1) * TILE] = peak + jnp.log2(total)


def backward_kernel(
    qkv_ref, do_ref, o_ref, top_ref, start_ref, rot_ref, out_ref,
    qt_s, kt_s, dot_s, q_s, k_s, v_s, do_s, dq_s, dk_s, dv_s,
):
    blocks = qt_s.shape[0]
    pieces = TILE // 128
    for i in range(blocks):
        for j in range(pieces):
            part = slice(j * 128, (j + 1) * 128)
            c = i * pieces + j
            qt_s[i, :, part] = qkv_ref[c, 0]
            kt_s[i, :, part] = qkv_ref[c, 1]
            dot_s[i, :, part] = do_ref[c]
            q_s[i, part, :] = turned(qkv_ref[c, 0])
            k_s[i, part, :] = turned(qkv_ref[c, 1])
            v_s[i, part, :] = turned(qkv_ref[c, 2])
            do_s[i, part, :] = turned(do_ref[c])
    scale = 1.0 / math.sqrt(HDIM)
    factor = math.log2(math.e) * scale
    key_line = lax.broadcasted_iota(jnp.int32, (TILE, TILE), 0)
    query_line = lax.broadcasted_iota(jnp.int32, (TILE, TILE), 1)
    for i in range(blocks):
        span = slice(i * TILE, (i + 1) * TILE)
        begin = start_ref[:, span]
        top = top_ref[:, span]
        delta = jnp.concatenate(
            [
                jnp.sum(
                    do_ref[i * pieces + j].astype(F32) * o_ref[i * pieces + j],
                    axis=0,
                    keepdims=True,
                )
                for j in range(pieces)
            ],
            axis=1,
        )
        dq = jnp.zeros((HDIM, TILE), F32)
        for b in range(i + 1):
            s = dot(k_s[b], qt_s[i], 1, 0) * factor
            keep = key_line >= begin - b * TILE
            if b == i:
                keep = keep & (key_line <= query_line)
            p = jnp.where(keep, jnp.exp2(s - top), 0.0)
            dp = dot(v_s[b], dot_s[i], 1, 0)
            ds = (p * (dp - delta)).astype(BF16)
            dq = dq + dot(kt_s[b], ds, 1, 0)
            dk = dot(ds, q_s[i], 1, 0)
            dv = dot(p.astype(BF16), do_s[i], 1, 0)
            if b == i:
                dk_s[b] = dk
                dv_s[b] = dv
            else:
                dk_s[b] += dk
                dv_s[b] += dv
        dq_s[i] = dq
    for i in range(blocks):
        span = slice(i * TILE, (i + 1) * TILE)
        dq = dq_s[i] * scale
        dk = jnp.transpose(dk_s[i]) * scale
        dv = jnp.transpose(dv_s[i])
        results = []
        for n, g in enumerate((dq, dk)):
            co, si = rot_ref[2 * n, :, span], rot_ref[2 * n + 1, :, span]
            front, back = g[:HALF], g[HALF:]
            results.append(
                jnp.concatenate([front * co + back * si, back * co - front * si], axis=0)
            )
        results.append(dv)
        for n, g in enumerate(results):
            for j in range(pieces):
                out_ref[i * pieces + j, n] = g[:, j * 128 : (j + 1) * 128].astype(BF16)


def attend(qkv, start):
    count = qkv.shape[0]
    blocks = count * 128 // TILE
    return pl.pallas_call(
        forward_kernel,
        out_shape=(
            jax.ShapeDtypeStruct((count, HDIM, 128), F32),
            jax.ShapeDtypeStruct((1, count * 128), F32),
        ),
        scratch_shapes=[
            pltpu.VMEM((blocks, HDIM, TILE), BF16),
            pltpu.VMEM((blocks, TILE, HDIM), BF16),
            pltpu.VMEM((blocks, HDIM, TILE), BF16),
            pltpu.VMEM((blocks, TILE, TILE), F32),
        ],
        compiler_params=pltpu.CompilerParams(vmem_limit_bytes=32 * 1024 * 1024),
        cost_estimate=pl.CostEstimate(
            flops=2000000000, bytes_accessed=4000000, transcendentals=2400000
        ),
        name="attend",
    )(qkv, start)


def attend_back(qkv, d_out, out, top, start, tables):
    count = qkv.shape[0]
    blocks = count * 128 // TILE
    wide = pltpu.VMEM((blocks, HDIM, TILE), BF16)
    tall = pltpu.VMEM((blocks, TILE, HDIM), BF16)
    return pl.pallas_call(
        backward_kernel,
        out_shape=jax.ShapeDtypeStruct((count, 3, HDIM, 128), BF16),
        scratch_shapes=[
            wide, wide, wide, tall, tall, tall, tall,
            pltpu.VMEM((blocks, HDIM, TILE), F32),
            pltpu.VMEM((blocks, TILE, HDIM), F32),
            pltpu.VMEM((blocks, TILE, HDIM), F32),
        ],
        compiler_params=pltpu.CompilerParams(vmem_limit_bytes=40 * 1024 * 1024),
        cost_estimate=pl.CostEstimate(
            flops=6000000000, bytes_accessed=6000000, transcendentals=2400000
        ),
        name="attend_back",
    )(qkv, d_out, out, top, start, tables)


def rotation_tables(row_slots):
    index_half = np.arange(HALF, dtype=np.float64)
    places = np.arange(row_slots, dtype=np.float64) - row_slots // 2
    inverse = rope_base ** (-2.0 * index_half / HDIM)
    angles = inverse[:, None] * places[None, :]
    zeta = (2.0 * index_half + 0.4 * HDIM) / (1.4 * HDIM)
    stretch = zeta[:, None] ** (places[None, :] / xpos_base)
    cosine, sine = np.cos(angles), np.sin(angles)
    tables = [cosine * stretch, sine * stretch, cosine / stretch, sine / stretch]
    return np.stack(tables).astype(np.float32)


def moments(values):
    center = jnp.mean(values, axis=-1, keepdims=True)
    spread = jnp.mean(jnp.square(values - center), axis=-1, keepdims=True)
    inverse = lax.rsqrt(spread + norm_eps)
    return (values - center) * inverse, inverse


def norm_back(upstream, gain, normed, inverse):
    scaled = upstream * gain
    return inverse * (
        scaled
        - jnp.mean(scaled, axis=-1, keepdims=True)
        - normed * jnp.mean(scaled * normed, axis=-1, keepdims=True)
    )


def adam_update(weight, moment, squares, gradient, factor, step_rate, decay_weight):
    clipped = gradient * factor
    moment_new = beta_first * moment + (1.0 - beta_first) * clipped
    squares_new = beta_second * squares + (1.0 - beta_second) * clipped * clipped
    moment_hat = moment_new / (1.0 - beta_first**STEP)
    squares_hat = squares_new / (1.0 - beta_second**STEP)
    updated = weight - step_rate * (
        moment_hat / (jnp.sqrt(squares_hat) + adam_eps) + decay_weight * weight
    )
    return (updated, moment_new, squares_new)


def shards(
    hidden_in, cotangent, doc_lengths,
    inward, inward_moment, inward_squares,
    outward, outward_moment, outward_squares,
    upward, upward_moment, upward_squares,
    downward, downward_moment, downward_squares,
    prenorm, prenorm_moment, prenorm_squares,
    subnorm, subnorm_moment, subnorm_squares,
):
    rows, seq_slots, width = hidden_in.shape
    quarter = cotangent.shape[1]
    group_slots = 2 * seq_slots
    row_slots = group_slots * lax.axis_size(ZX)
    half = inward.shape[2] // 2
    heads = half // HDIM
    tokens = rows * group_slots
    share = rows * quarter
    zx = lax.axis_index(ZX)
    row_index = lax.axis_index(Z)
    yh = lax.axis_index(YH)
    core = lax.axis_index(C)
    ffn = lax.axis_index(FFN)
    me = lax.axis_index(EIGHT)
    low_side = yh == 0

    def mine_theirs(array, axis):
        low = array.astype(BF16)
        mine = lax.dynamic_slice_in_dim(low, yh * half, half, axis)
        theirs = lax.dynamic_slice_in_dim(low, (1 - yh) * half, half, axis)
        return mine, theirs

    def in_order(own, other):
        return jnp.concatenate(
            [jnp.where(low_side, own, other), jnp.where(low_side, other, own)], axis=0
        )

    def gathered(lines):
        other = lax.ppermute(jnp.concatenate([t for _, t in lines], axis=1), YH, SWAP)
        own = jnp.concatenate([m for m, _ in lines], axis=1)
        return lax.all_gather(in_order(own, other), ZX, axis=0, tiled=True)

    def rows_of(pair, order):
        return tuple(jnp.transpose(t, order).reshape(seq_slots, -1) for t in pair)

    in_pair = rows_of(mine_theirs(inward, 2), (0, 1, 2))
    out_pair = rows_of(mine_theirs(outward, 0), (1, 0))
    up_pair = rows_of(mine_theirs(upward, 2), (0, 1, 2))
    down_pair = rows_of(mine_theirs(downward, 1), (2, 0, 1))
    w_in = gathered([in_pair])
    w_rest = gathered([out_pair, up_pair, down_pair])
    hidden_units = 4 * half
    w_out = w_rest[:, :half]
    w_up = w_rest[:, half : half + hidden_units]
    w_down = w_rest[:, half + hidden_units :]

    doc_ends = jnp.cumsum(doc_lengths, axis=1)
    places = jnp.arange(row_slots, dtype=jnp.int32)
    my_ends = lax.dynamic_slice_in_dim(doc_ends, row_index, 1, 0)
    start = jnp.max(
        jnp.where(places[None, :] >= my_ends.reshape(-1, 1), my_ends.reshape(-1, 1), 0),
        axis=0,
        keepdims=True,
    )
    own_places = zx * group_slots + me * quarter + jnp.arange(quarter, dtype=jnp.int32)
    own_usable = (own_places[None, :] < doc_ends[:, -1:]).astype(F32).reshape(share, 1)

    t_rel = jnp.arange(tokens, dtype=jnp.int32)
    rel_share, rel_row, rel_slot = (
        t_rel // share,
        (t_rel % share) // quarter,
        t_rel % quarter,
    )
    rel_place = rel_row * group_slots + (rel_share ^ me) * quarter + rel_slot
    order = (jnp.arange(tokens, dtype=jnp.int32)[:, None] == rel_place[None, :]).astype(BF16)

    half_slots = seq_slots // 2
    sent = lax.dynamic_slice_in_dim(hidden_in, core * half_slots, half_slots, 1)
    got_mine = lax.ppermute(sent, YY, [(i, 3 - i) for i in range(4)])
    got_other = lax.ppermute(got_mine, C, SWAP)
    first_core = core == 0
    other_half = jnp.concatenate(
        [
            jnp.where(first_core, got_mine, got_other),
            jnp.where(first_core, got_other, got_mine),
        ],
        axis=1,
    )
    hidden = jnp.concatenate(
        [jnp.where(low_side, hidden_in, other_half), jnp.where(low_side, other_half, hidden_in)],
        axis=1,
    ).reshape(tokens, width)
    own_hidden = (
        lax.dynamic_slice_in_dim(hidden_in, ffn * quarter, quarter, 1)
        .astype(F32)
        .reshape(share, width)
    )
    own_cot = cotangent.astype(F32).reshape(share, width)
    df = eight_gather((own_usable * own_cot).astype(BF16))

    normed_one, _ = moments(hidden.astype(F32))
    a = (normed_one * prenorm[0] + prenorm[1]).astype(BF16)
    proj = dot(w_in, a, 0, 1).reshape(3, heads, HDIM, rows, group_slots)
    tables = jnp.asarray(rotation_tables(row_slots))
    near = lax.dynamic_slice_in_dim(tables, zx * group_slots, group_slots, 2)

    def rotate(values, cosine, sine):
        front, back = values[:, :HALF], values[:, HALF:]
        cosine, sine = cosine[None, :, None, :], sine[None, :, None, :]
        return jnp.concatenate(
            [front * cosine - back * sine, front * sine + back * cosine], axis=1
        )

    qkv = jnp.stack(
        [rotate(proj[0], near[0], near[1]), rotate(proj[1], near[2], near[3]), proj[2]]
    ).astype(BF16)
    qkv = jnp.transpose(qkv, (3, 1, 0, 2, 4)).reshape(rows * heads, 3, HDIM, group_slots)
    qkv = lax.all_to_all(qkv, ZX, 0, 0, tiled=True)
    o_head, top = attend(qkv, start)

    def to_tokens(chunks):
        parts = chunks.shape[1]
        back = lax.all_to_all(chunks, ZX, 0, 0, tiled=True)
        back = back.reshape(rows, heads, parts, HDIM, group_slots)
        return jnp.transpose(back, (2, 1, 3, 0, 4)).reshape(parts * heads * HDIM, tokens)

    o_wide = to_tokens(o_head.astype(BF16)[:, None])
    o = dot(order, o_wide, 0, 1)

    sub = lax.dynamic_slice_in_dim(subnorm, yh * half, half, 2)
    gain_o, shift_o = sub[0, 0], sub[1, 0]
    gain_h, shift_h = sub[0, 1:].reshape(-1), sub[1, 1:].reshape(-1)
    sums = eight_sum(jnp.stack([jnp.sum(o, axis=1), jnp.sum(o * o, axis=1)]))
    center = sums[0] / width
    inv_o = lax.rsqrt(sums[1] / width - center * center + norm_eps)[:, None]
    o_hat = (o - center[:, None]) * inv_o
    c = (o_hat * gain_o + shift_o).astype(BF16)
    attn = eight_scatter(dot(c, w_out, 1, 1))
    r1 = own_hidden + own_usable * attn
    r1_hat, r1_inv = moments(r1)
    bb = eight_gather((r1_hat * prenorm[2] + prenorm[3]).astype(BF16))

    dhn = dot(df, w_down, 1, 0)
    u = dot(bb, w_up, 1, 0)
    cdf = 0.5 * (1.0 + lax.erf(u * (1.0 / math.sqrt(2.0))))
    h = u * cdf
    slope = cdf + u * (jnp.exp(-0.5 * u * u) * (1.0 / math.sqrt(2.0 * math.pi)))
    scaled = dhn * gain_h
    sums = eight_sum(
        jnp.stack(
            [
                jnp.sum(h, axis=1),
                jnp.sum(h * h, axis=1),
                jnp.sum(scaled, axis=1),
                jnp.sum(scaled * h, axis=1),
            ]
        )
    )
    center = sums[0] / FF
    inv_h = lax.rsqrt(sums[1] / FF - center * center + norm_eps)
    mean_scaled = sums[2] / FF
    mean_both = inv_h * (sums[3] / FF - center * mean_scaled)
    center, inv_h, mean_scaled, mean_both = (
        t[:, None] for t in (center, inv_h, mean_scaled, mean_both)
    )
    h_hat = (h - center) * inv_h
    hn = (h_hat * gain_h + shift_h).astype(BF16)
    du = (inv_h * (scaled - mean_scaled - h_hat * mean_both) * slope).astype(BF16)
    sub_gain_h = jnp.sum(dhn * h_hat, axis=0)
    sub_shift_h = jnp.sum(dhn, axis=0)
    dbb = eight_scatter(dot(du, w_up, 1, 1))
    f = eight_scatter(dot(hn, w_down, 1, 1))
    hidden_out = (r1 + own_usable * f).astype(BF16).reshape(rows, quarter, width)
    g_mlp = jnp.concatenate([dot(df, hn, 0, 0), dot(bb, du, 0, 0)], axis=1).astype(BF16)
    g_mlp = lax.psum_scatter(g_mlp, ZX, scatter_dimension=0, tiled=True)

    dr1 = own_cot + norm_back(dbb, prenorm[2], r1_hat, r1_inv)
    pre_three = jnp.stack([jnp.sum(dbb * r1_hat, axis=0), jnp.sum(dbb, axis=0)])
    dattn = eight_gather((own_usable * dr1).astype(BF16))

    dc = dot(dattn, w_out, 1, 0)
    sub_gain_o = jnp.sum(dc * o_hat, axis=0)
    sub_shift_o = jnp.sum(dc, axis=0)
    scaled_o = dc * gain_o
    sums = eight_sum(jnp.stack([jnp.sum(scaled_o, axis=1), jnp.sum(scaled_o * o_hat, axis=1)]))
    do = inv_o * (scaled_o - (sums[0] / width)[:, None] - o_hat * (sums[1] / width)[:, None])
    do_wide = dot(do.astype(BF16), order, 0, 1).astype(BF16)
    do_wide = do_wide.reshape(heads, HDIM, rows, group_slots)
    do_head = jnp.transpose(do_wide, (2, 0, 1, 3)).reshape(rows * heads, HDIM, group_slots)
    do_head = lax.all_to_all(do_head, ZX, 0, 0, tiled=True)
    dqkv = attend_back(qkv, do_head, o_head, top, start, tables)
    dproj = to_tokens(dqkv)

    g_att = jnp.concatenate([dot(a, dproj, 0, 1), dot(dattn, c, 0, 0)], axis=1).astype(BF16)
    g_att = lax.psum_scatter(g_att, ZX, scatter_dimension=0, tiled=True)
    dproj_rel = dot(order, dproj, 0, 1).astype(BF16)
    da = eight_scatter(dot(dproj_rel, w_in, 1, 1))
    x_hat, x_inv = moments(own_hidden)
    own_grad = dr1 + norm_back(da, prenorm[0], x_hat, x_inv)
    pre_one = jnp.stack([jnp.sum(da * x_hat, axis=0), jnp.sum(da, axis=0)])
    own_grad = own_grad.astype(BF16).reshape(rows, quarter, width)
    core_grad = lax.ppermute(own_grad, C, SWAP)
    pair = jnp.concatenate(
        [jnp.where(first_core, own_grad, core_grad), jnp.where(first_core, core_grad, own_grad)],
        axis=1,
    )
    line_grad = lax.ppermute(pair, YL, SWAP)
    first_line = lax.axis_index(YL) == 0
    input_grad = jnp.concatenate(
        [jnp.where(first_line, pair, line_grad), jnp.where(first_line, line_grad, pair)], axis=1
    )

    g_mlp = g_mlp.astype(F32)
    g_att = g_att.astype(F32)
    local = jnp.sum(g_mlp * g_mlp) + jnp.sum(g_att * g_att)
    sub_grad = jnp.stack(
        [
            jnp.concatenate([sub_gain_o, sub_gain_h]),
            jnp.concatenate([sub_shift_o, sub_shift_h]),
        ]
    )
    pre_grad = jnp.concatenate([pre_one, pre_three], axis=0)

    def parted(value):
        high = value.astype(BF16)
        return jnp.stack([high, (value - high.astype(F32)).astype(BF16)])

    small = jnp.concatenate(
        [pre_grad.astype(BF16).ravel(), sub_grad.astype(BF16).ravel(), parted(local)]
    )
    pre_size, sub_size = pre_grad.size, sub_grad.size
    total = jnp.sum(copies_of(small, ZX).astype(F32), axis=0)
    sub_total = total[pre_size : pre_size + sub_size]
    local = total[pre_size + sub_size] + total[pre_size + sub_size + 1]
    local = local + jnp.sum(sub_total * sub_total)
    small = jnp.concatenate([total[:pre_size].astype(BF16), parted(local)])
    total = jnp.sum(copies_of(small, EIGHT).astype(F32), axis=0)
    pre_total = total[:pre_size].reshape(pre_grad.shape)
    squares_total = total[pre_size] + total[pre_size + 1] + jnp.sum(pre_total * pre_total)
    grad_norm = jnp.sqrt(squares_total)
    factor = jnp.minimum(1.0, clip_limit / (grad_norm + 1e-06))

    own_sub = sub_total.reshape(2, 5, half).astype(BF16)
    their_sub = lax.ppermute(own_sub, YH, SWAP)
    sub_full = jnp.concatenate(
        [jnp.where(low_side, own_sub, their_sub), jnp.where(low_side, their_sub, own_sub)], axis=2
    ).astype(F32)
    grads = jnp.concatenate([g_att, g_mlp], axis=1).astype(BF16)
    keep = lax.dynamic_slice_in_dim(grads, yh * seq_slots, seq_slots, 0)
    give = lax.dynamic_slice_in_dim(grads, (1 - yh) * seq_slots, seq_slots, 0)
    take = lax.ppermute(give, YH, SWAP)

    def whole(begin, count):
        mine = keep[:, begin : begin + count * half].reshape(seq_slots, count, half)
        theirs = take[:, begin : begin + count * half].reshape(seq_slots, count, half)
        return jnp.concatenate(
            [jnp.where(low_side, mine, theirs), jnp.where(low_side, theirs, mine)], axis=2
        ).astype(F32)

    grad_in = whole(0, 3)
    grad_out = whole(3 * half, 1)[:, 0].T
    grad_down = jnp.transpose(whole(4 * half, 4), (1, 2, 0))
    grad_up = whole(8 * half, 4)

    new_in = adam_update(
        inward, inward_moment, inward_squares, grad_in, factor, matrix_rate, decay_rate
    )
    new_out = adam_update(
        outward, outward_moment, outward_squares, grad_out, factor, matrix_rate, decay_rate
    )
    new_up = adam_update(
        upward, upward_moment, upward_squares, grad_up, factor, matrix_rate, decay_rate
    )
    new_down = adam_update(
        downward, downward_moment, downward_squares, grad_down, factor, matrix_rate, decay_rate
    )
    new_pre = adam_update(
        prenorm, prenorm_moment, prenorm_squares, pre_total, factor, norm_rate, 0.0
    )
    new_sub = adam_update(
        subnorm, subnorm_moment, subnorm_squares, sub_full, factor, norm_rate, 0.0
    )
    return (
        hidden_out, input_grad, *new_in, *new_out, *new_up, *new_down, *new_pre, *new_sub, grad_norm,
    )


def solution(mesh):
    finer = Mesh(mesh.devices.reshape(4, 4, 2, 2, 2), SEQ_FFN)
    matrices = (P(SEQ, None, FFN),) * 3 + (P(FFN, SEQ),) * 3
    matrices += (P(SEQ, None, FFN),) * 3 + (P(None, FFN, SEQ),) * 3
    norms = (P(),) * 3 + (P(None, None, FFN),) * 3
    return jax.shard_map(
        shards,
        mesh=finer,
        in_specs=(P(None, SEQ, None), P(None, SEQ_FFN, None), P(), *matrices, *norms),
        out_specs=(P(None, SEQ_FFN, None), P(None, SEQ, None), *matrices, *norms, P()),
        check_vma=False,
    )
```

```python
import math

import jax
import jax.numpy as jnp
import numpy as np
from jax import lax
from jax.experimental import pallas as pl
from jax.experimental.pallas import tpu as pltpu
from jax.sharding import Mesh
from jax.sharding import PartitionSpec as P

HDIM = 64
HALF = 32
FF = 8192
STEP = 10
Z, X, YH, YL, C = "seq_0", "seq_1", "seq_2", "ffn_0", "ffn_1"
FFN = (YL, C)
SEQ = (Z, X, YH)
SEQ_FFN = (Z, X, YH, YL, C)
ZX = (Z, X)
YY = (YH, YL)
EIGHT = (YH, YL, C)
TILE = 256

norm_eps = 1e-05
rope_base = 10000.0
xpos_base = 512.0
clip_limit = 1.0
beta_first = 0.9
beta_second = 0.95
adam_eps = 1e-08
decay_rate = 0.1
matrix_rate = 0.04
norm_rate = 0.6

F32 = jnp.float32
BF16 = jnp.bfloat16
SWAP = [(0, 1), (1, 0)]
MIB = 1024 * 1024


def xor_pairs(count, k):
    return [(i, i ^ k) for i in range(count)]


def dot(a, b, da, db):
    return lax.dot_general(a, b, (((da,), (db,)), ((), ())), preferred_element_type=F32)


def shape(dims, kind=F32):
    return jax.ShapeDtypeStruct(dims, kind)


def bytes_of(dims, kind):
    size = math.prod(dims[:-2]) * jnp.dtype(kind).itemsize
    tall = dims[-2] if len(dims) > 1 else 1
    return size * (-(-tall // 8) * 8) * (-(-dims[-1] // 128) * 128)


def in_hbm(out):
    return pltpu.HBM(out.shape, out.dtype)


def local_call(kernel, name, outs, ins, scratch=(), flops=0, moved=0, spare=4, far=(), stay=()):
    need = sum(bytes_of(a.shape, a.dtype) for a in (*ins, *outs))
    need += sum(bytes_of(s.shape, s.dtype) for s in scratch)
    scalar, vector = pltpu.SMEM, pltpu.VMEM
    return pl.pallas_call(
        kernel,
        out_shape=tuple(in_hbm(o) if n in far else o for n, o in enumerate(outs)),
        in_specs=[
            pl.BlockSpec(memory_space=scalar if a.dtype == jnp.int32 else vector) for a in ins
        ],
        out_specs=tuple(pl.BlockSpec(memory_space=vector) for _ in outs),
        scratch_shapes=list(scratch),
        compiler_params=pltpu.CompilerParams(vmem_limit_bytes=need + spare * MIB),
        cost_estimate=pl.CostEstimate(flops=flops, bytes_accessed=moved, transcendentals=0),
        name=name,
    )(*(pltpu.with_memory_space_constraint(a, pltpu.HBM) if n in stay else a for n, a in enumerate(ins)))


def turned(tile):
    return jnp.transpose(tile.astype(F32)).astype(BF16)


def forward_kernel(qkv_ref, start_ref, out_ref, low_ref, top_ref, q_s, k_s, v_s, s_s):
    blocks = q_s.shape[0]
    pieces = TILE // 128
    for i in range(blocks):
        for j in range(pieces):
            part = slice(j * 128, (j + 1) * 128)
            q_s[i, :, part] = qkv_ref[i * pieces + j, 0]
            k_s[i, part, :] = turned(qkv_ref[i * pieces + j, 1])
            v_s[i, :, part] = qkv_ref[i * pieces + j, 2]
    factor = math.log2(math.e) / math.sqrt(HDIM)
    key_line = lax.broadcasted_iota(jnp.int32, (TILE, TILE), 0)
    query_line = lax.broadcasted_iota(jnp.int32, (TILE, TILE), 1)
    for i in range(blocks):
        query = q_s[i]
        begin = start_ref[:, i * TILE : (i + 1) * TILE]
        peak = None
        for b in range(i + 1):
            s = dot(k_s[b], query, 1, 0) * factor
            keep = key_line >= begin - b * TILE
            if b == i:
                keep = keep & (key_line <= query_line)
            s = jnp.where(keep, s, -1e30)
            s_s[b] = s
            high = jnp.max(s, axis=0, keepdims=True)
            peak = high if peak is None else jnp.maximum(peak, high)
        total = jnp.zeros((1, TILE), F32)
        acc = jnp.zeros((HDIM, TILE), F32)
        for b in range(i + 1):
            e = jnp.exp2(s_s[b] - peak)
            total = total + jnp.sum(e, axis=0, keepdims=True)
            acc = acc + dot(v_s[b], e.astype(BF16), 1, 0)
        out = acc / total
        for j in range(pieces):
            out_ref[i * pieces + j] = out[:, j * 128 : (j + 1) * 128]
            low_ref[i * pieces + j] = out[:, j * 128 : (j + 1) * 128].astype(BF16)
        top_ref[:, i * TILE : (i + 1) * TILE] = peak + jnp.log2(total)


def backward_kernel(
    qkv_ref, do_ref, o_ref, top_ref, start_ref, rot_ref, out_ref,
    qt_s, kt_s, dot_s, q_s, k_s, v_s, do_s, dq_s, dk_s, dv_s,
):
    blocks = qt_s.shape[0]
    pieces = TILE // 128
    for i in range(blocks):
        for j in range(pieces):
            part = slice(j * 128, (j + 1) * 128)
            c = i * pieces + j
            qt_s[i, :, part] = qkv_ref[c, 0]
            kt_s[i, :, part] = qkv_ref[c, 1]
            dot_s[i, :, part] = do_ref[c]
            q_s[i, part, :] = turned(qkv_ref[c, 0])
            k_s[i, part, :] = turned(qkv_ref[c, 1])
            v_s[i, part, :] = turned(qkv_ref[c, 2])
            do_s[i, part, :] = turned(do_ref[c])
    scale = 1.0 / math.sqrt(HDIM)
    factor = math.log2(math.e) * scale
    key_line = lax.broadcasted_iota(jnp.int32, (TILE, TILE), 0)
    query_line = lax.broadcasted_iota(jnp.int32, (TILE, TILE), 1)
    for i in range(blocks):
        span = slice(i * TILE, (i + 1) * TILE)
        begin = start_ref[:, span]
        top = top_ref[:, span]
        delta = jnp.concatenate(
            [
                jnp.sum(
                    do_ref[i * pieces + j].astype(F32) * o_ref[i * pieces + j],
                    axis=0,
                    keepdims=True,
                )
                for j in range(pieces)
            ],
            axis=1,
        )
        dq = jnp.zeros((HDIM, TILE), F32)
        for b in range(i + 1):
            s = dot(k_s[b], qt_s[i], 1, 0) * factor
            keep = key_line >= begin - b * TILE
            if b == i:
                keep = keep & (key_line <= query_line)
            p = jnp.where(keep, jnp.exp2(s - top), 0.0)
            dp = dot(v_s[b], dot_s[i], 1, 0)
            ds = (p * (dp - delta)).astype(BF16)
            dq = dq + dot(kt_s[b], ds, 1, 0)
            dk = dot(ds, q_s[i], 1, 0)
            dv = dot(p.astype(BF16), do_s[i], 1, 0)
            if b == i:
                dk_s[b] = dk
                dv_s[b] = dv
            else:
                dk_s[b] += dk
                dv_s[b] += dv
        dq_s[i] = dq
    for i in range(blocks):
        span = slice(i * TILE, (i + 1) * TILE)
        dq = dq_s[i] * scale
        dk = jnp.transpose(dk_s[i]) * scale
        dv = jnp.transpose(dv_s[i])
        results = []
        for n, g in enumerate((dq, dk)):
            co, si = rot_ref[2 * n, :, span], rot_ref[2 * n + 1, :, span]
            front, back = g[:HALF], g[HALF:]
            results.append(
                jnp.concatenate([front * co + back * si, back * co - front * si], axis=0)
            )
        results.append(dv)
        for n, g in enumerate(results):
            for j in range(pieces):
                out_ref[i * pieces + j, n] = g[:, j * 128 : (j + 1) * 128].astype(BF16)


def attend(qkv, start):
    count = qkv.shape[0]
    blocks = count * 128 // TILE
    return pl.pallas_call(
        forward_kernel,
        out_shape=(
            pltpu.HBM((count, HDIM, 128), F32),
            pltpu.HBM((count, HDIM, 128), BF16),
            jax.ShapeDtypeStruct((1, count * 128), F32),
        ),
        scratch_shapes=[
            pltpu.VMEM((blocks, HDIM, TILE), BF16),
            pltpu.VMEM((blocks, TILE, HDIM), BF16),
            pltpu.VMEM((blocks, HDIM, TILE), BF16),
            pltpu.VMEM((blocks, TILE, TILE), F32),
        ],
        compiler_params=pltpu.CompilerParams(vmem_limit_bytes=20 * MIB),
        cost_estimate=pl.CostEstimate(
            flops=2000000000, bytes_accessed=4000000, transcendentals=2400000
        ),
        name="attend",
    )(qkv, start)


def attend_back(qkv, d_out, out, top, start, tables):
    count = qkv.shape[0]
    blocks = count * 128 // TILE
    wide = pltpu.VMEM((blocks, HDIM, TILE), BF16)
    tall = pltpu.VMEM((blocks, TILE, HDIM), BF16)
    return pl.pallas_call(
        backward_kernel,
        out_shape=pltpu.HBM((count, 3, HDIM, 128), BF16),
        scratch_shapes=[
            wide, wide, wide, tall, tall, tall, tall,
            pltpu.VMEM((blocks, HDIM, TILE), F32),
            pltpu.VMEM((blocks, TILE, HDIM), F32),
            pltpu.VMEM((blocks, TILE, HDIM), F32),
        ],
        compiler_params=pltpu.CompilerParams(vmem_limit_bytes=28 * MIB),
        cost_estimate=pl.CostEstimate(
            flops=6000000000, bytes_accessed=6000000, transcendentals=2400000
        ),
        name="attend_back",
    )(qkv, d_out, out, top, start, tables)


def rotation_tables(row_slots):
    index_half = np.arange(HALF, dtype=np.float64)
    places = np.arange(row_slots, dtype=np.float64) - row_slots // 2
    inverse = rope_base ** (-2.0 * index_half / HDIM)
    angles = inverse[:, None] * places[None, :]
    zeta = (2.0 * index_half + 0.4 * HDIM) / (1.4 * HDIM)
    stretch = zeta[:, None] ** (places[None, :] / xpos_base)
    cosine, sine = np.cos(angles), np.sin(angles)
    tables = [cosine * stretch, sine * stretch, cosine / stretch, sine / stretch]
    return np.stack(tables).astype(np.float32)


def moments(values):
    center = jnp.mean(values, axis=-1, keepdims=True)
    spread = jnp.mean(jnp.square(values - center), axis=-1, keepdims=True)
    inverse = lax.rsqrt(spread + norm_eps)
    return (values - center) * inverse, inverse


def norm_back(upstream, gain, normed, inverse):
    scaled = upstream * gain
    return inverse * (
        scaled
        - jnp.mean(scaled, axis=-1, keepdims=True)
        - normed * jnp.mean(scaled * normed, axis=-1, keepdims=True)
    )


def place_parts(parts, target, me):
    share = parts[0].shape[0]
    for k, part in enumerate(parts):
        target[pl.ds(pl.multiple_of((me ^ k) * share, share), share), :] = part[...]


def take_for_scatter(source, target, me):
    share = source.shape[0] // 8
    for side in range(2):
        for j in range(4):
            at = pl.multiple_of((me ^ (2 * j + side)) * share, share)
            target[pl.ds((side * 4 + j) * share, share), :] = source[pl.ds(at, share), :]


def scatter_product(left, right, keep_ref, send_ref):
    half = left.shape[0] // 2
    width = keep_ref.shape[1]
    step = 256

    def body(i, _):
        at = pl.ds(pl.multiple_of(i * step, step), step)
        product = dot(left[...], right[at, : left.shape[1]], 1, 1)
        keep_ref[:, at] = product[:half]
        send_ref[:, at] = product[half:].astype(BF16)
        return 0

    lax.fori_loop(0, width // step, body, 0)


def project_kernel(
    ids, here_ref, near_ref, far_ref, pre_ref, rot_ref, w_ref, qkv_ref, hat_ref, a_ref, x_s, y_s
):
    half, core = ids[1], ids[2]
    rows, slots, width = here_ref.shape
    other = (1 - half) * slots
    for r in range(rows):
        x_s[pl.ds(pl.multiple_of(half * slots, slots), slots), :] = here_ref[r]
        x_s[pl.ds(pl.multiple_of(other + core * 32, 32), 32), :] = near_ref[r]
        x_s[pl.ds(pl.multiple_of(other + (1 - core) * 32, 32), 32), :] = far_ref[r]
        normed, _ = moments(x_s[...].astype(F32))
        low = normed * pre_ref[0:1] + pre_ref[1:2]
        hat_ref[r * 2 * slots : (r + 1) * 2 * slots, :] = normed.astype(BF16)
        a_ref[r * 2 * slots : (r + 1) * 2 * slots, :] = low.astype(BF16)
    span = 2 * slots
    heads = y_s.shape[1] // HDIM
    for n in range(3):
        y_s[...] = dot(a_ref[...], w_ref[:, n * heads * HDIM : (n + 1) * heads * HDIM], 1, 0)
        for r in range(rows):
            for pair in range(heads // 2):
                t = jnp.transpose(
                    y_s[r * span : (r + 1) * span, pair * 128 : (pair + 1) * 128]
                )
                for e in range(2):
                    g = t[e * HDIM : (e + 1) * HDIM]
                    if n < 2:
                        co, si = rot_ref[2 * n], rot_ref[2 * n + 1]
                        front, back = g[:HALF], g[HALF:]
                        g = jnp.concatenate(
                            [front * co - back * si, front * si + back * co], axis=0
                        )
                    qkv_ref[r * heads + pair * 2 + e, n] = g.astype(BF16)


def head_sums_kernel(o_ref, out_ref):
    count, _, span = o_ref.shape
    heads = count // 4
    rows = []
    for r in range(4):
        first = jnp.zeros((1, span), F32)
        second = jnp.zeros((1, span), F32)
        for h in range(heads):
            o = o_ref[r * heads + h].astype(F32)
            first = first + jnp.sum(o, axis=0, keepdims=True)
            second = second + jnp.sum(o * o, axis=0, keepdims=True)
        rows.append(jnp.concatenate([first, second, jnp.zeros((6, span), F32)], axis=0))
    line = jnp.concatenate(rows, axis=1)
    for k in range(8):
        out_ref[k] = line


def inner_moments(sums_ref, width):
    sums = sums_ref[0]
    for k in range(1, 8):
        sums = sums + sums_ref[k]
    center = sums[0:1] / width
    inverse = lax.rsqrt(sums[1:2] / width - center * center + norm_eps)
    return sums, center, inverse


def out_kernel(ids, o_ref, sums_ref, gain_ref, shift_ref, w_ref, keep_ref, send_ref, c_ref, l_s):
    count, _, span = o_ref.shape
    heads = count // 4
    width = keep_ref.shape[1]
    _, center, inverse = inner_moments(sums_ref, width)
    for r in range(4):
        at = slice(r * span, (r + 1) * span)
        o = jnp.concatenate([o_ref[r * heads + h] for h in range(heads)], axis=0).astype(F32)
        c = (o - center[:, at]) * inverse[:, at] * gain_ref[...] + shift_ref[...]
        c = jnp.transpose(c).astype(BF16)
        for s in range(8):
            c_ref[s * 64 + r * 16 : s * 64 + (r + 1) * 16, :] = c[s * 16 : (s + 1) * 16]
    take_for_scatter(c_ref, l_s, ids[0])
    scatter_product(l_s, w_ref, keep_ref, send_ref)


def core_sum_kernel(keep_ref, got_ref, own_ref, one_ref, two_ref, three_ref):
    share = own_ref.shape[0]
    both = keep_ref[...] + got_ref[...].astype(F32)
    own_ref[...] = both[:share]
    for j, ref in ((1, one_ref), (2, two_ref), (3, three_ref)):
        ref[...] = both[j * share : (j + 1) * share].astype(BF16)


def summed(own_ref, refs):
    total = own_ref[...]
    for ref in refs:
        total = total + ref[...].astype(F32)
    return total


def middle_kernel(own_ref, one, two, three, x_ref, usable_ref, pre_ref, r1_ref, bb_ref):
    r1 = x_ref[...].astype(F32) + usable_ref[...] * summed(own_ref, (one, two, three))
    normed, _ = moments(r1)
    r1_ref[...] = r1
    bb_ref[...] = (normed * pre_ref[2:3] + pre_ref[3:4]).astype(BF16)


def result_kernel(own_ref, one, two, three, r1_ref, usable_ref, out_ref):
    f = summed(own_ref, (one, two, three))
    out_ref[...] = (r1_ref[...] + usable_ref[...] * f).astype(BF16)


def down_back_kernel(ids, *refs):
    parts, (w_ref, df_ref, dhn_ref) = refs[:8], refs[8:]
    place_parts(parts, df_ref, ids[0])

    def body(i, _):
        at = pl.ds(pl.multiple_of(i * 256, 256), 256)
        dhn_ref[:, at] = dot(df_ref[...], w_ref[:, at], 1, 0)
        return 0

    lax.fori_loop(0, dhn_ref.shape[1] // 256, body, 0)


def up_kernel(ids, *refs):
    parts, (w_ref, dhn_ref, gain_ref, bb_ref, h_ref, slope_ref, sums_ref) = refs[:8], refs[8:]
    place_parts(parts, bb_ref, ids[0])
    tokens, units = h_ref.shape
    step = 256

    def body(i, carry):
        at = pl.ds(pl.multiple_of(i * step, step), step)
        u = dot(bb_ref[...], w_ref[:, at], 1, 0)
        cdf = 0.5 * (1.0 + lax.erf(u * (1.0 / math.sqrt(2.0))))
        h = u * cdf
        h_ref[:, at] = h
        slope_ref[:, at] = cdf + u * (
            jnp.exp(-0.5 * u * u) * (1.0 / math.sqrt(2.0 * math.pi))
        )
        scaled = dhn_ref[:, at] * gain_ref[:, at]
        terms = (h, h * h, scaled, scaled * h)
        return tuple(c + jnp.sum(t, axis=1, keepdims=True) for c, t in zip(carry, terms))

    zero = jnp.zeros((tokens, 1), F32)
    sums = lax.fori_loop(0, units // step, body, (zero,) * 4)
    lane = lax.broadcasted_iota(jnp.int32, (tokens, 128), 1)
    wide = jnp.zeros((tokens, 128), F32)
    for n, s in enumerate(sums):
        wide = jnp.where(lane == n, s, wide)
    line = jnp.transpose(wide)[:8]
    for k in range(8):
        sums_ref[k] = line


def inner_back_kernel(
    ids, h_ref, slope_ref, dhn_ref, sums_ref, gain_ref, shift_ref, w_ref,
    keep_ref, send_ref, hn_ref, du_ref, sub_ref, l_s,
):
    sums, center, inverse = inner_moments(sums_ref, FF)
    mean_scaled = sums[2:3] / FF
    mean_both = inverse * (sums[3:4] / FF - center * mean_scaled)
    rows = jnp.concatenate([center, inverse, mean_scaled, mean_both, sums[4:8]], axis=0)
    columns = jnp.transpose(jnp.concatenate([rows] * 16, axis=0))
    tokens = h_ref.shape[0]
    center, inverse, mean_scaled, mean_both = (columns[:, n : n + 1] for n in range(4))
    units = h_ref.shape[1]

    def body(i, _):
        at = pl.ds(pl.multiple_of(i * 256, 256), 256)
        hat = (h_ref[:, at] - center) * inverse
        dhn = dhn_ref[:, at]
        gain = gain_ref[:, at]
        hn_ref[:, at] = (hat * gain + shift_ref[:, at]).astype(BF16)
        du = inverse * (dhn * gain - mean_scaled - hat * mean_both) * slope_ref[:, at]
        du_ref[:, at] = du.astype(BF16)
        sub_ref[0:1, at] = jnp.sum(dhn * hat, axis=0, keepdims=True)
        sub_ref[1:2, at] = jnp.sum(dhn, axis=0, keepdims=True)
        return 0

    lax.fori_loop(0, units // 256, body, 0)
    take_for_scatter(du_ref, l_s, ids[0])
    scatter_product(l_s, w_ref, keep_ref, send_ref)


def down_kernel(ids, hn_ref, w_ref, keep_ref, send_ref, l_s):
    take_for_scatter(hn_ref, l_s, ids[0])
    scatter_product(l_s, w_ref, keep_ref, send_ref)


def mlp_grad_kernel(df_ref, hn_ref, bb_ref, du_ref, out_ref):
    units = hn_ref.shape[1]
    out_ref[:, :units] = dot(jnp.transpose(bb_ref[...]), du_ref[...], 1, 0).astype(BF16)
    out_ref[:, units:] = dot(jnp.transpose(df_ref[...]), hn_ref[...], 1, 0).astype(BF16)


def mlp_grad(df, hn, bb, du):
    tokens, width = df.shape
    units = hn.shape[1]
    step = 256
    narrow = pl.BlockSpec((tokens, step), lambda i: (0, i))
    whole = pl.BlockSpec((tokens, units), lambda i: (0, 0))
    return pl.pallas_call(
        mlp_grad_kernel,
        grid=(width // step,),
        out_shape=pltpu.HBM((width, 2 * units), BF16),
        in_specs=[narrow, whole, narrow, whole],
        out_specs=pl.BlockSpec((step, 2 * units), lambda i: (i, 0)),
        compiler_params=pltpu.CompilerParams(vmem_limit_bytes=20 * MIB),
        cost_estimate=pl.CostEstimate(
            flops=4 * tokens * width * units, bytes_accessed=14 * MIB, transcendentals=0
        ),
        name="mlp_grad",
    )(df, hn, bb, du)


def middle_back_kernel(
    own_ref, one, two, three, r1_ref, cot_ref, usable_ref, pre_ref, dr1_ref, dattn_ref, grad_ref
):
    dbb = summed(own_ref, (one, two, three))
    hat, inverse = moments(r1_ref[...])
    dr1 = cot_ref[...].astype(F32) + norm_back(dbb, pre_ref[2:3], hat, inverse)
    dr1_ref[...] = dr1
    dattn_ref[...] = (usable_ref[...] * dr1).astype(BF16)
    grad_ref[0:1] = jnp.sum(dbb * hat, axis=0, keepdims=True)
    grad_ref[1:2] = jnp.sum(dbb, axis=0, keepdims=True)


def out_back_kernel(ids, *refs):
    parts, refs = refs[:8], refs[8:]
    w_ref, o_ref, sums_ref, gain_ref, dattn_ref, dc_ref, out_ref, sub_ref, y_s = refs
    place_parts(parts, dattn_ref, ids[0])
    y_s[...] = dot(dattn_ref[...], w_ref[...], 1, 0)
    count, _, span = o_ref.shape
    heads = count // 4
    _, center, inverse = inner_moments(sums_ref, dattn_ref.shape[1])
    gain_grad, shift_grad, lines = 0.0, 0.0, []
    for r in range(4):
        at = slice(r * span, (r + 1) * span)
        dc = jnp.concatenate(
            [y_s[s * 64 + r * 16 : s * 64 + (r + 1) * 16, :] for s in range(8)], axis=0
        )
        dc = jnp.transpose(dc)
        dc_ref[:, at] = dc
        o = jnp.concatenate([o_ref[r * heads + h] for h in range(heads)], axis=0).astype(F32)
        hat = (o - center[:, at]) * inverse[:, at]
        gain_grad = gain_grad + jnp.sum(dc * hat, axis=1, keepdims=True)
        shift_grad = shift_grad + jnp.sum(dc, axis=1, keepdims=True)
        scaled = dc * gain_ref[...]
        lines.append(
            jnp.concatenate(
                [
                    jnp.sum(scaled, axis=0, keepdims=True),
                    jnp.sum(scaled * hat, axis=0, keepdims=True),
                    jnp.zeros((6, span), F32),
                ],
                axis=0,
            )
        )
    line = jnp.concatenate(lines, axis=1)
    for k in range(8):
        out_ref[k] = line
    sub_ref[...] = jnp.concatenate(
        [
            jnp.transpose(jnp.broadcast_to(g, (g.shape[0], 128)))[0:1]
            for g in (gain_grad, shift_grad)
        ],
        axis=0,
    )


def head_grad_kernel(dc_ref, o_ref, sums_ref, back_ref, gain_ref, out_ref, *, width):
    count, _, span = o_ref.shape
    heads = count // 4
    _, center, inverse = inner_moments(sums_ref, width)
    back = back_ref[0]
    for k in range(1, 8):
        back = back + back_ref[k]
    for r in range(4):
        at = slice(r * span, (r + 1) * span)
        first, second = back[0:1, at] / width, back[1:2, at] / width
        for h in range(heads):
            part = slice(h * HDIM, (h + 1) * HDIM)
            hat = (o_ref[r * heads + h].astype(F32) - center[:, at]) * inverse[:, at]
            scaled = dc_ref[part, at] * gain_ref[part]
            out_ref[r * heads + h] = (
                inverse[:, at] * (scaled - first - hat * second)
            ).astype(BF16)


def out_grad_kernel(dattn_ref, c_ref, out_ref):
    out_ref[...] = dot(jnp.transpose(dattn_ref[...]), c_ref[...], 1, 0).astype(BF16)


def out_grad(dattn, c):
    tokens, width = dattn.shape
    units = c.shape[1]
    step = 512
    return pl.pallas_call(
        out_grad_kernel,
        grid=(width // step,),
        out_shape=pltpu.HBM((width, units), BF16),
        in_specs=[
            pl.BlockSpec((tokens, step), lambda i: (0, i)),
            pl.BlockSpec((tokens, units), lambda i: (0, 0)),
        ],
        out_specs=pl.BlockSpec((step, units), lambda i: (i, 0)),
        compiler_params=pltpu.CompilerParams(vmem_limit_bytes=16 * MIB),
        cost_estimate=pl.CostEstimate(
            flops=2 * tokens * width * units, bytes_accessed=4 * MIB, transcendentals=0
        ),
        name="out_grad",
    )(dattn, c)


def turn_kernel(a_ref, out_ref):
    for r in range(a_ref.shape[1] // 256):
        out_ref[r * 256 : (r + 1) * 256, :] = jnp.transpose(a_ref[:, r * 256 : (r + 1) * 256])


def column(row):
    return jnp.transpose(jnp.broadcast_to(row, (128, row.shape[1])))[:, 0:1]


def row_of(col):
    return jnp.transpose(jnp.broadcast_to(col, (col.shape[0], 128)))[0:1]


def in_grad_kernel(
    dqkv_ref, xt_ref, w_ref, pre_ref, out_ref, grad_ref, tokens_ref, pre_grad_ref, d_s, sum_s
):
    count = dqkv_ref.shape[0]
    heads = count // 4
    units = d_s.shape[0]

    @pl.when(pl.program_id(0) == 0)
    def _():
        for r in range(4):
            for n in range(3):
                for h in range(heads):
                    base = (n * heads + h) * HDIM
                    d_s[base : base + HDIM, r * 128 : (r + 1) * 128] = dqkv_ref[r * heads + h, n]
        for n in range(0, units, 128):
            total = jnp.zeros((1, 128), F32)
            for r in range(4):
                t = jnp.transpose(d_s[n : n + 128, r * 128 : (r + 1) * 128].astype(F32))
                total = total + jnp.sum(t, axis=0, keepdims=True)
                t = t.astype(BF16)
                for s in range(8):
                    tokens_ref[s * 64 + r * 16 : s * 64 + (r + 1) * 16, n : n + 128] = t[
                        s * 16 : (s + 1) * 16
                    ]
            sum_s[:, n : n + 128] = total

    product = dot(xt_ref[...], d_s[...], 1, 1)
    sums = sum_s[...]
    gradient = product * column(pre_ref[0:1]) + column(pre_ref[1:2]) * sums
    for c in range(grad_ref.shape[0]):
        at = slice(c * 128, (c + 1) * 128)
        grad_ref[c, :128, :units] = gradient[at].astype(BF16)
        grad_ref[c, :128, units:] = out_ref[at]
    w = w_ref[:, :units].astype(F32)
    pre_grad_ref[0:1] = row_of(jnp.sum(w * product, axis=1, keepdims=True))
    pre_grad_ref[1:2] = row_of(jnp.sum(w * sums, axis=1, keepdims=True))


def in_grad(dqkv, x_turned, w_att, prenorm, g_out):
    width, tokens = x_turned.shape
    half = g_out.shape[1]
    units = 3 * half
    step = 512
    return pl.pallas_call(
        in_grad_kernel,
        grid=(width // step,),
        out_shape=(
            pltpu.HBM((width // 128, 144, units + half), BF16),
            shape((tokens, units), BF16),
            shape((2, width)),
        ),
        in_specs=[
            pl.BlockSpec(dqkv.shape, lambda i: (0, 0, 0, 0)),
            pl.BlockSpec((step, tokens), lambda i: (i, 0)),
            pl.BlockSpec((step, units + half), lambda i: (i, 0)),
            pl.BlockSpec((4, step), lambda i: (0, i)),
            pl.BlockSpec((step, half), lambda i: (i, 0)),
        ],
        out_specs=(
            pl.BlockSpec((step // 128, 144, units + half), lambda i: (i, 0, 0)),
            pl.BlockSpec((tokens, units), lambda i: (0, 0)),
            pl.BlockSpec((2, step), lambda i: (0, i)),
        ),
        scratch_shapes=[pltpu.VMEM((units, tokens), BF16), pltpu.VMEM((1, units), F32)],
        compiler_params=pltpu.CompilerParams(vmem_limit_bytes=24 * MIB),
        cost_estimate=pl.CostEstimate(
            flops=2 * tokens * width * units, bytes_accessed=13 * MIB, transcendentals=0
        ),
        name="in_grad",
    )(dqkv, x_turned, w_att, prenorm, g_out)


def small_kernel(one_ref, three_ref, o_ref, h_ref, _, out_ref):
    width = out_ref.shape[2]
    half = o_ref.shape[1]
    lines = []
    for ref in (one_ref, three_ref):
        for n in range(2):
            lines += [ref[n : n + 1, :width], ref[n : n + 1, width:]]
    for n in range(2):
        first = [o_ref[n : n + 1], h_ref[n : n + 1, : width - half]]
        last = [h_ref[n : n + 1, width - half :], jnp.zeros((1, width - half), F32)]
        lines += [jnp.concatenate(first, axis=1), jnp.concatenate(last, axis=1)]
    lines.append(jnp.zeros((16 - len(lines), width), F32))
    lines = jnp.concatenate(lines, axis=0).astype(BF16)
    for k in range(out_ref.shape[0]):
        out_ref[k] = lines


def add_small(pre_one, pre_three, sub_o, sub_h, grads):
    count, rows, width = grads.shape
    ins = [pre_one, pre_three, sub_o, sub_h]
    return pl.pallas_call(
        small_kernel,
        grid=(1,),
        out_shape=pltpu.HBM(grads.shape, BF16),
        in_specs=[pl.BlockSpec(a.shape, lambda i: (0, 0)) for a in ins]
        + [pl.BlockSpec(memory_space=pl.ANY)],
        out_specs=pl.BlockSpec((count, 16, width), lambda i: (0, rows // 16 - 1, 0)),
        input_output_aliases={4: 0},
        compiler_params=pltpu.CompilerParams(vmem_limit_bytes=8 * MIB),
        name="add_small",
    )(*ins, grads)


def in_back_kernel(ids, d_ref, w_ref, keep_ref, send_ref, l_s):
    take_for_scatter(d_ref, l_s, ids[0])
    scatter_product(l_s, w_ref, keep_ref, send_ref)


def last_sum_kernel(ids, g_ref, mlp_ref, keep_ref, give_ref, sub_ref, out_ref):
    slots = keep_ref.shape[0]
    width = g_ref.shape[2]
    low = ids[1] == 0

    def total(begin, end):
        out = g_ref[0, begin:end].astype(F32)
        for k in range(1, g_ref.shape[0]):
            out = out + g_ref[k, begin:end].astype(F32)
        return out

    first, second = total(0, slots), total(slots, 2 * slots)
    keep_ref[...] = jnp.where(low, first, second).astype(BF16)
    give_ref[...] = jnp.where(low, second, first).astype(BF16)
    squares = whole_sum(first * first + second * second) + mlp_ref[0:1, 0:1]
    small = total(2 * slots, 2 * slots + 16)

    def joined(begin):
        return jnp.concatenate([small[begin : begin + 1], small[begin + 1 : begin + 2]], axis=1)

    sub = jnp.concatenate([joined(8), joined(10)], axis=0)
    sub_ref[...] = jnp.concatenate([sub] * 4, axis=0)[:, : sub_ref.shape[1]]
    lane = lax.broadcasted_iota(jnp.int32, (4, 2 * width), 1)
    scalars = jnp.where(lane < 128, squares, whole_sum(sub * sub))
    lines = jnp.concatenate([joined(2 * n) for n in range(4)] + [scalars], axis=0)
    for k in range(out_ref.shape[0]):
        out_ref[k] = lines


def input_back_kernel(own_ref, one, two, three, x_ref, dr1_ref, pre_ref, out_ref):
    da = summed(own_ref, (one, two, three))
    hat, inverse = moments(x_ref[...].astype(F32))
    out_ref[...] = (dr1_ref[...] + norm_back(da, pre_ref[0:1], hat, inverse)).astype(BF16)


def whole_sum(values):
    return jnp.sum(jnp.sum(values, axis=1, keepdims=True), axis=0, keepdims=True)


def rest_kernel(ids, g_ref, keep_ref, give_ref, sum_ref):
    slots = keep_ref.shape[0]
    half = ids[1]
    keep_ref[...] = g_ref[pl.ds(pl.multiple_of(half * slots, slots), slots), :]
    give_ref[...] = g_ref[pl.ds(pl.multiple_of((1 - half) * slots, slots), slots), :]
    total = jnp.zeros((1, 1), F32)
    for k in range(g_ref.shape[0] // 32):
        g = g_ref[k * 32 : (k + 1) * 32, :].astype(F32)
        total = total + whole_sum(g * g)
    sum_ref[...] = jnp.broadcast_to(total, sum_ref.shape)


def pre_kernel(small_ref, total_ref, out_ref):
    total = small_ref[0]
    for k in range(1, small_ref.shape[0]):
        total = total + small_ref[k]
    total_ref[...] = total
    for k in range(out_ref.shape[0]):
        out_ref[k] = jnp.broadcast_to(total[4:5, 0:128], out_ref.shape[1:])


def adam_step(weight, moment, squares, gradient, factor, step_rate, decay_weight):
    clipped = gradient * factor
    moment_new = beta_first * moment + (1.0 - beta_first) * clipped
    squares_new = beta_second * squares + (1.0 - beta_second) * clipped * clipped
    moment_hat = moment_new * (1.0 / (1.0 - beta_first**STEP))
    squares_hat = squares_new * (1.0 / (1.0 - beta_second**STEP))
    updated = weight - step_rate * (
        moment_hat / (jnp.sqrt(squares_hat) + adam_eps) + decay_weight * weight
    )
    return updated, moment_new, squares_new


def adam_kernel(
    ids, pre_total, norm_part, att_keep, att_take, mlp_keep, mlp_take, sub_own, sub_take, *refs
):
    states, outs, norm_out = refs[:18], refs[18:36], refs[36]
    low = ids[1] == 0
    squares = norm_part[0, 0:1, 0:1]
    for k in range(1, norm_part.shape[0]):
        squares = squares + norm_part[k, 0:1, 0:1]
    pre = pre_total[0:4]
    squares = squares + pre_total[4:5, 128:129] + whole_sum(pre * pre)
    norm = jnp.sqrt(squares)
    factor = jnp.minimum(1.0, clip_limit / (norm + 1e-06))
    half = att_keep.shape[1] // 4

    def pair(mine, theirs, at):
        mine = mine[:, at * half : (at + 1) * half].astype(F32)
        theirs = theirs[:, at * half : (at + 1) * half].astype(F32)
        return jnp.concatenate(
            [jnp.where(low, mine, theirs), jnp.where(low, theirs, mine)], axis=1
        )

    def step(which, index, gradient, rate, decay):
        state = [states[3 * which + n][index] for n in range(3)]
        for n, value in enumerate(adam_step(*state, gradient, factor, rate, decay)):
            outs[3 * which + n][index] = value

    everything = slice(None)
    for k in range(3):
        step(0, (k,), pair(att_keep, att_take, k), matrix_rate, decay_rate)
    step(1, (everything,), pair(att_keep, att_take, 3), matrix_rate, decay_rate)
    for b in range(4):
        step(2, (everything, b), pair(mlp_keep, mlp_take, b), matrix_rate, decay_rate)
        step(3, (b,), pair(mlp_keep, mlp_take, 4 + b), matrix_rate, decay_rate)

    @pl.when(pl.program_id(0) == 0)
    def _():
        step(4, (everything,), pre, norm_rate, 0.0)
        for b in range(5):
            step(5, (b,), pair(sub_own, sub_take, b)[0:2], norm_rate, 0.0)
        norm_out[...] = jnp.broadcast_to(norm, norm_out.shape)


def adam(ids, pre_total, norm_part, gradients, subs, states):
    flat = [a for state in states for a in state]
    step = 16

    def whole(a):
        return pl.BlockSpec(a.shape, lambda i, nd=a.ndim: (0,) * nd)

    def blocks(which, a):
        if which > 3:
            return whole(a)
        dim = (1, 0, 0, 1)[which]
        block = tuple(step if n == dim else d for n, d in enumerate(a.shape))
        return pl.BlockSpec(
            block, lambda i, nd=a.ndim, dim=dim: tuple(i if n == dim else 0 for n in range(nd))
        )

    specs = [blocks(n // 3, a) for n, a in enumerate(flat)]
    rows = [pl.BlockSpec((step, g.shape[1]), lambda i: (i, 0)) for g in gradients]
    norm = shape((8, 128))
    return pl.pallas_call(
        adam_kernel,
        grid=(gradients[0].shape[0] // step,),
        out_shape=tuple(shape(a.shape) for a in flat) + (norm,),
        in_specs=[
            pl.BlockSpec(memory_space=pltpu.SMEM),
            whole(pre_total),
            whole(norm_part),
            *rows,
            *(whole(a) for a in subs),
            *specs,
        ],
        out_specs=tuple(specs) + (whole(norm),),
        compiler_params=pltpu.CompilerParams(vmem_limit_bytes=56 * MIB),
        cost_estimate=pl.CostEstimate(flops=0, bytes_accessed=12 * MIB, transcendentals=0),
        name="adam",
    )(ids, pre_total, norm_part, *gradients, *subs, *flat)


def eight_parts(own, *meanwhile):
    lines = [lax.ppermute(own, YY, xor_pairs(4, k)) for k in (1, 2, 3)]
    if meanwhile:
        lines = [after(line, *meanwhile) for line in lines]
    lines = [own] + lines
    parts = []
    for line in lines:
        parts += [line, lax.ppermute(line, C, SWAP)]
    return parts


def finish_scatter(keep, send, work=None):
    share, width = keep.shape[0] // 4, keep.shape[1]
    got = lax.ppermute(send, C, SWAP)
    own, *sent = local_call(
        core_sum_kernel,
        "core_sum",
        [shape((share, width))] + [shape((share, width), BF16)] * 3,
        [keep, got],
        moved=5 * MIB,
    )
    lines = [lax.ppermute(s, YY, xor_pairs(4, k)) for k, s in zip((1, 2, 3), sent)]
    if work is None:
        return [own] + lines
    done = work(own)
    return [own] + [after(line, *done) for line in lines], done


def each_to_all(copies, axis):
    return lax.all_to_all(copies, axis, split_axis=0, concat_axis=0, tiled=True)


def after(value, *others):
    return lax.optimization_barrier((value, *others))[0]


def shards(
    hidden_in, cotangent, doc_lengths,
    inward, inward_moment, inward_squares,
    outward, outward_moment, outward_squares,
    upward, upward_moment, upward_squares,
    downward, downward_moment, downward_squares,
    prenorm, prenorm_moment, prenorm_squares,
    subnorm, subnorm_moment, subnorm_squares,
):
    rows, seq_slots, width = hidden_in.shape
    quarter = cotangent.shape[1]
    group_slots = 2 * seq_slots
    row_slots = group_slots * lax.axis_size(ZX)
    half = inward.shape[2] // 2
    heads = half // HDIM
    units = 4 * half
    tokens = rows * group_slots
    share = rows * quarter
    zx = lax.axis_index(ZX)
    row_index = lax.axis_index(Z)
    yh = lax.axis_index(YH)
    core = lax.axis_index(C)
    ffn = lax.axis_index(FFN)
    me = lax.axis_index(EIGHT)
    low_side = yh == 0
    first_core = core == 0
    ids = jnp.stack([me, yh, core, zx]).astype(jnp.int32)

    def mine_theirs(array, axis):
        low = array.astype(BF16)
        mine = lax.dynamic_slice_in_dim(low, yh * half, half, axis)
        theirs = lax.dynamic_slice_in_dim(low, (1 - yh) * half, half, axis)
        return mine, theirs

    def in_order(own, other):
        return jnp.concatenate(
            [jnp.where(low_side, own, other), jnp.where(low_side, other, own)], axis=0
        )

    def both_halves(pairs):
        other = lax.ppermute(jnp.concatenate([t for _, t in pairs], axis=1), YH, SWAP)
        own = jnp.concatenate([m for m, _ in pairs], axis=1)
        return in_order(own, other)

    def rows_of(pair, order):
        return tuple(jnp.transpose(t, order).reshape(seq_slots, -1) for t in pair)

    in_pair = rows_of(mine_theirs(inward, 2), (0, 1, 2))
    out_pair = rows_of(mine_theirs(outward, 0), (1, 0))
    up_pair = rows_of(mine_theirs(upward, 2), (0, 1, 2))
    down_pair = rows_of(mine_theirs(downward, 1), (2, 0, 1))
    w_att = both_halves([in_pair, out_pair])
    w_att = lax.all_gather(w_att, ZX, axis=0, tiled=True)
    w_out = w_att[:, 3 * half :]
    w_mlp = both_halves([up_pair, down_pair])
    w_mlp = lax.all_gather(w_mlp, ZX, axis=0, tiled=True)
    w_up, w_down = w_mlp[:, :units], w_mlp[:, units:]

    doc_ends = jnp.cumsum(doc_lengths, axis=1)
    places = jnp.arange(row_slots, dtype=jnp.int32)
    my_ends = lax.dynamic_slice_in_dim(doc_ends, row_index, 1, 0)
    start = jnp.max(
        jnp.where(places[None, :] >= my_ends.reshape(-1, 1), my_ends.reshape(-1, 1), 0),
        axis=0,
        keepdims=True,
    )
    own_places = zx * group_slots + me * quarter + jnp.arange(quarter, dtype=jnp.int32)
    own_usable = (own_places[None, :] < doc_ends[:, -1:]).astype(F32).reshape(share, 1)

    half_slots = seq_slots // 2
    sent = lax.dynamic_slice_in_dim(hidden_in, core * half_slots, half_slots, 1)
    got_near = lax.ppermute(sent, YY, [(i, 3 - i) for i in range(4)])
    got_far = lax.ppermute(got_near, C, SWAP)
    own_hidden = lax.dynamic_slice_in_dim(hidden_in, ffn * quarter, quarter, 1)
    own_hidden = own_hidden.reshape(share, width)
    own_cot = cotangent.reshape(share, width)
    df_own = (own_usable * own_cot.astype(F32)).astype(BF16)
    df_parts = eight_parts(after(df_own, got_near))

    tables = jnp.asarray(rotation_tables(row_slots))
    near = lax.dynamic_slice_in_dim(tables, zx * group_slots, group_slots, 2)
    qkv, x_hat = local_call(
        project_kernel,
        "project",
        [
            shape((rows * heads, 3, HDIM, group_slots), BF16),
            shape((tokens, width), BF16),
        ],
        [ids, hidden_in, got_near, got_far, after(prenorm, *df_parts), near, w_att],
        [
            pltpu.VMEM((tokens, width), BF16),
            pltpu.VMEM((group_slots, width), BF16),
            pltpu.VMEM((tokens, half), F32),
        ],
        flops=2 * tokens * width * 3 * half,
        moved=8 * MIB,
        far=(0, 1),
    )
    qkv = each_to_all(qkv, ZX)
    o_head, o_low, top = attend(qkv, start)
    o = each_to_all(o_low, ZX)
    (x_turned,) = local_call(
        turn_kernel, "turn", [shape((width, tokens), BF16)], [x_hat], moved=4 * MIB, far=(0,)
    )

    sub = lax.dynamic_slice_in_dim(subnorm, yh * half, half, 2)
    gain_o, shift_o = sub[0, 0].reshape(half, 1), sub[1, 0].reshape(half, 1)
    gain_h, shift_h = sub[0, 1:].reshape(1, units), sub[1, 1:].reshape(1, units)
    stat = shape((8, 8, tokens))
    (sums_o,) = local_call(head_sums_kernel, "head_sums", [stat], [o])
    sums_o = each_to_all(sums_o, EIGHT)
    pieces = [shape((tokens // 2, width)), shape((tokens // 2, width), BF16)]
    keep, send, c = local_call(
        out_kernel,
        "out",
        pieces + [shape((tokens, half), BF16)],
        [ids, o, sums_o, gain_o, shift_o, w_out],
        [pltpu.VMEM((tokens, half), BF16)],
        flops=2 * tokens * width * half,
        moved=4 * MIB,
        far=(2,),
    )
    df_work = lambda own: local_call(
        down_back_kernel,
        "down_back",
        [shape((tokens, width), BF16), shape((tokens, units))],
        [ids] + df_parts + [after(w_down, own)],
        flops=2 * tokens * width * units,
        moved=10 * MIB,
        stay=range(1, 9),
        far=(0,),
    )
    scattered, (df, dhn) = finish_scatter(keep, send, df_work)
    r1, bb_own = local_call(
        middle_kernel,
        "middle",
        [shape((share, width)), shape((share, width), BF16)],
        scattered + [own_hidden, own_usable, prenorm],
        moved=3 * MIB,
        far=(0,),
    )

    bb_parts = eight_parts(bb_own)
    bb, h, slope, sums_h = local_call(
        up_kernel,
        "up",
        [shape((tokens, width), BF16), shape((tokens, units)), shape((tokens, units)), stat],
        [ids] + bb_parts + [w_up, dhn, gain_h],
        flops=2 * tokens * width * units,
        moved=14 * MIB,
        stay=range(1, 9),
        far=(0,),
    )
    sums_h = each_to_all(sums_h, EIGHT)
    keep, send, hn, du, sub_h = local_call(
        inner_back_kernel,
        "inner_back",
        pieces + [shape((tokens, units), BF16)] * 2 + [shape((2, units))],
        [ids, h, slope, dhn, sums_h, gain_h, shift_h, w_up],
        [pltpu.VMEM((tokens, units), BF16)],
        flops=2 * tokens * width * units,
        moved=14 * MIB,
        far=(2, 3),
    )
    scattered = finish_scatter(keep, send)
    g_mlp = mlp_grad(df, hn, bb, du)
    dr1, dattn_own, pre_three = local_call(
        middle_back_kernel,
        "middle_back",
        [shape((share, width)), shape((share, width), BF16), shape((2, width))],
        scattered + [r1, own_cot, own_usable, prenorm],
        moved=4 * MIB,
        far=(0,),
    )
    dattn_parts = eight_parts(dattn_own, g_mlp)
    g_mlp = lax.psum_scatter(after(g_mlp, *dattn_parts), ZX, scatter_dimension=0, tiled=True)

    dattn, dc, back_o, sub_o = local_call(
        out_back_kernel,
        "out_back",
        [shape((tokens, width), BF16), shape((half, tokens)), stat, shape((2, half))],
        [ids] + dattn_parts + [w_out, o, sums_o, gain_o],
        [pltpu.VMEM((tokens, half), F32)],
        flops=2 * tokens * width * half,
        moved=6 * MIB,
        stay=range(1, 9),
        far=(0,),
    )
    g_out = out_grad(dattn, c)
    back_o = after(each_to_all(back_o, EIGHT), g_out)
    (do,) = local_call(
        lambda *refs: head_grad_kernel(*refs, width=width),
        "head_grad",
        [shape((rows * heads, HDIM, group_slots), BF16)],
        [dc, o, sums_o, back_o, gain_o],
        moved=MIB,
    )
    keep, send = local_call(
        down_kernel,
        "down",
        pieces,
        [ids, hn, w_down],
        [pltpu.VMEM((tokens, units), BF16)],
        flops=2 * tokens * width * units,
        moved=8 * MIB,
    )
    do = after(each_to_all(do, ZX), x_turned, keep)
    scattered = finish_scatter(after(keep, do), send)
    dqkv = attend_back(qkv, do, o_head, top, start, tables)
    dqkv = each_to_all(dqkv, ZX)

    g_att, dproj, pre_one = in_grad(
        after(dqkv, *scattered), x_turned, w_att, prenorm, g_out
    )
    g_att = each_to_all(add_small(pre_one, pre_three, sub_o, sub_h, g_att), ZX)
    keep, send = local_call(
        in_back_kernel,
        "in_back",
        pieces,
        [ids, dproj, w_att],
        [pltpu.VMEM((tokens, 3 * half), BF16)],
        flops=2 * tokens * width * 3 * half,
        moved=7 * MIB,
    )
    da_parts = finish_scatter(keep, send)
    mlp_keep, mlp_give, squares_mlp = local_call(
        rest_kernel,
        "rest",
        [shape((seq_slots, 2 * units), BF16)] * 2 + [shape((8, 128))],
        [ids, g_mlp],
        far=(0,),
    )
    mlp_take = lax.ppermute(mlp_give, YH, SWAP)
    (own_grad,) = local_call(
        input_back_kernel,
        "input_back",
        [shape((share, width), BF16)],
        da_parts + [own_hidden, dr1, prenorm],
        moved=3 * MIB,
    )
    hidden_out = local_call(
        result_kernel,
        "result",
        [shape((share, width), BF16)],
        scattered + [r1, own_usable],
        moved=3 * MIB,
    )[0].reshape(rows, quarter, width)

    own_grad = own_grad.reshape(rows, quarter, width)
    core_grad = lax.ppermute(own_grad, C, SWAP)
    pair = jnp.concatenate(
        [jnp.where(first_core, own_grad, core_grad), jnp.where(first_core, core_grad, own_grad)],
        axis=1,
    )
    line_grad = lax.ppermute(pair, YL, SWAP)
    first_line = lax.axis_index(YL) == 0
    input_grad = jnp.concatenate(
        [jnp.where(first_line, pair, line_grad), jnp.where(first_line, line_grad, pair)], axis=1
    )

    grad_piece = shape((seq_slots, 4 * half), BF16)
    att_keep, att_give, sub_own, small = local_call(
        last_sum_kernel,
        "last_sum",
        [grad_piece, grad_piece, shape((8, 5 * half)), shape((8, 8, width))],
        [ids, after(g_att, mlp_take), squares_mlp],
        moved=5 * MIB,
        far=(0,),
    )
    att_take = lax.ppermute(att_give, YH, SWAP)
    sub_take = lax.ppermute(sub_own, YH, SWAP)
    small = each_to_all(small, EIGHT)
    pre_total, norm_part = local_call(
        pre_kernel, "pre", [shape((8, width)), shape((16, 8, 128))], [small], far=(0,)
    )
    norm_part = each_to_all(norm_part, ZX)
    turns = ((1, 0, 2), (1, 0), (0, 1, 2), (0, 2, 1), (0, 1), (1, 0, 2))
    states = [
        (inward, inward_moment, inward_squares),
        (outward, outward_moment, outward_squares),
        (upward, upward_moment, upward_squares),
        (downward, downward_moment, downward_squares),
        (prenorm, prenorm_moment, prenorm_squares),
        (subnorm, subnorm_moment, subnorm_squares),
    ]
    *updated, norm = adam(
        ids,
        pre_total,
        norm_part,
        [att_keep, att_take, mlp_keep, mlp_take],
        [sub_own, sub_take],
        [tuple(jnp.transpose(a, turn) for a in state) for state, turn in zip(states, turns)],
    )
    updated = [jnp.transpose(a, turns[n // 3]) for n, a in enumerate(updated)]
    return (hidden_out, input_grad, *updated, norm[0, 0])


def solution(mesh):
    finer = Mesh(mesh.devices.reshape(4, 4, 2, 2, 2), SEQ_FFN)
    matrices = (P(SEQ, None, FFN),) * 3 + (P(FFN, SEQ),) * 3
    matrices += (P(SEQ, None, FFN),) * 3 + (P(None, FFN, SEQ),) * 3
    norms = (P(),) * 3 + (P(None, None, FFN),) * 3
    return jax.shard_map(
        shards,
        mesh=finer,
        in_specs=(P(None, SEQ, None), P(None, SEQ_FFN, None), P(), *matrices, *norms),
        out_specs=(P(None, SEQ_FFN, None), P(None, SEQ, None), *matrices, *norms, P()),
        check_vma=False,
    )
```

```python
import math

import jax
import jax.numpy as jnp
import numpy as np
from jax import lax
from jax.experimental import pallas as pl
from jax.experimental.pallas import tpu as pltpu
from jax.sharding import Mesh
from jax.sharding import PartitionSpec as P

HDIM = 64
HALF = 32
FF = 8192
STEP = 10
Z, X, YH, YL, C = "seq_0", "seq_1", "seq_2", "ffn_0", "ffn_1"
FFN = (YL, C)
SEQ = (Z, X, YH)
SEQ_FFN = (Z, X, YH, YL, C)
ZX = (Z, X)
YY = (YH, YL)
EIGHT = (YH, YL, C)
TILE = 256

norm_eps = 1e-05
rope_base = 10000.0
xpos_base = 512.0
clip_limit = 1.0
beta_first = 0.9
beta_second = 0.95
adam_eps = 1e-08
decay_rate = 0.1
matrix_rate = 0.04
norm_rate = 0.6

F32 = jnp.float32
BF16 = jnp.bfloat16
SWAP = [(0, 1), (1, 0)]
MIB = 1024 * 1024


def xor_pairs(count, k):
    return [(i, i ^ k) for i in range(count)]


def dot(a, b, da, db):
    return lax.dot_general(a, b, (((da,), (db,)), ((), ())), preferred_element_type=F32)


def shape(dims, kind=F32):
    return jax.ShapeDtypeStruct(dims, kind)


def bytes_of(dims, kind):
    size = math.prod(dims[:-2]) * jnp.dtype(kind).itemsize
    tall = dims[-2] if len(dims) > 1 else 1
    return size * (-(-tall // 8) * 8) * (-(-dims[-1] // 128) * 128)


def in_hbm(out):
    return pltpu.HBM(out.shape, out.dtype)


def local_call(kernel, name, outs, ins, scratch=(), flops=0, moved=0, spare=4, far=(), stay=()):
    need = sum(bytes_of(a.shape, a.dtype) for a in (*ins, *outs))
    need += sum(bytes_of(s.shape, s.dtype) for s in scratch)
    scalar, vector = pltpu.SMEM, pltpu.VMEM
    return pl.pallas_call(
        kernel,
        out_shape=tuple(in_hbm(o) if n in far else o for n, o in enumerate(outs)),
        in_specs=[
            pl.BlockSpec(memory_space=scalar if a.dtype == jnp.int32 else vector) for a in ins
        ],
        out_specs=tuple(pl.BlockSpec(memory_space=vector) for _ in outs),
        scratch_shapes=list(scratch),
        compiler_params=pltpu.CompilerParams(vmem_limit_bytes=need + spare * MIB),
        cost_estimate=pl.CostEstimate(flops=flops, bytes_accessed=moved, transcendentals=0),
        name=name,
    )(*(pltpu.with_memory_space_constraint(a, pltpu.HBM) if n in stay else a for n, a in enumerate(ins)))


def turned(tile):
    return jnp.transpose(tile.astype(F32)).astype(BF16)


def forward_kernel(qkv_ref, start_ref, out_ref, low_ref, top_ref, q_s, k_s, v_s, s_s):
    blocks = q_s.shape[0]
    pieces = TILE // 128
    for i in range(blocks):
        for j in range(pieces):
            part = slice(j * 128, (j + 1) * 128)
            q_s[i, :, part] = qkv_ref[i * pieces + j, 0]
            k_s[i, part, :] = turned(qkv_ref[i * pieces + j, 1])
            v_s[i, :, part] = qkv_ref[i * pieces + j, 2]
    factor = math.log2(math.e) / math.sqrt(HDIM)
    key_line = lax.broadcasted_iota(jnp.int32, (TILE, TILE), 0)
    query_line = lax.broadcasted_iota(jnp.int32, (TILE, TILE), 1)
    for i in range(blocks):
        query = q_s[i]
        begin = start_ref[:, i * TILE : (i + 1) * TILE]
        peak = None
        for b in range(i + 1):
            s = dot(k_s[b], query, 1, 0) * factor
            keep = key_line >= begin - b * TILE
            if b == i:
                keep = keep & (key_line <= query_line)
            s = jnp.where(keep, s, -1e30)
            s_s[b] = s
            high = jnp.max(s, axis=0, keepdims=True)
            peak = high if peak is None else jnp.maximum(peak, high)
        total = jnp.zeros((1, TILE), F32)
        acc = jnp.zeros((HDIM, TILE), F32)
        for b in range(i + 1):
            e = jnp.exp2(s_s[b] - peak)
            total = total + jnp.sum(e, axis=0, keepdims=True)
            acc = acc + dot(v_s[b], e.astype(BF16), 1, 0)
        out = acc / total
        for j in range(pieces):
            out_ref[i * pieces + j] = out[:, j * 128 : (j + 1) * 128]
            low_ref[i * pieces + j] = out[:, j * 128 : (j + 1) * 128].astype(BF16)
        top_ref[:, i * TILE : (i + 1) * TILE] = peak + jnp.log2(total)


def backward_kernel(
    qkv_ref, do_ref, o_ref, top_ref, start_ref, rot_ref, out_ref,
    qt_s, kt_s, dot_s, q_s, k_s, v_s, do_s, dq_s, dk_s, dv_s,
):
    blocks = qt_s.shape[0]
    pieces = TILE // 128
    for i in range(blocks):
        for j in range(pieces):
            part = slice(j * 128, (j + 1) * 128)
            c = i * pieces + j
            qt_s[i, :, part] = qkv_ref[c, 0]
            kt_s[i, :, part] = qkv_ref[c, 1]
            dot_s[i, :, part] = do_ref[c]
            q_s[i, part, :] = turned(qkv_ref[c, 0])
            k_s[i, part, :] = turned(qkv_ref[c, 1])
            v_s[i, part, :] = turned(qkv_ref[c, 2])
            do_s[i, part, :] = turned(do_ref[c])
    scale = 1.0 / math.sqrt(HDIM)
    factor = math.log2(math.e) * scale
    key_line = lax.broadcasted_iota(jnp.int32, (TILE, TILE), 0)
    query_line = lax.broadcasted_iota(jnp.int32, (TILE, TILE), 1)
    for i in range(blocks):
        span = slice(i * TILE, (i + 1) * TILE)
        begin = start_ref[:, span]
        top = top_ref[:, span]
        delta = jnp.concatenate(
            [
                jnp.sum(
                    do_ref[i * pieces + j].astype(F32) * o_ref[i * pieces + j],
                    axis=0,
                    keepdims=True,
                )
                for j in range(pieces)
            ],
            axis=1,
        )
        dq = jnp.zeros((HDIM, TILE), F32)
        for b in range(i + 1):
            s = dot(k_s[b], qt_s[i], 1, 0) * factor
            keep = key_line >= begin - b * TILE
            if b == i:
                keep = keep & (key_line <= query_line)
            p = jnp.where(keep, jnp.exp2(s - top), 0.0)
            dp = dot(v_s[b], dot_s[i], 1, 0)
            ds = (p * (dp - delta)).astype(BF16)
            dq = dq + dot(kt_s[b], ds, 1, 0)
            dk = dot(ds, q_s[i], 1, 0)
            dv = dot(p.astype(BF16), do_s[i], 1, 0)
            if b == i:
                dk_s[b] = dk
                dv_s[b] = dv
            else:
                dk_s[b] += dk
                dv_s[b] += dv
        dq_s[i] = dq
    for i in range(blocks):
        span = slice(i * TILE, (i + 1) * TILE)
        dq = dq_s[i] * scale
        dk = jnp.transpose(dk_s[i]) * scale
        dv = jnp.transpose(dv_s[i])
        results = []
        for n, g in enumerate((dq, dk)):
            co, si = rot_ref[2 * n, :, span], rot_ref[2 * n + 1, :, span]
            front, back = g[:HALF], g[HALF:]
            results.append(
                jnp.concatenate([front * co + back * si, back * co - front * si], axis=0)
            )
        results.append(dv)
        for n, g in enumerate(results):
            for j in range(pieces):
                out_ref[i * pieces + j, n] = g[:, j * 128 : (j + 1) * 128].astype(BF16)


def attend(qkv, start):
    count = qkv.shape[0]
    blocks = count * 128 // TILE
    return pl.pallas_call(
        forward_kernel,
        out_shape=(
            pltpu.HBM((count, HDIM, 128), F32),
            pltpu.HBM((count, HDIM, 128), BF16),
            jax.ShapeDtypeStruct((1, count * 128), F32),
        ),
        scratch_shapes=[
            pltpu.VMEM((blocks, HDIM, TILE), BF16),
            pltpu.VMEM((blocks, TILE, HDIM), BF16),
            pltpu.VMEM((blocks, HDIM, TILE), BF16),
            pltpu.VMEM((blocks, TILE, TILE), F32),
        ],
        compiler_params=pltpu.CompilerParams(vmem_limit_bytes=20 * MIB),
        cost_estimate=pl.CostEstimate(
            flops=2000000000, bytes_accessed=4000000, transcendentals=2400000
        ),
        name="attend",
    )(qkv, start)


def attend_back(qkv, d_out, out, top, start, tables):
    count = qkv.shape[0]
    blocks = count * 128 // TILE
    wide = pltpu.VMEM((blocks, HDIM, TILE), BF16)
    tall = pltpu.VMEM((blocks, TILE, HDIM), BF16)
    return pl.pallas_call(
        backward_kernel,
        out_shape=pltpu.HBM((count, 3, HDIM, 128), BF16),
        scratch_shapes=[
            wide, wide, wide, tall, tall, tall, tall,
            pltpu.VMEM((blocks, HDIM, TILE), F32),
            pltpu.VMEM((blocks, TILE, HDIM), F32),
            pltpu.VMEM((blocks, TILE, HDIM), F32),
        ],
        compiler_params=pltpu.CompilerParams(vmem_limit_bytes=28 * MIB),
        cost_estimate=pl.CostEstimate(
            flops=6000000000, bytes_accessed=6000000, transcendentals=2400000
        ),
        name="attend_back",
    )(qkv, d_out, out, top, start, tables)


def rotation_tables(row_slots):
    index_half = np.arange(HALF, dtype=np.float64)
    places = np.arange(row_slots, dtype=np.float64) - row_slots // 2
    inverse = rope_base ** (-2.0 * index_half / HDIM)
    angles = inverse[:, None] * places[None, :]
    zeta = (2.0 * index_half + 0.4 * HDIM) / (1.4 * HDIM)
    stretch = zeta[:, None] ** (places[None, :] / xpos_base)
    cosine, sine = np.cos(angles), np.sin(angles)
    tables = [cosine * stretch, sine * stretch, cosine / stretch, sine / stretch]
    return np.stack(tables).astype(np.float32)


def moments(values):
    center = jnp.mean(values, axis=-1, keepdims=True)
    spread = jnp.mean(jnp.square(values - center), axis=-1, keepdims=True)
    inverse = lax.rsqrt(spread + norm_eps)
    return (values - center) * inverse, inverse


def norm_back(upstream, gain, normed, inverse):
    scaled = upstream * gain
    return inverse * (
        scaled
        - jnp.mean(scaled, axis=-1, keepdims=True)
        - normed * jnp.mean(scaled * normed, axis=-1, keepdims=True)
    )


def place_parts(parts, target, me):
    share = parts[0].shape[0]
    for k, part in enumerate(parts):
        target[pl.ds(pl.multiple_of((me ^ k) * share, share), share), :] = part[...]


def take_for_scatter(source, target, me):
    share = source.shape[0] // 8
    for side in range(2):
        for j in range(4):
            at = pl.multiple_of((me ^ (2 * j + side)) * share, share)
            target[pl.ds((side * 4 + j) * share, share), :] = source[pl.ds(at, share), :]


def scatter_product(left, right, keep_ref, send_ref, width=None):
    half = left.shape[0] // 2
    width = width or keep_ref.shape[1]
    step = 256

    def body(i, _):
        at = pl.ds(pl.multiple_of(i * step, step), step)
        product = dot(left[...], right[at, : left.shape[1]], 1, 1)
        keep_ref[:, at] = product[:half]
        send_ref[:, at] = product[half:].astype(BF16)
        return 0

    lax.fori_loop(0, width // step, body, 0)


def project_kernel(
    ids, here_ref, near_ref, far_ref, pre_ref, rot_ref, w_ref, qkv_ref, hat_ref, a_ref, x_s, y_s
):
    half, core = ids[1], ids[2]
    rows, slots, width = here_ref.shape
    other = (1 - half) * slots
    for r in range(rows):
        x_s[pl.ds(pl.multiple_of(half * slots, slots), slots), :] = here_ref[r]
        x_s[pl.ds(pl.multiple_of(other + core * 32, 32), 32), :] = near_ref[r]
        x_s[pl.ds(pl.multiple_of(other + (1 - core) * 32, 32), 32), :] = far_ref[r]
        normed, _ = moments(x_s[...].astype(F32))
        low = normed * pre_ref[0:1] + pre_ref[1:2]
        hat_ref[r * 2 * slots : (r + 1) * 2 * slots, :] = normed.astype(BF16)
        a_ref[r * 2 * slots : (r + 1) * 2 * slots, :] = low.astype(BF16)
    span = 2 * slots
    heads = y_s.shape[1] // HDIM
    for n in range(3):
        y_s[...] = dot(a_ref[...], w_ref[:, n * heads * HDIM : (n + 1) * heads * HDIM], 1, 0)
        for r in range(rows):
            for pair in range(heads // 2):
                t = jnp.transpose(
                    y_s[r * span : (r + 1) * span, pair * 128 : (pair + 1) * 128]
                )
                for e in range(2):
                    g = t[e * HDIM : (e + 1) * HDIM]
                    if n < 2:
                        co, si = rot_ref[2 * n], rot_ref[2 * n + 1]
                        front, back = g[:HALF], g[HALF:]
                        g = jnp.concatenate(
                            [front * co - back * si, front * si + back * co], axis=0
                        )
                    qkv_ref[r * heads + pair * 2 + e, n] = g.astype(BF16)


def inner_moments(sums_ref, width, row=0):
    sums = sums_ref[0]
    for k in range(1, 8):
        sums = sums + sums_ref[k]
    center = sums[row : row + 1] / width
    inverse = lax.rsqrt(sums[row + 1 : row + 2] / width - center * center + norm_eps)
    return sums, center, inverse


def high_low(value):
    high = value.astype(BF16).astype(F32)
    return [high, value - high]


def out_kernel(
    ids, o_ref, gain_ref, w_ref, keep_ref, send_ref, line_ref, c_s, sum_s, l_s, k_s
):
    count, _, span = o_ref.shape
    heads = count // 4
    width = w_ref.shape[0]
    half = keep_ref.shape[0]
    for r in range(4):
        o = jnp.concatenate([o_ref[r * heads + h] for h in range(heads)], axis=0).astype(F32)
        first = jnp.sum(o, axis=0, keepdims=True)
        second = jnp.sum(o * o, axis=0, keepdims=True)
        line_ref[0:1, r * span : (r + 1) * span] = first
        line_ref[1:2, r * span : (r + 1) * span] = second
        lines = [first, second, *high_low(first), *high_low(second)]
        lines.append(jnp.zeros((128 - len(lines), span), F32))
        sums = jnp.transpose(jnp.concatenate(lines, axis=0))
        c = jnp.transpose(o * gain_ref[...]).astype(BF16)
        for s in range(8):
            at = slice(s * 64 + r * 16, s * 64 + (r + 1) * 16)
            c_s[at, :] = c[s * 16 : (s + 1) * 16]
            sum_s[at, :] = sums[s * 16 : (s + 1) * 16]
    take_for_scatter(c_s, l_s, ids[0])
    take_for_scatter(sum_s, k_s, ids[0])
    scatter_product(l_s, w_ref, keep_ref, send_ref, width)
    keep_ref[:, width:] = k_s[:half]
    send_ref[:, width:] = k_s[half:].astype(BF16)


def normed_heads_kernel(o_ref, sums_ref, gain_ref, shift_ref, c_ref, *, width):
    count, _, span = o_ref.shape
    heads = count // 4
    _, center, inverse = inner_moments(sums_ref, width, 4)
    for r in range(4):
        at = slice(r * span, (r + 1) * span)
        o = jnp.concatenate([o_ref[r * heads + h] for h in range(heads)], axis=0).astype(F32)
        c = (o - center[:, at]) * inverse[:, at] * gain_ref[...] + shift_ref[...]
        c = jnp.transpose(c).astype(BF16)
        for s in range(8):
            c_ref[s * 64 + r * 16 : s * 64 + (r + 1) * 16, :] = c[s * 16 : (s + 1) * 16]


def gain_product_kernel(gain_ref, shift_ref, w_ref, out_ref):
    rows = [*high_low(gain_ref[...]), *high_low(shift_ref[...])]
    rows = jnp.concatenate(rows + [jnp.zeros((12, rows[0].shape[1]), F32)], axis=0).astype(BF16)
    product = dot(rows, w_ref[...], 1, 1)
    both = [product[0:1] + product[1:2], product[2:3] + product[3:4]]
    out_ref[...] = jnp.concatenate(both + [jnp.zeros((6, product.shape[1]), F32)], axis=0)


def two_sums(stats, other):
    first = stats[:, 0:1] + (other[:, 2:3] + other[:, 3:4])
    second = stats[:, 1:2] + (other[:, 4:5] + other[:, 5:6])
    return first, second


def core_sum_stats_kernel(keep_ref, got_ref, own_ref, one_ref, two_ref, three_ref):
    share = own_ref.shape[0]
    width = own_ref.shape[1] - 128
    both = keep_ref[:, :width] + got_ref[:, :width].astype(F32)
    first, second = two_sums(keep_ref[:, width:], got_ref[:, width:].astype(F32))
    lane = lax.broadcasted_iota(jnp.int32, (keep_ref.shape[0], 128), 1)
    stats = jnp.zeros(lane.shape, F32)
    for n, v in enumerate([first, second, *high_low(first), *high_low(second)]):
        stats = jnp.where(lane == n, v, stats)
    own_ref[:, :width] = both[:share]
    own_ref[:, width:] = stats[:share]
    for j, ref in ((1, one_ref), (2, two_ref), (3, three_ref)):
        ref[:, :width] = both[j * share : (j + 1) * share].astype(BF16)
        ref[:, width:] = stats[j * share : (j + 1) * share].astype(BF16)


def core_sum_kernel(keep_ref, got_ref, own_ref, one_ref, two_ref, three_ref):
    share = own_ref.shape[0]
    both = keep_ref[...] + got_ref[...].astype(F32)
    own_ref[...] = both[:share]
    for j, ref in ((1, one_ref), (2, two_ref), (3, three_ref)):
        ref[...] = both[j * share : (j + 1) * share].astype(BF16)


def summed(own_ref, refs):
    total = own_ref[...]
    for ref in refs:
        total = total + ref[...].astype(F32)
    return total


def middle_kernel(
    own_ref, one, two, three, x_ref, usable_ref, pre_ref, g_ref, g_one, g_two, g_three,
    r1_ref, bb_ref,
):
    width = r1_ref.shape[1]
    total = own_ref[...]
    product, stats = total[:, :width], total[:, width:]
    for ref in (one, two, three):
        product = product + ref[:, :width].astype(F32)
        first, second = two_sums(stats, ref[:, width:].astype(F32))
        lane = lax.broadcasted_iota(jnp.int32, stats.shape, 1)
        stats = jnp.where(lane == 0, first, jnp.where(lane == 1, second, 0.0))
    center = stats[:, 0:1] / width
    inverse = lax.rsqrt(stats[:, 1:2] / width - center * center + norm_eps)
    g = (g_ref[...] + g_one[...]) + (g_two[...] + g_three[...])
    attn = inverse * (product - center * g[0:1]) + g[1:2]
    r1 = x_ref[...].astype(F32) + usable_ref[...] * attn
    normed, _ = moments(r1)
    r1_ref[...] = r1
    bb_ref[...] = (normed * pre_ref[2:3] + pre_ref[3:4]).astype(BF16)


def result_kernel(own_ref, one, two, three, r1_ref, usable_ref, out_ref):
    f = summed(own_ref, (one, two, three))
    out_ref[...] = (r1_ref[...] + usable_ref[...] * f).astype(BF16)


def down_back_kernel(ids, *refs):
    parts, (w_ref, df_ref, dhn_ref) = refs[:8], refs[8:]
    place_parts(parts, df_ref, ids[0])

    def body(i, _):
        at = pl.ds(pl.multiple_of(i * 256, 256), 256)
        dhn_ref[:, at] = dot(df_ref[...], w_ref[:, at], 1, 0)
        return 0

    lax.fori_loop(0, dhn_ref.shape[1] // 256, body, 0)


def up_kernel(ids, *refs):
    parts, refs = refs[:8], refs[8:]
    w_ref, dhn_ref, gain_ref, o_ref, bb_ref, h_ref, slope_ref, sums_ref = refs
    place_parts(parts, bb_ref, ids[0])
    tokens, units = h_ref.shape
    step = 256

    def body(i, carry):
        at = pl.ds(pl.multiple_of(i * step, step), step)
        u = dot(bb_ref[...], w_ref[:, at], 1, 0)
        cdf = 0.5 * (1.0 + lax.erf(u * (1.0 / math.sqrt(2.0))))
        h = u * cdf
        h_ref[:, at] = h
        slope_ref[:, at] = cdf + u * (
            jnp.exp(-0.5 * u * u) * (1.0 / math.sqrt(2.0 * math.pi))
        )
        scaled = dhn_ref[:, at] * gain_ref[:, at]
        terms = (h, h * h, scaled, scaled * h)
        return tuple(c + jnp.sum(t, axis=1, keepdims=True) for c, t in zip(carry, terms))

    zero = jnp.zeros((tokens, 1), F32)
    sums = lax.fori_loop(0, units // step, body, (zero,) * 4)
    lane = lax.broadcasted_iota(jnp.int32, (tokens, 128), 1)
    wide = jnp.zeros((tokens, 128), F32)
    for n, s in enumerate(sums):
        wide = jnp.where(lane == n, s, wide)
    line = jnp.transpose(wide)
    line = jnp.concatenate([line[:4], o_ref[...], line[6:8]], axis=0)
    for k in range(8):
        sums_ref[k] = line


def inner_back_kernel(
    ids, h_ref, slope_ref, dhn_ref, sums_ref, gain_ref, shift_ref, w_ref,
    keep_ref, send_ref, hn_ref, du_ref, sub_ref, l_s,
):
    sums, center, inverse = inner_moments(sums_ref, FF)
    mean_scaled = sums[2:3] / FF
    mean_both = inverse * (sums[3:4] / FF - center * mean_scaled)
    rows = jnp.concatenate([center, inverse, mean_scaled, mean_both, sums[4:8]], axis=0)
    columns = jnp.transpose(jnp.concatenate([rows] * 16, axis=0))
    tokens = h_ref.shape[0]
    center, inverse, mean_scaled, mean_both = (columns[:, n : n + 1] for n in range(4))
    units = h_ref.shape[1]

    def body(i, _):
        at = pl.ds(pl.multiple_of(i * 256, 256), 256)
        hat = (h_ref[:, at] - center) * inverse
        dhn = dhn_ref[:, at]
        gain = gain_ref[:, at]
        hn_ref[:, at] = (hat * gain + shift_ref[:, at]).astype(BF16)
        du = inverse * (dhn * gain - mean_scaled - hat * mean_both) * slope_ref[:, at]
        du_ref[:, at] = du.astype(BF16)
        sub_ref[0:1, at] = jnp.sum(dhn * hat, axis=0, keepdims=True)
        sub_ref[1:2, at] = jnp.sum(dhn, axis=0, keepdims=True)
        return 0

    lax.fori_loop(0, units // 256, body, 0)
    take_for_scatter(du_ref, l_s, ids[0])
    scatter_product(l_s, w_ref, keep_ref, send_ref)


def down_kernel(ids, hn_ref, w_ref, keep_ref, send_ref, l_s):
    take_for_scatter(hn_ref, l_s, ids[0])
    scatter_product(l_s, w_ref, keep_ref, send_ref)


def mlp_grad_kernel(df_ref, hn_ref, bb_ref, du_ref, out_ref):
    units = hn_ref.shape[1]
    out_ref[:, :units] = dot(jnp.transpose(bb_ref[...]), du_ref[...], 1, 0).astype(BF16)
    out_ref[:, units:] = dot(jnp.transpose(df_ref[...]), hn_ref[...], 1, 0).astype(BF16)


def mlp_grad(df, hn, bb, du):
    tokens, width = df.shape
    units = hn.shape[1]
    step = 256
    narrow = pl.BlockSpec((tokens, step), lambda i: (0, i))
    whole = pl.BlockSpec((tokens, units), lambda i: (0, 0))
    return pl.pallas_call(
        mlp_grad_kernel,
        grid=(width // step,),
        out_shape=pltpu.HBM((width, 2 * units), BF16),
        in_specs=[narrow, whole, narrow, whole],
        out_specs=pl.BlockSpec((step, 2 * units), lambda i: (i, 0)),
        compiler_params=pltpu.CompilerParams(vmem_limit_bytes=20 * MIB),
        cost_estimate=pl.CostEstimate(
            flops=4 * tokens * width * units, bytes_accessed=14 * MIB, transcendentals=0
        ),
        name="mlp_grad",
    )(df, hn, bb, du)


def middle_back_kernel(
    own_ref, one, two, three, r1_ref, cot_ref, usable_ref, pre_ref, dr1_ref, dattn_ref, grad_ref
):
    dbb = summed(own_ref, (one, two, three))
    hat, inverse = moments(r1_ref[...])
    dr1 = cot_ref[...].astype(F32) + norm_back(dbb, pre_ref[2:3], hat, inverse)
    dr1_ref[...] = dr1
    dattn_ref[...] = (usable_ref[...] * dr1).astype(BF16)
    grad_ref[0:1] = jnp.sum(dbb * hat, axis=0, keepdims=True)
    grad_ref[1:2] = jnp.sum(dbb, axis=0, keepdims=True)


def out_back_kernel(ids, *refs):
    parts, refs = refs[:8], refs[8:]
    w_ref, o_ref, sums_ref, gain_ref, dattn_ref, dc_ref, out_ref, sub_ref, y_s = refs
    place_parts(parts, dattn_ref, ids[0])
    y_s[...] = dot(dattn_ref[...], w_ref[...], 1, 0)
    count, _, span = o_ref.shape
    heads = count // 4
    _, center, inverse = inner_moments(sums_ref, dattn_ref.shape[1], 4)
    gain_grad, shift_grad, lines = 0.0, 0.0, []
    for r in range(4):
        at = slice(r * span, (r + 1) * span)
        dc = jnp.concatenate(
            [y_s[s * 64 + r * 16 : s * 64 + (r + 1) * 16, :] for s in range(8)], axis=0
        )
        dc = jnp.transpose(dc)
        dc_ref[:, at] = dc
        o = jnp.concatenate([o_ref[r * heads + h] for h in range(heads)], axis=0).astype(F32)
        hat = (o - center[:, at]) * inverse[:, at]
        gain_grad = gain_grad + jnp.sum(dc * hat, axis=1, keepdims=True)
        shift_grad = shift_grad + jnp.sum(dc, axis=1, keepdims=True)
        scaled = dc * gain_ref[...]
        lines.append(
            jnp.concatenate(
                [
                    jnp.sum(scaled, axis=0, keepdims=True),
                    jnp.sum(scaled * hat, axis=0, keepdims=True),
                    jnp.zeros((6, span), F32),
                ],
                axis=0,
            )
        )
    line = jnp.concatenate(lines, axis=1)
    for k in range(8):
        out_ref[k] = line
    sub_ref[...] = jnp.concatenate(
        [
            jnp.transpose(jnp.broadcast_to(g, (g.shape[0], 128)))[0:1]
            for g in (gain_grad, shift_grad)
        ],
        axis=0,
    )


def head_grad_kernel(dc_ref, o_ref, sums_ref, back_ref, gain_ref, out_ref, *, width):
    count, _, span = o_ref.shape
    heads = count // 4
    _, center, inverse = inner_moments(sums_ref, width, 4)
    back = back_ref[0]
    for k in range(1, 8):
        back = back + back_ref[k]
    for r in range(4):
        at = slice(r * span, (r + 1) * span)
        first, second = back[0:1, at] / width, back[1:2, at] / width
        for h in range(heads):
            part = slice(h * HDIM, (h + 1) * HDIM)
            hat = (o_ref[r * heads + h].astype(F32) - center[:, at]) * inverse[:, at]
            scaled = dc_ref[part, at] * gain_ref[part]
            out_ref[r * heads + h] = (
                inverse[:, at] * (scaled - first - hat * second)
            ).astype(BF16)


def out_grad_kernel(dattn_ref, c_ref, out_ref):
    out_ref[...] = dot(jnp.transpose(dattn_ref[...]), c_ref[...], 1, 0).astype(BF16)


def out_grad(dattn, c):
    tokens, width = dattn.shape
    units = c.shape[1]
    step = 512
    return pl.pallas_call(
        out_grad_kernel,
        grid=(width // step,),
        out_shape=pltpu.HBM((width, units), BF16),
        in_specs=[
            pl.BlockSpec((tokens, step), lambda i: (0, i)),
            pl.BlockSpec((tokens, units), lambda i: (0, 0)),
        ],
        out_specs=pl.BlockSpec((step, units), lambda i: (i, 0)),
        compiler_params=pltpu.CompilerParams(vmem_limit_bytes=16 * MIB),
        cost_estimate=pl.CostEstimate(
            flops=2 * tokens * width * units, bytes_accessed=4 * MIB, transcendentals=0
        ),
        name="out_grad",
    )(dattn, c)


def turn_kernel(ids, a_ref, out_ref):
    for r in range(16):
        at = pl.ds(pl.multiple_of((ids[3] ^ r) * 128, 128), 128)
        to = (r % 4) * 4 + r // 4
        out_ref[to * 128 : (to + 1) * 128, :] = jnp.transpose(a_ref[:, at])


def column(row):
    return jnp.transpose(jnp.broadcast_to(row, (128, row.shape[1])))[:, 0:1]


def row_of(col):
    return jnp.transpose(jnp.broadcast_to(col, (col.shape[0], 128)))[0:1]


def in_grad_kernel(
    ids, dqkv_ref, xt_ref, w_ref, pre_ref, out_ref, three_ref, o_ref, h_ref, *refs
):
    lines, (tokens_ref, d_s, one_s) = refs[:8], refs[8:]
    count = dqkv_ref.shape[0]
    heads = count // 4
    units = d_s.shape[0]
    for r in range(4):
        for n in range(3):
            for h in range(heads):
                base = (n * heads + h) * HDIM
                d_s[base : base + HDIM, r * 128 : (r + 1) * 128] = dqkv_ref[r * heads + h, n]
    sums = []
    for n in range(0, units, 128):
        total = jnp.zeros((1, 128), F32)
        for r in range(4):
            t = jnp.transpose(d_s[n : n + 128, r * 128 : (r + 1) * 128].astype(F32))
            total = total + jnp.sum(t, axis=0, keepdims=True)
            t = t.astype(BF16)
            for s in range(8):
                tokens_ref[s * 64 + r * 16 : s * 64 + (r + 1) * 16, n : n + 128] = t[
                    s * 16 : (s + 1) * 16
                ]
        sums.append(total)
    sums = jnp.concatenate(sums, axis=1)
    for j in range(4):
        products = dot(xt_ref[j * 512 : (j + 1) * 512, :], d_s[...], 1, 1)
        for i in range(4):
            at = pl.ds(pl.multiple_of((ids[3] ^ (4 * i + j)) * 128, 128), 128)
            product = products[i * 128 : (i + 1) * 128]
            gradient = product * column(pre_ref[0:1, at]) + column(pre_ref[1:2, at]) * sums
            gradient = gradient.astype(BF16)
            lines[j][i * 64 : (i + 1) * 64, :units] = gradient[:64]
            lines[4 + i][j * 64 : (j + 1) * 64, :units] = gradient[64:]
            outward = out_ref[at, :]
            lines[j][i * 64 : (i + 1) * 64, units:] = outward[:64]
            lines[4 + i][j * 64 : (j + 1) * 64, units:] = outward[64:]
            w = w_ref[at, :units].astype(F32)
            one_s[0:1, at] = row_of(jnp.sum(w * product, axis=1, keepdims=True))
            one_s[1:2, at] = row_of(jnp.sum(w * sums, axis=1, keepdims=True))
    width = lines[0].shape[1]
    half = o_ref.shape[1]
    small = []
    for ref in (one_s, three_ref):
        for n in range(2):
            small += [ref[n : n + 1, :width], ref[n : n + 1, width:]]
    for n in range(2):
        first = [o_ref[n : n + 1], h_ref[n : n + 1, : width - half]]
        last = [h_ref[n : n + 1, width - half :], jnp.zeros((1, width - half), F32)]
        small += [jnp.concatenate(first, axis=1), jnp.concatenate(last, axis=1)]
    small.append(jnp.zeros((16 - len(small), width), F32))
    small = jnp.concatenate(small, axis=0).astype(BF16)
    for j in range(4):
        lines[j][256:272, :] = small


def in_back_kernel(ids, d_ref, w_ref, keep_ref, send_ref, l_s):
    take_for_scatter(d_ref, l_s, ids[0])
    scatter_product(l_s, w_ref, keep_ref, send_ref)


def summed_low(refs):
    total = refs[0][...].astype(F32)
    for ref in refs[1:]:
        total = total + ref[...].astype(F32)
    return total


def line_sum_kernel(*refs):
    first, second, outs = refs[:4], refs[4:8], refs[8:]
    total = summed_low(first)
    small = total[256:272]
    outs[0][0:64, :] = total[0:64]
    outs[0][64:80, :] = small
    for k in (1, 2, 3):
        outs[k][0:64, :] = total[k * 64 : (k + 1) * 64].astype(BF16)
        outs[k][64:80, :] = small.astype(BF16)
    total = summed_low(second)
    outs[4][...] = total[0:64]
    for k in (1, 2, 3):
        outs[4 + k][...] = total[k * 64 : (k + 1) * 64].astype(BF16)


def last_sum_kernel(ids, *refs):
    ins, (mlp_ref, keep_ref, give_ref, out_ref) = refs[:8], refs[8:]
    width = keep_ref.shape[1]
    low = ids[1] == 0
    second = summed_low(ins[4:])
    slots = second.shape[0]
    total = summed_low(ins[:4])
    first, small = total[:slots], total[slots:]
    keep_ref[:slots, :] = jnp.where(low, first, second).astype(BF16)
    give_ref[:slots, :] = jnp.where(low, second, first).astype(BF16)
    keep_ref[slots:, :] = small.astype(BF16)
    give_ref[slots:, :] = small.astype(BF16)
    squares = whole_sum(first * first + second * second) + mlp_ref[0:1, 0:1]

    def joined(begin):
        return jnp.concatenate([small[begin : begin + 1], small[begin + 1 : begin + 2]], axis=1)

    sub = jnp.concatenate([joined(8), joined(10)], axis=0)
    lane = lax.broadcasted_iota(jnp.int32, (4, 2 * width), 1)
    scalars = jnp.zeros(lane.shape, F32)
    for n, term in enumerate([*high_low(squares), *high_low(whole_sum(sub * sub))]):
        scalars = jnp.where(lane // 128 == n, term, scalars)
    lines = jnp.concatenate([joined(2 * n) for n in range(4)] + [scalars], axis=0).astype(BF16)
    for k in range(out_ref.shape[0]):
        out_ref[k] = lines


def group_total_kernel(small_ref, total_ref, out_ref):
    total = small_ref[0].astype(F32)
    for k in range(1, small_ref.shape[0]):
        total = total + small_ref[k].astype(F32)
    total_ref[...] = total
    squares = total[4:5, 0:128] + total[4:5, 128:256]
    for k in range(out_ref.shape[0]):
        out_ref[k] = jnp.broadcast_to(squares, out_ref.shape[1:])


def input_back_kernel(own_ref, one, two, three, x_ref, dr1_ref, pre_ref, out_ref):
    da = summed(own_ref, (one, two, three))
    hat, inverse = moments(x_ref[...].astype(F32))
    out_ref[...] = (dr1_ref[...] + norm_back(da, pre_ref[0:1], hat, inverse)).astype(BF16)


def whole_sum(values):
    return jnp.sum(jnp.sum(values, axis=1, keepdims=True), axis=0, keepdims=True)


def rest_kernel(ids, g_ref, keep_ref, give_ref, sum_ref):
    slots = keep_ref.shape[0]
    half = ids[1]
    keep_ref[...] = g_ref[pl.ds(pl.multiple_of(half * slots, slots), slots), :]
    give_ref[...] = g_ref[pl.ds(pl.multiple_of((1 - half) * slots, slots), slots), :]
    total = jnp.zeros((1, 1), F32)
    for k in range(g_ref.shape[0] // 32):
        g = g_ref[k * 32 : (k + 1) * 32, :].astype(F32)
        total = total + whole_sum(g * g)
    sum_ref[...] = jnp.broadcast_to(total, sum_ref.shape)


def adam_step(weight, moment, squares, gradient, factor, step_rate, decay_weight):
    clipped = gradient * factor
    moment_new = beta_first * moment + (1.0 - beta_first) * clipped
    squares_new = beta_second * squares + (1.0 - beta_second) * clipped * clipped
    moment_hat = moment_new * (1.0 / (1.0 - beta_first**STEP))
    squares_hat = squares_new * (1.0 / (1.0 - beta_second**STEP))
    updated = weight - step_rate * (
        moment_hat / (jnp.sqrt(squares_hat) + adam_eps) + decay_weight * weight
    )
    return updated, moment_new, squares_new


def adam_kernel(
    ids, small_ref, norm_part, sub_own, sub_take, att_keep, att_take, mlp_keep, mlp_take, *refs
):
    states, outs, norm_out = refs[:18], refs[18:36], refs[36]
    low = ids[1] == 0
    squares = norm_part[0, 0:1, 0:1]
    for k in range(1, norm_part.shape[0]):
        squares = squares + norm_part[k, 0:1, 0:1]
    pre = small_ref[0:4]
    squares = squares + small_ref[4:5, 256:257] + small_ref[4:5, 384:385] + whole_sum(pre * pre)
    norm = jnp.sqrt(squares)
    factor = jnp.minimum(1.0, clip_limit / (norm + 1e-06))
    half = att_keep.shape[1] // 4

    def pair(mine, theirs, at):
        mine = mine[:, at * half : (at + 1) * half].astype(F32)
        theirs = theirs[:, at * half : (at + 1) * half].astype(F32)
        return jnp.concatenate(
            [jnp.where(low, mine, theirs), jnp.where(low, theirs, mine)], axis=1
        )

    def step(which, index, gradient, rate, decay):
        state = [states[3 * which + n][index] for n in range(3)]
        for n, value in enumerate(adam_step(*state, gradient, factor, rate, decay)):
            outs[3 * which + n][index] = value

    everything = slice(None)
    for k in range(3):
        step(0, (k,), pair(att_keep, att_take, k), matrix_rate, decay_rate)
    step(1, (everything,), pair(att_keep, att_take, 3), matrix_rate, decay_rate)
    for b in range(4):
        step(2, (everything, b), pair(mlp_keep, mlp_take, b), matrix_rate, decay_rate)
        step(3, (b,), pair(mlp_keep, mlp_take, 4 + b), matrix_rate, decay_rate)

    @pl.when(pl.program_id(0) == 0)
    def _():
        step(4, (everything,), pre, norm_rate, 0.0)
        for b in range(5):
            row, at = (0, b) if b < 4 else (1, 0)
            both = pair(sub_own, sub_take, at)
            both = jnp.concatenate([both[8 + row : 9 + row], both[10 + row : 11 + row]], axis=0)
            step(5, (b,), both, norm_rate, 0.0)
        norm_out[...] = jnp.broadcast_to(norm, norm_out.shape)


def adam(ids, small, norm_part, gradients, states):
    flat = [a for state in states for a in state]
    step = 32

    def whole(a):
        return pl.BlockSpec(a.shape, lambda i, nd=a.ndim: (0,) * nd)

    def blocks(which, a):
        if which > 3:
            return whole(a)
        dim = (1, 0, 0, 1)[which]
        block = tuple(step if n == dim else d for n, d in enumerate(a.shape))
        return pl.BlockSpec(
            block, lambda i, nd=a.ndim, dim=dim: tuple(i if n == dim else 0 for n in range(nd))
        )

    specs = [blocks(n // 3, a) for n, a in enumerate(flat)]
    rows = [pl.BlockSpec((step, g.shape[1]), lambda i: (i, 0)) for g in gradients]
    a_rows = gradients[2].shape[0] // 16
    norm = shape((8, 128))
    return pl.pallas_call(
        adam_kernel,
        grid=(gradients[2].shape[0] // step,),
        out_shape=tuple(shape(a.shape) for a in flat) + (norm,),
        in_specs=[
            pl.BlockSpec(memory_space=pltpu.SMEM),
            whole(small),
            whole(norm_part),
            *(pl.BlockSpec((16, a.shape[1]), lambda i: (a_rows, 0)) for a in gradients[:2]),
            *rows,
            *specs,
        ],
        out_specs=tuple(specs) + (whole(norm),),
        compiler_params=pltpu.CompilerParams(vmem_limit_bytes=56 * MIB),
        cost_estimate=pl.CostEstimate(flops=0, bytes_accessed=12 * MIB, transcendentals=0),
        name="adam",
    )(ids, small, norm_part, *gradients[:2], *gradients, *flat)


def eight_parts(own, *meanwhile):
    lines = [lax.ppermute(own, YY, xor_pairs(4, k)) for k in (1, 2, 3)]
    if meanwhile:
        lines = [after(line, *meanwhile) for line in lines]
    lines = [own] + lines
    parts = []
    for line in lines:
        parts += [line, lax.ppermute(line, C, SWAP)]
    return parts


def core_scatter(keep, send, kernel=core_sum_kernel):
    share, width = keep.shape[0] // 4, keep.shape[1]
    got = lax.ppermute(send, C, SWAP)
    return local_call(
        kernel,
        "core_sum",
        [shape((share, width))] + [shape((share, width), BF16)] * 3,
        [keep, got],
        moved=5 * MIB,
    )


def line_scatter(own, *sent):
    return [own] + [lax.ppermute(s, YY, xor_pairs(4, k)) for k, s in zip((1, 2, 3), sent)]


def finish_scatter(keep, send, work=None, kernel=core_sum_kernel):
    own, *sent = core_scatter(keep, send, kernel)
    lines = line_scatter(own, *sent)
    if work is None:
        return lines
    done = work(own)
    return lines[:1] + [after(line, *done) for line in lines[1:]], done


def crossing(lines, first_axis, second_axis):
    first, second = list(lines[:4]), list(lines[4:])
    for k in (2, 1, 3):
        first[k] = lax.ppermute(first[k], first_axis, xor_pairs(4, k))
        second[k] = lax.ppermute(second[k], second_axis, xor_pairs(4, k))
    return first, second


def each_to_all(copies, axis):
    return lax.all_to_all(copies, axis, split_axis=0, concat_axis=0, tiled=True)


def after(value, *others):
    return lax.optimization_barrier((value, *others))[0]


def shards(
    hidden_in, cotangent, doc_lengths,
    inward, inward_moment, inward_squares,
    outward, outward_moment, outward_squares,
    upward, upward_moment, upward_squares,
    downward, downward_moment, downward_squares,
    prenorm, prenorm_moment, prenorm_squares,
    subnorm, subnorm_moment, subnorm_squares,
):
    rows, seq_slots, width = hidden_in.shape
    quarter = cotangent.shape[1]
    group_slots = 2 * seq_slots
    row_slots = group_slots * lax.axis_size(ZX)
    half = inward.shape[2] // 2
    heads = half // HDIM
    units = 4 * half
    tokens = rows * group_slots
    share = rows * quarter
    zx = lax.axis_index(ZX)
    row_index = lax.axis_index(Z)
    yh = lax.axis_index(YH)
    core = lax.axis_index(C)
    ffn = lax.axis_index(FFN)
    me = lax.axis_index(EIGHT)
    low_side = yh == 0
    first_core = core == 0
    ids = jnp.stack([me, yh, core, zx]).astype(jnp.int32)

    def mine_theirs(array, axis):
        low = array.astype(BF16)
        mine = lax.dynamic_slice_in_dim(low, yh * half, half, axis)
        theirs = lax.dynamic_slice_in_dim(low, (1 - yh) * half, half, axis)
        return mine, theirs

    def in_order(own, other):
        return jnp.concatenate(
            [jnp.where(low_side, own, other), jnp.where(low_side, other, own)], axis=0
        )

    def both_halves(pairs):
        other = lax.ppermute(jnp.concatenate([t for _, t in pairs], axis=1), YH, SWAP)
        own = jnp.concatenate([m for m, _ in pairs], axis=1)
        return in_order(own, other)

    def rows_of(pair, order):
        return tuple(jnp.transpose(t, order).reshape(seq_slots, -1) for t in pair)

    in_pair = rows_of(mine_theirs(inward, 2), (0, 1, 2))
    out_pair = rows_of(mine_theirs(outward, 0), (1, 0))
    up_pair = rows_of(mine_theirs(upward, 2), (0, 1, 2))
    down_pair = rows_of(mine_theirs(downward, 1), (2, 0, 1))
    w_att = both_halves([in_pair, out_pair])
    w_att = lax.all_gather(w_att, ZX, axis=0, tiled=True)
    w_out = w_att[:, 3 * half :]
    w_mlp = both_halves([up_pair, down_pair])
    w_mlp = lax.all_gather(w_mlp, ZX, axis=0, tiled=True)
    w_up, w_down = w_mlp[:, :units], w_mlp[:, units:]

    doc_ends = jnp.cumsum(doc_lengths, axis=1)
    places = jnp.arange(row_slots, dtype=jnp.int32)
    my_ends = lax.dynamic_slice_in_dim(doc_ends, row_index, 1, 0)
    start = jnp.max(
        jnp.where(places[None, :] >= my_ends.reshape(-1, 1), my_ends.reshape(-1, 1), 0),
        axis=0,
        keepdims=True,
    )
    own_places = zx * group_slots + me * quarter + jnp.arange(quarter, dtype=jnp.int32)
    own_usable = (own_places[None, :] < doc_ends[:, -1:]).astype(F32).reshape(share, 1)

    half_slots = seq_slots // 2
    sent = lax.dynamic_slice_in_dim(hidden_in, core * half_slots, half_slots, 1)
    got_near = lax.ppermute(sent, YY, [(i, 3 - i) for i in range(4)])
    got_far = lax.ppermute(got_near, C, SWAP)
    own_hidden = lax.dynamic_slice_in_dim(hidden_in, ffn * quarter, quarter, 1)
    own_hidden = own_hidden.reshape(share, width)
    own_cot = cotangent.reshape(share, width)
    df_own = (own_usable * own_cot.astype(F32)).astype(BF16)
    df_parts = eight_parts(after(df_own, got_near))

    tables = jnp.asarray(rotation_tables(row_slots))
    near = lax.dynamic_slice_in_dim(tables, zx * group_slots, group_slots, 2)
    qkv, x_hat = local_call(
        project_kernel,
        "project",
        [
            shape((rows * heads, 3, HDIM, group_slots), BF16),
            shape((tokens, width), BF16),
        ],
        [ids, hidden_in, got_near, got_far, after(prenorm, *df_parts), near, w_att],
        [
            pltpu.VMEM((tokens, width), BF16),
            pltpu.VMEM((group_slots, width), BF16),
            pltpu.VMEM((tokens, half), F32),
        ],
        flops=2 * tokens * width * 3 * half,
        moved=8 * MIB,
        far=(0, 1),
    )
    sub = lax.dynamic_slice_in_dim(subnorm, yh * half, half, 2)
    gain_o, shift_o = sub[0, 0].reshape(half, 1), sub[1, 0].reshape(half, 1)
    gain_h, shift_h = sub[0, 1:].reshape(1, units), sub[1, 1:].reshape(1, units)
    (gains,) = local_call(
        gain_product_kernel,
        "gain_product",
        [shape((8, width))],
        [sub[0, 0].reshape(1, half), sub[1, 0].reshape(1, half), after(w_out, x_hat)],
    )
    gains = gains + lax.ppermute(gains, C, SWAP)
    gains = [gains] + [lax.ppermute(gains, YY, xor_pairs(4, k)) for k in (2, 1, 3)]
    qkv = after(each_to_all(qkv, ZX), *gains)
    o_head, o_low, top = attend(qkv, start)
    o = each_to_all(o_low, ZX)
    (x_turned,) = local_call(
        turn_kernel, "turn", [shape((width, tokens), BF16)], [ids, x_hat], moved=4 * MIB, far=(0,)
    )

    stat = shape((8, 8, tokens))
    pieces = [shape((tokens // 2, width)), shape((tokens // 2, width), BF16)]
    wide = [shape((tokens // 2, width + 128)), shape((tokens // 2, width + 128), BF16)]
    keep, send, sums_o = local_call(
        out_kernel,
        "out",
        wide + [shape((2, tokens))],
        [ids, o, gain_o, w_out],
        [
            pltpu.VMEM((tokens, half), BF16),
            pltpu.VMEM((tokens, 128), F32),
            pltpu.VMEM((tokens, half), BF16),
            pltpu.VMEM((tokens, 128), F32),
        ],
        flops=2 * tokens * width * half,
        moved=4 * MIB,
    )
    scattered = finish_scatter(keep, send, kernel=core_sum_stats_kernel)
    r1, bb_own = local_call(
        middle_kernel,
        "middle",
        [shape((share, width)), shape((share, width), BF16)],
        scattered + [own_hidden, own_usable, prenorm] + gains,
        moved=3 * MIB,
        far=(0,),
    )

    df, dhn = local_call(
        down_back_kernel,
        "down_back",
        [shape((tokens, width), BF16), shape((tokens, units))],
        [ids] + df_parts + [after(w_down, bb_own)],
        flops=2 * tokens * width * units,
        moved=10 * MIB,
        stay=range(1, 9),
        far=(0,),
    )
    bb_parts = eight_parts(bb_own, dhn)
    bb, h, slope, sums_h = local_call(
        up_kernel,
        "up",
        [shape((tokens, width), BF16), shape((tokens, units)), shape((tokens, units)), stat],
        [ids] + bb_parts + [w_up, dhn, gain_h, sums_o],
        flops=2 * tokens * width * units,
        moved=14 * MIB,
        stay=range(1, 9),
        far=(0,),
    )
    sums_h = each_to_all(sums_h, EIGHT)
    keep, send, hn, du, sub_h = local_call(
        inner_back_kernel,
        "inner_back",
        pieces + [shape((tokens, units), BF16)] * 2 + [shape((2, units))],
        [ids, h, slope, dhn, sums_h, gain_h, shift_h, w_up],
        [pltpu.VMEM((tokens, units), BF16)],
        flops=2 * tokens * width * units,
        moved=14 * MIB,
        far=(2, 3),
    )
    scattered, (g_mlp,) = finish_scatter(
        keep, send, lambda own: [mlp_grad(df, hn, bb, after(du, own))]
    )
    g_mlp = lax.psum_scatter(after(g_mlp, *scattered), ZX, scatter_dimension=0, tiled=True)
    dr1, dattn_own, pre_three = local_call(
        middle_back_kernel,
        "middle_back",
        [shape((share, width)), shape((share, width), BF16), shape((2, width))],
        scattered + [r1, own_cot, own_usable, prenorm],
        moved=4 * MIB,
        far=(0,),
    )
    keep, send = local_call(
        down_kernel,
        "down",
        pieces,
        [ids, hn, w_down],
        [pltpu.VMEM((tokens, units), BF16)],
        flops=2 * tokens * width * units,
        moved=8 * MIB,
    )
    dattn_parts = eight_parts(dattn_own, keep)

    (c,) = local_call(
        lambda *refs: normed_heads_kernel(*refs, width=width),
        "normed_heads",
        [shape((tokens, half), BF16)],
        [o, sums_h, gain_o, shift_o],
        far=(0,),
    )
    dattn, dc, back_o, sub_o = local_call(
        out_back_kernel,
        "out_back",
        [shape((tokens, width), BF16), shape((half, tokens)), stat, shape((2, half))],
        [ids] + dattn_parts + [w_out, o, sums_h, gain_o],
        [pltpu.VMEM((tokens, half), F32)],
        flops=2 * tokens * width * half,
        moved=6 * MIB,
        stay=range(1, 9),
        far=(0,),
    )
    g_out = out_grad(dattn, c)
    back_o = after(each_to_all(back_o, EIGHT), g_out)
    (do,) = local_call(
        lambda *refs: head_grad_kernel(*refs, width=width),
        "head_grad",
        [shape((rows * heads, HDIM, group_slots), BF16)],
        [dc, o, sums_h, back_o, gain_o],
        moved=MIB,
    )
    f_parts = core_scatter(keep, after(send, *dattn_parts))
    do = after(each_to_all(do, ZX), x_turned, f_parts[0])
    scattered = line_scatter(*f_parts)
    dqkv = attend_back(qkv, do, o_head, top, start, tables)
    dqkv = each_to_all(after(dqkv, *scattered), ZX)

    both = 4 * half
    line = [shape((4 * seq_slots + 16, both), BF16)] * 4 + [shape((4 * seq_slots, both), BF16)] * 4
    *lines, dproj = local_call(
        in_grad_kernel,
        "in_grad",
        line + [shape((tokens, 3 * half), BF16)],
        [ids, dqkv, x_turned, w_att, prenorm, g_out, pre_three, sub_o, sub_h],
        [pltpu.VMEM((3 * half, tokens), BF16), pltpu.VMEM((2, width), F32)],
        flops=2 * tokens * width * 3 * half,
        moved=13 * MIB,
        far=range(8),
    )
    first, second = crossing(lines, X, Z)
    mlp_keep, mlp_give, squares_mlp = local_call(
        rest_kernel,
        "rest",
        [shape((seq_slots, 2 * units), BF16)] * 2 + [shape((8, 128))],
        [ids, after(g_mlp, dproj)],
        stay=(1,),
        far=(0,),
    )
    mlp_take = lax.ppermute(mlp_give, YH, SWAP)
    keep, send = local_call(
        in_back_kernel,
        "in_back",
        pieces,
        [ids, dproj, w_att],
        [pltpu.VMEM((tokens, 3 * half), BF16)],
        flops=2 * tokens * width * 3 * half,
        moved=7 * MIB,
    )
    da_parts = finish_scatter(keep, after(send, *first[1:], *second[1:], squares_mlp))
    piece = [shape((seq_slots + 16, both))] + [shape((seq_slots + 16, both), BF16)] * 3
    piece += [shape((seq_slots, both))] + [shape((seq_slots, both), BF16)] * 3
    lines = [*local_call(
        line_sum_kernel,
        "line_sum",
        piece,
        first + second,
        moved=6 * MIB,
    )]
    first, second = crossing(lines, Z, X)
    da_parts = da_parts[:1] + [after(part, *first[1:], *second[1:]) for part in da_parts[1:]]
    (own_grad,) = local_call(
        input_back_kernel,
        "input_back",
        [shape((share, width), BF16)],
        da_parts[:1] + [after(part, mlp_take) for part in da_parts[1:]] + [own_hidden, dr1, prenorm],
        moved=3 * MIB,
    )
    own_grad = own_grad.reshape(rows, quarter, width)
    line_grad = lax.ppermute(own_grad, YL, SWAP)
    grads = [own_grad, lax.ppermute(own_grad, C, SWAP), line_grad, lax.ppermute(line_grad, C, SWAP)]
    first_line = lax.axis_index(YL) == 0
    pairs = [
        jnp.concatenate([jnp.where(first_core, a, b), jnp.where(first_core, b, a)], axis=1)
        for a, b in (grads[:2], grads[2:])
    ]
    input_grad = jnp.concatenate(
        [jnp.where(first_line, *pairs), jnp.where(first_line, *pairs[::-1])], axis=1
    )

    grad_piece = shape((seq_slots + 16, 4 * half), BF16)
    att_keep, att_give, small = local_call(
        last_sum_kernel,
        "last_sum",
        [grad_piece, grad_piece, shape((8, 8, width), BF16)],
        [ids, *first, *second, squares_mlp],
        moved=MIB,
        far=(0,),
    )
    att_take = lax.ppermute(att_give, YH, SWAP)
    mlp_take = lax.ppermute(mlp_give, YH, SWAP)
    small = each_to_all(small, EIGHT)
    small_total, squares = local_call(
        group_total_kernel,
        "group_total",
        [shape((8, width)), shape((16, 8, 128))],
        [small],
        far=(0,),
    )
    squares = each_to_all(squares, ZX)
    hidden_out = local_call(
        result_kernel,
        "result",
        [shape((share, width), BF16)],
        scattered + [after(r1, small_total), own_usable],
        moved=3 * MIB,
        stay=range(5),
    )[0].reshape(rows, quarter, width)
    turns = ((1, 0, 2), (1, 0), (0, 1, 2), (0, 2, 1), (0, 1), (1, 0, 2))
    states = [
        (inward, inward_moment, inward_squares),
        (outward, outward_moment, outward_squares),
        (upward, upward_moment, upward_squares),
        (downward, downward_moment, downward_squares),
        (prenorm, prenorm_moment, prenorm_squares),
        (subnorm, subnorm_moment, subnorm_squares),
    ]
    *updated, norm = adam(
        ids,
        small_total,
        squares,
        [att_keep, att_take, mlp_keep, mlp_take],
        [tuple(jnp.transpose(a, turn) for a in state) for state, turn in zip(states, turns)],
    )
    updated = [jnp.transpose(a, turns[n // 3]) for n, a in enumerate(updated)]
    return (hidden_out, input_grad, *updated, norm[0, 0])


def solution(mesh):
    finer = Mesh(mesh.devices.reshape(4, 4, 2, 2, 2), SEQ_FFN)
    matrices = (P(SEQ, None, FFN),) * 3 + (P(FFN, SEQ),) * 3
    matrices += (P(SEQ, None, FFN),) * 3 + (P(None, FFN, SEQ),) * 3
    norms = (P(),) * 3 + (P(None, None, FFN),) * 3
    return jax.shard_map(
        shards,
        mesh=finer,
        in_specs=(P(None, SEQ, None), P(None, SEQ_FFN, None), P(), *matrices, *norms),
        out_specs=(P(None, SEQ_FFN, None), P(None, SEQ, None), *matrices, *norms, P()),
        check_vma=False,
    )
```

```python
import math

import jax
import jax.numpy as jnp
import numpy as np
from jax import lax
from jax.experimental import pallas as pl
from jax.experimental.pallas import tpu as pltpu
from jax.sharding import Mesh
from jax.sharding import PartitionSpec as P

HDIM = 64
HALF = 32
FF = 8192
STEP = 10
Z, X, YH, YL, C = "seq_0", "seq_1", "seq_2", "ffn_0", "ffn_1"
FFN = (YL, C)
SEQ = (Z, X, YH)
SEQ_FFN = (Z, X, YH, YL, C)
ZX = (Z, X)
YY = (YH, YL)
EIGHT = (YH, YL, C)
TILE = 256

norm_eps = 1e-05
rope_base = 10000.0
xpos_base = 512.0
clip_limit = 1.0
beta_first = 0.9
beta_second = 0.95
adam_eps = 1e-08
decay_rate = 0.1
matrix_rate = 0.04
norm_rate = 0.6

F32 = jnp.float32
BF16 = jnp.bfloat16
SWAP = [(0, 1), (1, 0)]
MIB = 1024 * 1024


def xor_pairs(count, k):
    return [(i, i ^ k) for i in range(count)]


def dot(a, b, da, db):
    return lax.dot_general(a, b, (((da,), (db,)), ((), ())), preferred_element_type=F32)


def shape(dims, kind=F32):
    return jax.ShapeDtypeStruct(dims, kind)


def bytes_of(dims, kind):
    size = math.prod(dims[:-2]) * jnp.dtype(kind).itemsize
    tall = dims[-2] if len(dims) > 1 else 1
    return size * (-(-tall // 8) * 8) * (-(-dims[-1] // 128) * 128)


def in_hbm(out):
    return pltpu.HBM(out.shape, out.dtype)


def local_call(kernel, name, outs, ins, scratch=(), flops=0, moved=0, spare=4, far=(), stay=()):
    need = sum(bytes_of(a.shape, a.dtype) for a in (*ins, *outs))
    need += sum(bytes_of(s.shape, s.dtype) for s in scratch)
    scalar, vector = pltpu.SMEM, pltpu.VMEM
    return pl.pallas_call(
        kernel,
        out_shape=tuple(in_hbm(o) if n in far else o for n, o in enumerate(outs)),
        in_specs=[
            pl.BlockSpec(memory_space=scalar if a.dtype == jnp.int32 else vector) for a in ins
        ],
        out_specs=tuple(pl.BlockSpec(memory_space=vector) for _ in outs),
        scratch_shapes=list(scratch),
        compiler_params=pltpu.CompilerParams(vmem_limit_bytes=need + spare * MIB),
        cost_estimate=pl.CostEstimate(flops=flops, bytes_accessed=moved, transcendentals=0),
        name=name,
    )(*(pltpu.with_memory_space_constraint(a, pltpu.HBM) if n in stay else a for n, a in enumerate(ins)))


def turned(tile):
    return jnp.transpose(tile.astype(F32)).astype(BF16)


def forward_kernel(qkv_ref, start_ref, out_ref, low_ref, top_ref, q_s, k_s, v_s, s_s):
    blocks = q_s.shape[0]
    pieces = TILE // 128
    for i in range(blocks):
        for j in range(pieces):
            part = slice(j * 128, (j + 1) * 128)
            q_s[i, :, part] = qkv_ref[i * pieces + j, 0]
            k_s[i, part, :] = turned(qkv_ref[i * pieces + j, 1])
            v_s[i, :, part] = qkv_ref[i * pieces + j, 2]
    factor = math.log2(math.e) / math.sqrt(HDIM)
    key_line = lax.broadcasted_iota(jnp.int32, (TILE, TILE), 0)
    query_line = lax.broadcasted_iota(jnp.int32, (TILE, TILE), 1)
    for i in range(blocks):
        query = q_s[i]
        begin = start_ref[:, i * TILE : (i + 1) * TILE]
        peak = None
        for b in range(i + 1):
            s = dot(k_s[b], query, 1, 0) * factor
            keep = key_line >= begin - b * TILE
            if b == i:
                keep = keep & (key_line <= query_line)
            s = jnp.where(keep, s, -1e30)
            s_s[b] = s
            high = jnp.max(s, axis=0, keepdims=True)
            peak = high if peak is None else jnp.maximum(peak, high)
        total = jnp.zeros((1, TILE), F32)
        acc = jnp.zeros((HDIM, TILE), F32)
        for b in range(i + 1):
            e = jnp.exp2(s_s[b] - peak)
            total = total + jnp.sum(e, axis=0, keepdims=True)
            acc = acc + dot(v_s[b], e.astype(BF16), 1, 0)
        out = acc / total
        for j in range(pieces):
            out_ref[i * pieces + j] = out[:, j * 128 : (j + 1) * 128]
            low_ref[i * pieces + j] = out[:, j * 128 : (j + 1) * 128].astype(BF16)
        top_ref[:, i * TILE : (i + 1) * TILE] = peak + jnp.log2(total)


def backward_kernel(
    qkv_ref, do_ref, o_ref, top_ref, start_ref, rot_ref, out_ref,
    qt_s, kt_s, dot_s, q_s, k_s, v_s, do_s, dq_s, dk_s, dv_s,
):
    blocks = qt_s.shape[0]
    pieces = TILE // 128
    for i in range(blocks):
        for j in range(pieces):
            part = slice(j * 128, (j + 1) * 128)
            c = i * pieces + j
            qt_s[i, :, part] = qkv_ref[c, 0]
            kt_s[i, :, part] = qkv_ref[c, 1]
            dot_s[i, :, part] = do_ref[c]
            q_s[i, part, :] = turned(qkv_ref[c, 0])
            k_s[i, part, :] = turned(qkv_ref[c, 1])
            v_s[i, part, :] = turned(qkv_ref[c, 2])
            do_s[i, part, :] = turned(do_ref[c])
    scale = 1.0 / math.sqrt(HDIM)
    factor = math.log2(math.e) * scale
    key_line = lax.broadcasted_iota(jnp.int32, (TILE, TILE), 0)
    query_line = lax.broadcasted_iota(jnp.int32, (TILE, TILE), 1)
    for i in range(blocks):
        span = slice(i * TILE, (i + 1) * TILE)
        begin = start_ref[:, span]
        top = top_ref[:, span]
        delta = jnp.concatenate(
            [
                jnp.sum(
                    do_ref[i * pieces + j].astype(F32) * o_ref[i * pieces + j],
                    axis=0,
                    keepdims=True,
                )
                for j in range(pieces)
            ],
            axis=1,
        )
        dq = jnp.zeros((HDIM, TILE), F32)
        for b in range(i + 1):
            s = dot(k_s[b], qt_s[i], 1, 0) * factor
            keep = key_line >= begin - b * TILE
            if b == i:
                keep = keep & (key_line <= query_line)
            p = jnp.where(keep, jnp.exp2(s - top), 0.0)
            dp = dot(v_s[b], dot_s[i], 1, 0)
            ds = (p * (dp - delta)).astype(BF16)
            dq = dq + dot(kt_s[b], ds, 1, 0)
            dk = dot(ds, q_s[i], 1, 0)
            dv = dot(p.astype(BF16), do_s[i], 1, 0)
            if b == i:
                dk_s[b] = dk
                dv_s[b] = dv
            else:
                dk_s[b] += dk
                dv_s[b] += dv
        dq_s[i] = dq
    for i in range(blocks):
        span = slice(i * TILE, (i + 1) * TILE)
        dq = dq_s[i] * scale
        dk = jnp.transpose(dk_s[i]) * scale
        dv = jnp.transpose(dv_s[i])
        results = []
        for n, g in enumerate((dq, dk)):
            co, si = rot_ref[2 * n, :, span], rot_ref[2 * n + 1, :, span]
            front, back = g[:HALF], g[HALF:]
            results.append(
                jnp.concatenate([front * co + back * si, back * co - front * si], axis=0)
            )
        results.append(dv)
        for n, g in enumerate(results):
            for j in range(pieces):
                out_ref[i * pieces + j, n] = g[:, j * 128 : (j + 1) * 128].astype(BF16)


def attend(qkv, start):
    count = qkv.shape[0]
    blocks = count * 128 // TILE
    return pl.pallas_call(
        forward_kernel,
        out_shape=(
            pltpu.HBM((count, HDIM, 128), F32),
            pltpu.HBM((count, HDIM, 128), BF16),
            jax.ShapeDtypeStruct((1, count * 128), F32),
        ),
        scratch_shapes=[
            pltpu.VMEM((blocks, HDIM, TILE), BF16),
            pltpu.VMEM((blocks, TILE, HDIM), BF16),
            pltpu.VMEM((blocks, HDIM, TILE), BF16),
            pltpu.VMEM((blocks, TILE, TILE), F32),
        ],
        compiler_params=pltpu.CompilerParams(vmem_limit_bytes=20 * MIB),
        cost_estimate=pl.CostEstimate(
            flops=2000000000, bytes_accessed=4000000, transcendentals=2400000
        ),
        name="attend",
    )(qkv, start)


def attend_back(qkv, d_out, out, top, start, tables):
    count = qkv.shape[0]
    blocks = count * 128 // TILE
    wide = pltpu.VMEM((blocks, HDIM, TILE), BF16)
    tall = pltpu.VMEM((blocks, TILE, HDIM), BF16)
    return pl.pallas_call(
        backward_kernel,
        out_shape=pltpu.HBM((count, 3, HDIM, 128), BF16),
        scratch_shapes=[
            wide, wide, wide, tall, tall, tall, tall,
            pltpu.VMEM((blocks, HDIM, TILE), F32),
            pltpu.VMEM((blocks, TILE, HDIM), F32),
            pltpu.VMEM((blocks, TILE, HDIM), F32),
        ],
        compiler_params=pltpu.CompilerParams(vmem_limit_bytes=28 * MIB),
        cost_estimate=pl.CostEstimate(
            flops=6000000000, bytes_accessed=6000000, transcendentals=2400000
        ),
        name="attend_back",
    )(qkv, d_out, out, top, start, tables)


def rotation_tables(row_slots):
    index_half = np.arange(HALF, dtype=np.float64)
    places = np.arange(row_slots, dtype=np.float64) - row_slots // 2
    inverse = rope_base ** (-2.0 * index_half / HDIM)
    angles = inverse[:, None] * places[None, :]
    zeta = (2.0 * index_half + 0.4 * HDIM) / (1.4 * HDIM)
    stretch = zeta[:, None] ** (places[None, :] / xpos_base)
    cosine, sine = np.cos(angles), np.sin(angles)
    tables = [cosine * stretch, sine * stretch, cosine / stretch, sine / stretch]
    return np.stack(tables).astype(np.float32)


def moments(values):
    center = jnp.mean(values, axis=-1, keepdims=True)
    spread = jnp.mean(jnp.square(values - center), axis=-1, keepdims=True)
    inverse = lax.rsqrt(spread + norm_eps)
    return (values - center) * inverse, inverse


def norm_back(upstream, gain, normed, inverse):
    scaled = upstream * gain
    return inverse * (
        scaled
        - jnp.mean(scaled, axis=-1, keepdims=True)
        - normed * jnp.mean(scaled * normed, axis=-1, keepdims=True)
    )


def place_parts(parts, target, me):
    share = parts[0].shape[0]
    for k, part in enumerate(parts):
        target[pl.ds(pl.multiple_of((me ^ k) * share, share), share), :] = part[...]


def take_for_scatter(source, target, me):
    share = source.shape[0] // 8
    for side in range(2):
        for j in range(4):
            at = pl.multiple_of((me ^ (2 * j + side)) * share, share)
            target[pl.ds((side * 4 + j) * share, share), :] = source[pl.ds(at, share), :]


def scatter_product(left, right, keep_ref, send_ref, width=None):
    half = left.shape[0] // 2
    width = width or keep_ref.shape[1]
    step = 256

    def body(i, _):
        at = pl.ds(pl.multiple_of(i * step, step), step)
        product = dot(left[...], right[at, : left.shape[1]], 1, 1)
        keep_ref[:, at] = product[:half]
        send_ref[:, at] = product[half:].astype(BF16)
        return 0

    lax.fori_loop(0, width // step, body, 0)


def project_kernel(
    ids, here_ref, near_ref, far_ref, pre_ref, rot_ref, w_ref, qkv_ref, hat_ref, a_ref, x_s, y_s
):
    half, core = ids[1], ids[2]
    rows, slots, width = here_ref.shape
    other = (1 - half) * slots
    for r in range(rows):
        x_s[pl.ds(pl.multiple_of(half * slots, slots), slots), :] = here_ref[r]
        x_s[pl.ds(pl.multiple_of(other + core * 32, 32), 32), :] = near_ref[r]
        x_s[pl.ds(pl.multiple_of(other + (1 - core) * 32, 32), 32), :] = far_ref[r]
        normed, _ = moments(x_s[...].astype(F32))
        low = normed * pre_ref[0:1] + pre_ref[1:2]
        hat_ref[r * 2 * slots : (r + 1) * 2 * slots, :] = normed.astype(BF16)
        a_ref[r * 2 * slots : (r + 1) * 2 * slots, :] = low.astype(BF16)
    span = 2 * slots
    heads = y_s.shape[1] // HDIM
    for n in range(3):
        y_s[...] = dot(a_ref[...], w_ref[:, n * heads * HDIM : (n + 1) * heads * HDIM], 1, 0)
        for r in range(rows):
            for pair in range(heads // 2):
                t = jnp.transpose(
                    y_s[r * span : (r + 1) * span, pair * 128 : (pair + 1) * 128]
                )
                for e in range(2):
                    g = t[e * HDIM : (e + 1) * HDIM]
                    if n < 2:
                        co, si = rot_ref[2 * n], rot_ref[2 * n + 1]
                        front, back = g[:HALF], g[HALF:]
                        g = jnp.concatenate(
                            [front * co - back * si, front * si + back * co], axis=0
                        )
                    qkv_ref[r * heads + pair * 2 + e, n] = g.astype(BF16)


def inner_moments(sums_ref, width, row=0):
    sums = sums_ref[0]
    for k in range(1, 8):
        sums = sums + sums_ref[k]
    center = sums[row : row + 1] / width
    inverse = lax.rsqrt(sums[row + 1 : row + 2] / width - center * center + norm_eps)
    return sums, center, inverse


def high_low(value):
    high = value.astype(BF16).astype(F32)
    return [high, value - high]


def out_kernel(
    ids, o_ref, gain_ref, w_ref, keep_ref, send_ref, line_ref, c_s, sum_s, l_s, k_s
):
    count, _, span = o_ref.shape
    heads = count // 4
    width = w_ref.shape[0]
    half = keep_ref.shape[0]
    for r in range(4):
        o = jnp.concatenate([o_ref[r * heads + h] for h in range(heads)], axis=0).astype(F32)
        first = jnp.sum(o, axis=0, keepdims=True)
        second = jnp.sum(o * o, axis=0, keepdims=True)
        line_ref[0:1, r * span : (r + 1) * span] = first
        line_ref[1:2, r * span : (r + 1) * span] = second
        lines = [first, second, *high_low(first), *high_low(second)]
        lines.append(jnp.zeros((128 - len(lines), span), F32))
        sums = jnp.transpose(jnp.concatenate(lines, axis=0))
        c = jnp.transpose(o * gain_ref[...]).astype(BF16)
        for s in range(8):
            at = slice(s * 64 + r * 16, s * 64 + (r + 1) * 16)
            c_s[at, :] = c[s * 16 : (s + 1) * 16]
            sum_s[at, :] = sums[s * 16 : (s + 1) * 16]
    take_for_scatter(c_s, l_s, ids[0])
    take_for_scatter(sum_s, k_s, ids[0])
    scatter_product(l_s, w_ref, keep_ref, send_ref, width)
    keep_ref[:, width:] = k_s[:half]
    send_ref[:, width:] = k_s[half:].astype(BF16)


def normed_heads_kernel(o_ref, sums_ref, gain_ref, shift_ref, c_ref, *, width):
    count, _, span = o_ref.shape
    heads = count // 4
    _, center, inverse = inner_moments(sums_ref, width, 4)
    for r in range(4):
        at = slice(r * span, (r + 1) * span)
        o = jnp.concatenate([o_ref[r * heads + h] for h in range(heads)], axis=0).astype(F32)
        c = (o - center[:, at]) * inverse[:, at] * gain_ref[...] + shift_ref[...]
        c = jnp.transpose(c).astype(BF16)
        for s in range(8):
            c_ref[s * 64 + r * 16 : s * 64 + (r + 1) * 16, :] = c[s * 16 : (s + 1) * 16]


def gain_product_kernel(gain_ref, shift_ref, w_ref, out_ref):
    rows = [*high_low(gain_ref[...]), *high_low(shift_ref[...])]
    rows = jnp.concatenate(rows + [jnp.zeros((12, rows[0].shape[1]), F32)], axis=0).astype(BF16)
    product = dot(rows, w_ref[...], 1, 1)
    both = [product[0:1] + product[1:2], product[2:3] + product[3:4]]
    out_ref[...] = jnp.concatenate(both + [jnp.zeros((6, product.shape[1]), F32)], axis=0)


def two_sums(stats, other):
    first = stats[:, 0:1] + (other[:, 2:3] + other[:, 3:4])
    second = stats[:, 1:2] + (other[:, 4:5] + other[:, 5:6])
    return first, second


def core_sum_stats_kernel(keep_ref, got_ref, own_ref, one_ref, two_ref, three_ref):
    share = own_ref.shape[0]
    width = own_ref.shape[1] - 128
    both = keep_ref[:, :width] + got_ref[:, :width].astype(F32)
    first, second = two_sums(keep_ref[:, width:], got_ref[:, width:].astype(F32))
    lane = lax.broadcasted_iota(jnp.int32, (keep_ref.shape[0], 128), 1)
    stats = jnp.zeros(lane.shape, F32)
    for n, v in enumerate([first, second, *high_low(first), *high_low(second)]):
        stats = jnp.where(lane == n, v, stats)
    own_ref[:, :width] = both[:share]
    own_ref[:, width:] = stats[:share]
    for j, ref in ((1, one_ref), (2, two_ref), (3, three_ref)):
        ref[:, :width] = both[j * share : (j + 1) * share].astype(BF16)
        ref[:, width:] = stats[j * share : (j + 1) * share].astype(BF16)


def core_sum_kernel(keep_ref, got_ref, own_ref, one_ref, two_ref, three_ref):
    share = own_ref.shape[0]
    both = keep_ref[...] + got_ref[...].astype(F32)
    own_ref[...] = both[:share]
    for j, ref in ((1, one_ref), (2, two_ref), (3, three_ref)):
        ref[...] = both[j * share : (j + 1) * share].astype(BF16)


def summed(own_ref, refs):
    total = own_ref[...]
    for ref in refs:
        total = total + ref[...].astype(F32)
    return total


def middle_kernel(
    own_ref, one, two, three, x_ref, usable_ref, pre_ref, g_ref, g_one, g_two, g_three,
    r1_ref, bb_ref,
):
    width = r1_ref.shape[1]
    total = own_ref[...]
    product, stats = total[:, :width], total[:, width:]
    for ref in (one, two, three):
        product = product + ref[:, :width].astype(F32)
        first, second = two_sums(stats, ref[:, width:].astype(F32))
        lane = lax.broadcasted_iota(jnp.int32, stats.shape, 1)
        stats = jnp.where(lane == 0, first, jnp.where(lane == 1, second, 0.0))
    center = stats[:, 0:1] / width
    inverse = lax.rsqrt(stats[:, 1:2] / width - center * center + norm_eps)
    g = (g_ref[...] + g_one[...]) + (g_two[...] + g_three[...])
    attn = inverse * (product - center * g[0:1]) + g[1:2]
    r1 = x_ref[...].astype(F32) + usable_ref[...] * attn
    normed, _ = moments(r1)
    r1_ref[...] = r1
    bb_ref[...] = (normed * pre_ref[2:3] + pre_ref[3:4]).astype(BF16)


def result_kernel(own_ref, one, two, three, r1_ref, usable_ref, out_ref):
    f = summed(own_ref, (one, two, three))
    out_ref[...] = (r1_ref[...] + usable_ref[...] * f).astype(BF16)


def down_back_kernel(ids, *refs):
    parts, (w_ref, df_ref, dhn_ref) = refs[:8], refs[8:]
    place_parts(parts, df_ref, ids[0])

    def body(i, _):
        at = pl.ds(pl.multiple_of(i * 256, 256), 256)
        dhn_ref[:, at] = dot(df_ref[...], w_ref[:, at], 1, 0)
        return 0

    lax.fori_loop(0, dhn_ref.shape[1] // 256, body, 0)


def up_kernel(ids, *refs):
    parts, refs = refs[:8], refs[8:]
    w_ref, dhn_ref, gain_ref, o_ref, bb_ref, h_ref, slope_ref, sums_ref = refs
    place_parts(parts, bb_ref, ids[0])
    tokens, units = h_ref.shape
    step = 256

    def body(i, carry):
        at = pl.ds(pl.multiple_of(i * step, step), step)
        u = dot(bb_ref[...], w_ref[:, at], 1, 0)
        cdf = 0.5 * (1.0 + lax.erf(u * (1.0 / math.sqrt(2.0))))
        h = u * cdf
        h_ref[:, at] = h
        slope_ref[:, at] = cdf + u * (
            jnp.exp(-0.5 * u * u) * (1.0 / math.sqrt(2.0 * math.pi))
        )
        scaled = dhn_ref[:, at] * gain_ref[:, at]
        terms = (h, h * h, scaled, scaled * h)
        return tuple(c + jnp.sum(t, axis=1, keepdims=True) for c, t in zip(carry, terms))

    zero = jnp.zeros((tokens, 1), F32)
    sums = lax.fori_loop(0, units // step, body, (zero,) * 4)
    lane = lax.broadcasted_iota(jnp.int32, (tokens, 128), 1)
    wide = jnp.zeros((tokens, 128), F32)
    for n, s in enumerate(sums):
        wide = jnp.where(lane == n, s, wide)
    line = jnp.transpose(wide)
    line = jnp.concatenate([line[:4], o_ref[...], line[6:8]], axis=0)
    for k in range(8):
        sums_ref[k] = line


def inner_back_kernel(
    ids, h_ref, slope_ref, dhn_ref, sums_ref, gain_ref, shift_ref, w_ref,
    keep_ref, send_ref, hn_ref, du_ref, sub_ref, l_s,
):
    sums, center, inverse = inner_moments(sums_ref, FF)
    mean_scaled = sums[2:3] / FF
    mean_both = inverse * (sums[3:4] / FF - center * mean_scaled)
    rows = jnp.concatenate([center, inverse, mean_scaled, mean_both, sums[4:8]], axis=0)
    columns = jnp.transpose(jnp.concatenate([rows] * 16, axis=0))
    tokens = h_ref.shape[0]
    center, inverse, mean_scaled, mean_both = (columns[:, n : n + 1] for n in range(4))
    units = h_ref.shape[1]

    def body(i, _):
        at = pl.ds(pl.multiple_of(i * 256, 256), 256)
        hat = (h_ref[:, at] - center) * inverse
        dhn = dhn_ref[:, at]
        gain = gain_ref[:, at]
        hn_ref[:, at] = (hat * gain + shift_ref[:, at]).astype(BF16)
        du = inverse * (dhn * gain - mean_scaled - hat * mean_both) * slope_ref[:, at]
        du_ref[:, at] = du.astype(BF16)
        sub_ref[0:1, at] = jnp.sum(dhn * hat, axis=0, keepdims=True)
        sub_ref[1:2, at] = jnp.sum(dhn, axis=0, keepdims=True)
        return 0

    lax.fori_loop(0, units // 256, body, 0)
    take_for_scatter(du_ref, l_s, ids[0])
    scatter_product(l_s, w_ref, keep_ref, send_ref)


def down_kernel(ids, hn_ref, w_ref, keep_ref, send_ref, l_s):
    take_for_scatter(hn_ref, l_s, ids[0])
    scatter_product(l_s, w_ref, keep_ref, send_ref)


def mlp_grad_kernel(df_ref, hn_ref, bb_ref, du_ref, out_ref):
    units = hn_ref.shape[1]
    out_ref[:, :units] = dot(jnp.transpose(bb_ref[...]), du_ref[...], 1, 0).astype(BF16)
    out_ref[:, units:] = dot(jnp.transpose(df_ref[...]), hn_ref[...], 1, 0).astype(BF16)


def mlp_grad(df, hn, bb, du):
    tokens, width = df.shape
    units = hn.shape[1]
    step = 256
    narrow = pl.BlockSpec((tokens, step), lambda i: (0, i))
    whole = pl.BlockSpec((tokens, units), lambda i: (0, 0))
    return pl.pallas_call(
        mlp_grad_kernel,
        grid=(width // step,),
        out_shape=pltpu.HBM((width, 2 * units), BF16),
        in_specs=[narrow, whole, narrow, whole],
        out_specs=pl.BlockSpec((step, 2 * units), lambda i: (i, 0)),
        compiler_params=pltpu.CompilerParams(vmem_limit_bytes=20 * MIB),
        cost_estimate=pl.CostEstimate(
            flops=4 * tokens * width * units, bytes_accessed=14 * MIB, transcendentals=0
        ),
        name="mlp_grad",
    )(df, hn, bb, du)


def middle_back_kernel(
    own_ref, one, two, three, r1_ref, cot_ref, usable_ref, pre_ref, dr1_ref, dattn_ref, grad_ref
):
    dbb = summed(own_ref, (one, two, three))
    hat, inverse = moments(r1_ref[...])
    dr1 = cot_ref[...].astype(F32) + norm_back(dbb, pre_ref[2:3], hat, inverse)
    dr1_ref[...] = dr1
    dattn_ref[...] = (usable_ref[...] * dr1).astype(BF16)
    grad_ref[0:1] = jnp.sum(dbb * hat, axis=0, keepdims=True)
    grad_ref[1:2] = jnp.sum(dbb, axis=0, keepdims=True)


def out_back_kernel(ids, *refs):
    parts, refs = refs[:8], refs[8:]
    w_ref, o_ref, sums_ref, gain_ref, dattn_ref, dc_ref, out_ref, sub_ref, y_s = refs
    place_parts(parts, dattn_ref, ids[0])
    y_s[...] = dot(dattn_ref[...], w_ref[...], 1, 0)
    count, _, span = o_ref.shape
    heads = count // 4
    _, center, inverse = inner_moments(sums_ref, dattn_ref.shape[1], 4)
    gain_grad, shift_grad, lines = 0.0, 0.0, []
    for r in range(4):
        at = slice(r * span, (r + 1) * span)
        dc = jnp.concatenate(
            [y_s[s * 64 + r * 16 : s * 64 + (r + 1) * 16, :] for s in range(8)], axis=0
        )
        dc = jnp.transpose(dc)
        dc_ref[:, at] = dc
        o = jnp.concatenate([o_ref[r * heads + h] for h in range(heads)], axis=0).astype(F32)
        hat = (o - center[:, at]) * inverse[:, at]
        gain_grad = gain_grad + jnp.sum(dc * hat, axis=1, keepdims=True)
        shift_grad = shift_grad + jnp.sum(dc, axis=1, keepdims=True)
        scaled = dc * gain_ref[...]
        lines.append(
            jnp.concatenate(
                [
                    jnp.sum(scaled, axis=0, keepdims=True),
                    jnp.sum(scaled * hat, axis=0, keepdims=True),
                    jnp.zeros((6, span), F32),
                ],
                axis=0,
            )
        )
    line = jnp.concatenate(lines, axis=1)
    for k in range(8):
        out_ref[k] = line
    sub_ref[...] = jnp.concatenate(
        [
            jnp.transpose(jnp.broadcast_to(g, (g.shape[0], 128)))[0:1]
            for g in (gain_grad, shift_grad)
        ],
        axis=0,
    )


def head_grad_kernel(dc_ref, o_ref, sums_ref, back_ref, gain_ref, out_ref, *, width):
    count, _, span = o_ref.shape
    heads = count // 4
    _, center, inverse = inner_moments(sums_ref, width, 4)
    back = back_ref[0]
    for k in range(1, 8):
        back = back + back_ref[k]
    for r in range(4):
        at = slice(r * span, (r + 1) * span)
        first, second = back[0:1, at] / width, back[1:2, at] / width
        for h in range(heads):
            part = slice(h * HDIM, (h + 1) * HDIM)
            hat = (o_ref[r * heads + h].astype(F32) - center[:, at]) * inverse[:, at]
            scaled = dc_ref[part, at] * gain_ref[part]
            out_ref[r * heads + h] = (
                inverse[:, at] * (scaled - first - hat * second)
            ).astype(BF16)


def out_grad_kernel(dattn_ref, c_ref, out_ref):
    out_ref[...] = dot(jnp.transpose(dattn_ref[...]), c_ref[...], 1, 0).astype(BF16)


def out_grad(dattn, c):
    tokens, width = dattn.shape
    units = c.shape[1]
    step = 512
    return pl.pallas_call(
        out_grad_kernel,
        grid=(width // step,),
        out_shape=pltpu.HBM((width, units), BF16),
        in_specs=[
            pl.BlockSpec((tokens, step), lambda i: (0, i)),
            pl.BlockSpec((tokens, units), lambda i: (0, 0)),
        ],
        out_specs=pl.BlockSpec((step, units), lambda i: (i, 0)),
        compiler_params=pltpu.CompilerParams(vmem_limit_bytes=16 * MIB),
        cost_estimate=pl.CostEstimate(
            flops=2 * tokens * width * units, bytes_accessed=4 * MIB, transcendentals=0
        ),
        name="out_grad",
    )(dattn, c)


def ring_block(group, i, j):
    return (((group >> 2) + i) & 3) * 4 + ((group + j) & 3)


def turn_kernel(ids, a_ref, out_ref):
    for r in range(16):
        at = pl.ds(pl.multiple_of(ring_block(ids[3], r // 4, r % 4) * 128, 128), 128)
        to = (r % 4) * 4 + r // 4
        out_ref[to * 128 : (to + 1) * 128, :] = jnp.transpose(a_ref[:, at])


def column(row):
    return jnp.transpose(jnp.broadcast_to(row, (128, row.shape[1])))[:, 0:1]


def row_of(col):
    return jnp.transpose(jnp.broadcast_to(col, (col.shape[0], 128)))[0:1]


def in_grad_kernel(
    ids, dqkv_ref, xt_ref, w_ref, pre_ref, out_ref, three_ref, o_ref, h_ref, *refs
):
    lines, (tokens_ref, d_s, one_s) = refs[:10], refs[10:]

    def put(side, place, other, columns, value):
        refs = lines[5 * side : 5 * side + 5]
        if place == 2:
            ref, row = refs[2 + other // 2], (other % 2) * 64
        else:
            ref, row = refs[(0, 1, None, 4)[place]], other * 64
        ref[row : row + 64, columns] = value

    count = dqkv_ref.shape[0]
    heads = count // 4
    units = d_s.shape[0]
    for r in range(4):
        for n in range(3):
            for h in range(heads):
                base = (n * heads + h) * HDIM
                d_s[base : base + HDIM, r * 128 : (r + 1) * 128] = dqkv_ref[r * heads + h, n]
    sums = []
    for n in range(0, units, 128):
        total = jnp.zeros((1, 128), F32)
        for r in range(4):
            t = jnp.transpose(d_s[n : n + 128, r * 128 : (r + 1) * 128].astype(F32))
            total = total + jnp.sum(t, axis=0, keepdims=True)
            t = t.astype(BF16)
            for s in range(8):
                tokens_ref[s * 64 + r * 16 : s * 64 + (r + 1) * 16, n : n + 128] = t[
                    s * 16 : (s + 1) * 16
                ]
        sums.append(total)
    sums = jnp.concatenate(sums, axis=1)
    for j in range(4):
        products = dot(xt_ref[j * 512 : (j + 1) * 512, :], d_s[...], 1, 1)
        for i in range(4):
            at = pl.ds(pl.multiple_of(ring_block(ids[3], i, j) * 128, 128), 128)
            product = products[i * 128 : (i + 1) * 128]
            gradient = product * column(pre_ref[0:1, at]) + column(pre_ref[1:2, at]) * sums
            gradient = gradient.astype(BF16)
            outward = out_ref[at, :]
            for columns, value in ((slice(units), gradient), (slice(units, None), outward)):
                put(0, j, i, columns, value[:64])
                put(1, i, j, columns, value[64:])
            w = w_ref[at, :units].astype(F32)
            one_s[0:1, at] = row_of(jnp.sum(w * product, axis=1, keepdims=True))
            one_s[1:2, at] = row_of(jnp.sum(w * sums, axis=1, keepdims=True))
    width = lines[0].shape[1]
    half = o_ref.shape[1]
    small = []
    for ref in (one_s, three_ref):
        for n in range(2):
            small += [ref[n : n + 1, :width], ref[n : n + 1, width:]]
    for n in range(2):
        first = [o_ref[n : n + 1], h_ref[n : n + 1, : width - half]]
        last = [h_ref[n : n + 1, width - half :], jnp.zeros((1, width - half), F32)]
        small += [jnp.concatenate(first, axis=1), jnp.concatenate(last, axis=1)]
    small.append(jnp.zeros((16 - len(small), width), F32))
    small = jnp.concatenate(small, axis=0).astype(BF16)
    for ref in (lines[0], lines[1], lines[2], lines[4]):
        ref[ref.shape[0] - 16 :, :] = small


def in_back_kernel(ids, d_ref, w_ref, keep_ref, send_ref, l_s):
    take_for_scatter(d_ref, l_s, ids[0])
    scatter_product(l_s, w_ref, keep_ref, send_ref)


def summed_low(refs):
    total = refs[0][...].astype(F32)
    for ref in refs[1:]:
        total = total + ref[...].astype(F32)
    return total


def ring_sum_kernel(*refs):
    ins, outs = refs[:8], refs[8:]
    for side in range(2):
        on, back, got_on, got_back = ins[4 * side : 4 * side + 4]
        out_on, out_back = outs[2 * side : 2 * side + 2]
        rows = got_back.shape[0]
        out_on[:rows, :] = (on[:rows].astype(F32) + got_on[:rows].astype(F32)).astype(BF16)
        out_on[rows : 2 * rows, :] = on[rows : 2 * rows]
        out_back[:rows, :] = back[:rows]
        both = back[rows : 2 * rows].astype(F32) + got_back[...].astype(F32)
        out_back[rows : 2 * rows, :] = both.astype(BF16)
        if got_on.shape[0] > rows:
            small = on[2 * rows :].astype(F32) + got_on[rows:].astype(F32)
            out_on[2 * rows :, :] = small.astype(BF16)
            out_back[2 * rows :, :] = back[2 * rows :]


def line_sum_kernel(*refs):
    first, second, outs = refs[:3], refs[3:6], refs[6:]
    total = summed_low(first)
    small = total[256:272]
    outs[0][0:64, :] = total[0:64]
    outs[0][64:80, :] = small
    for k in (1, 2, 3):
        outs[k][0:64, :] = total[k * 64 : (k + 1) * 64].astype(BF16)
        outs[k][64:80, :] = small.astype(BF16)
    total = summed_low(second)
    outs[4][...] = total[0:64]
    for k in (1, 2, 3):
        outs[4 + k][...] = total[k * 64 : (k + 1) * 64].astype(BF16)


def last_sum_kernel(ids, *refs):
    ins, (mlp_ref, keep_ref, give_ref, out_ref) = refs[:8], refs[8:]
    width = keep_ref.shape[1]
    low = ids[1] == 0
    second = summed_low(ins[4:])
    slots = second.shape[0]
    total = summed_low(ins[:4])
    first, small = total[:slots], total[slots:]
    keep_ref[:slots, :] = jnp.where(low, first, second).astype(BF16)
    give_ref[:slots, :] = jnp.where(low, second, first).astype(BF16)
    keep_ref[slots:, :] = small.astype(BF16)
    give_ref[slots:, :] = small.astype(BF16)
    squares = whole_sum(first * first + second * second) + mlp_ref[0:1, 0:1]

    def joined(begin):
        return jnp.concatenate([small[begin : begin + 1], small[begin + 1 : begin + 2]], axis=1)

    sub = jnp.concatenate([joined(8), joined(10)], axis=0)
    lane = lax.broadcasted_iota(jnp.int32, (4, 2 * width), 1)
    scalars = jnp.zeros(lane.shape, F32)
    for n, term in enumerate([*high_low(squares), *high_low(whole_sum(sub * sub))]):
        scalars = jnp.where(lane // 128 == n, term, scalars)
    lines = jnp.concatenate([joined(2 * n) for n in range(4)] + [scalars], axis=0).astype(BF16)
    for k in range(out_ref.shape[0]):
        out_ref[k] = lines


def group_total_kernel(small_ref, total_ref, out_ref):
    total = small_ref[0].astype(F32)
    for k in range(1, small_ref.shape[0]):
        total = total + small_ref[k].astype(F32)
    total_ref[...] = total
    squares = total[4:5, 0:128] + total[4:5, 128:256]
    for k in range(out_ref.shape[0]):
        out_ref[k] = jnp.broadcast_to(squares, out_ref.shape[1:])


def input_back_kernel(own_ref, one, two, three, x_ref, dr1_ref, pre_ref, out_ref):
    da = summed(own_ref, (one, two, three))
    hat, inverse = moments(x_ref[...].astype(F32))
    out_ref[...] = (dr1_ref[...] + norm_back(da, pre_ref[0:1], hat, inverse)).astype(BF16)


def whole_sum(values):
    return jnp.sum(jnp.sum(values, axis=1, keepdims=True), axis=0, keepdims=True)


def rest_kernel(ids, g_ref, keep_ref, give_ref, sum_ref):
    slots = keep_ref.shape[0]
    half = ids[1]
    keep_ref[...] = g_ref[pl.ds(pl.multiple_of(half * slots, slots), slots), :]
    give_ref[...] = g_ref[pl.ds(pl.multiple_of((1 - half) * slots, slots), slots), :]
    total = jnp.zeros((1, 1), F32)
    for k in range(g_ref.shape[0] // 32):
        g = g_ref[k * 32 : (k + 1) * 32, :].astype(F32)
        total = total + whole_sum(g * g)
    sum_ref[...] = jnp.broadcast_to(total, sum_ref.shape)


def adam_step(weight, moment, squares, gradient, factor, step_rate, decay_weight):
    clipped = gradient * factor
    moment_new = beta_first * moment + (1.0 - beta_first) * clipped
    squares_new = beta_second * squares + (1.0 - beta_second) * clipped * clipped
    moment_hat = moment_new * (1.0 / (1.0 - beta_first**STEP))
    squares_hat = squares_new * (1.0 / (1.0 - beta_second**STEP))
    updated = weight - step_rate * (
        moment_hat / (jnp.sqrt(squares_hat) + adam_eps) + decay_weight * weight
    )
    return updated, moment_new, squares_new


def adam_kernel(
    ids, small_ref, norm_part, sub_own, sub_take, att_keep, att_take, mlp_keep, mlp_take, *refs
):
    states, outs, norm_out = refs[:18], refs[18:36], refs[36]
    low = ids[1] == 0
    squares = norm_part[0, 0:1, 0:1]
    for k in range(1, norm_part.shape[0]):
        squares = squares + norm_part[k, 0:1, 0:1]
    pre = small_ref[0:4]
    squares = squares + small_ref[4:5, 256:257] + small_ref[4:5, 384:385] + whole_sum(pre * pre)
    norm = jnp.sqrt(squares)
    factor = jnp.minimum(1.0, clip_limit / (norm + 1e-06))
    half = att_keep.shape[1] // 4

    def pair(mine, theirs, at):
        mine = mine[:, at * half : (at + 1) * half].astype(F32)
        theirs = theirs[:, at * half : (at + 1) * half].astype(F32)
        return jnp.concatenate(
            [jnp.where(low, mine, theirs), jnp.where(low, theirs, mine)], axis=1
        )

    def step(which, index, gradient, rate, decay):
        state = [states[3 * which + n][index] for n in range(3)]
        for n, value in enumerate(adam_step(*state, gradient, factor, rate, decay)):
            outs[3 * which + n][index] = value

    everything = slice(None)
    for k in range(3):
        step(0, (k,), pair(att_keep, att_take, k), matrix_rate, decay_rate)
    step(1, (everything,), pair(att_keep, att_take, 3), matrix_rate, decay_rate)
    for b in range(4):
        step(2, (everything, b), pair(mlp_keep, mlp_take, b), matrix_rate, decay_rate)
        step(3, (b,), pair(mlp_keep, mlp_take, 4 + b), matrix_rate, decay_rate)

    @pl.when(pl.program_id(0) == 0)
    def _():
        step(4, (everything,), pre, norm_rate, 0.0)
        for b in range(5):
            row, at = (0, b) if b < 4 else (1, 0)
            both = pair(sub_own, sub_take, at)
            both = jnp.concatenate([both[8 + row : 9 + row], both[10 + row : 11 + row]], axis=0)
            step(5, (b,), both, norm_rate, 0.0)
        norm_out[...] = jnp.broadcast_to(norm, norm_out.shape)


def adam(ids, small, norm_part, gradients, states):
    flat = [a for state in states for a in state]
    step = 32

    def whole(a):
        return pl.BlockSpec(a.shape, lambda i, nd=a.ndim: (0,) * nd)

    def blocks(which, a):
        if which > 3:
            return whole(a)
        dim = (1, 0, 0, 1)[which]
        block = tuple(step if n == dim else d for n, d in enumerate(a.shape))
        return pl.BlockSpec(
            block, lambda i, nd=a.ndim, dim=dim: tuple(i if n == dim else 0 for n in range(nd))
        )

    specs = [blocks(n // 3, a) for n, a in enumerate(flat)]
    rows = [pl.BlockSpec((step, g.shape[1]), lambda i: (i, 0)) for g in gradients]
    a_rows = gradients[2].shape[0] // 16
    norm = shape((1, 1))
    return pl.pallas_call(
        adam_kernel,
        grid=(gradients[2].shape[0] // step,),
        out_shape=tuple(shape(a.shape) for a in flat) + (norm,),
        in_specs=[
            pl.BlockSpec(memory_space=pltpu.SMEM),
            whole(small),
            whole(norm_part),
            *(pl.BlockSpec((16, a.shape[1]), lambda i: (a_rows, 0)) for a in gradients[:2]),
            *rows,
            *specs,
        ],
        out_specs=tuple(specs) + (whole(norm),),
        compiler_params=pltpu.CompilerParams(vmem_limit_bytes=56 * MIB),
        cost_estimate=pl.CostEstimate(flops=0, bytes_accessed=12 * MIB, transcendentals=0),
        name="adam",
    )(ids, small, norm_part, *gradients[:2], *gradients, *flat)


def eight_parts(own, *meanwhile):
    lines = [lax.ppermute(own, YY, xor_pairs(4, k)) for k in (1, 2, 3)]
    if meanwhile:
        lines = [after(line, *meanwhile) for line in lines]
    lines = [own] + lines
    parts = []
    for line in lines:
        parts += [line, lax.ppermute(line, C, SWAP)]
    return parts


def core_scatter(keep, send, kernel=core_sum_kernel):
    share, width = keep.shape[0] // 4, keep.shape[1]
    got = lax.ppermute(send, C, SWAP)
    return local_call(
        kernel,
        "core_sum",
        [shape((share, width))] + [shape((share, width), BF16)] * 3,
        [keep, got],
        moved=5 * MIB,
    )


def line_scatter(own, *sent):
    return [own] + [lax.ppermute(s, YY, xor_pairs(4, k)) for k, s in zip((1, 2, 3), sent)]


def finish_scatter(keep, send, work=None, kernel=core_sum_kernel):
    own, *sent = core_scatter(keep, send, kernel)
    lines = line_scatter(own, *sent)
    if work is None:
        return lines
    done = work(own)
    return lines[:1] + [after(line, *done) for line in lines[1:]], done


def ring_pairs(k):
    return [(i, (i + k) % 4) for i in range(4)]


def crossing(lines, first_axis, second_axis):
    first, second = list(lines[:4]), list(lines[4:])
    for k in (2, 1, 3):
        first[k] = lax.ppermute(first[k], first_axis, ring_pairs(k))
        second[k] = lax.ppermute(second[k], second_axis, ring_pairs(k))
    return first, second


def ring_crossing(lines):
    sides = [(lines[:5], X), (lines[5:], Z)]
    ins = []
    for (_, on, two_on, two_back, back), axis in sides:
        ins += [on, back]
        ins += [lax.ppermute(two_on, axis, ring_pairs(1)), lax.ppermute(two_back, axis, ring_pairs(3))]
    outs = [shape(ins[n].shape, BF16) for n in (0, 1, 4, 5)]
    sums = local_call(ring_sum_kernel, "ring_sum", outs, ins, moved=5 * MIB)
    return [
        [side[0], lax.ppermute(on, axis, ring_pairs(1)), lax.ppermute(back, axis, ring_pairs(3))]
        for (side, axis), on, back in zip(sides, sums[::2], sums[1::2])
    ]


def each_to_all(copies, axis):
    return lax.all_to_all(copies, axis, split_axis=0, concat_axis=0, tiled=True)


def after(value, *others):
    return lax.optimization_barrier((value, *others))[0]


def shards(
    hidden_in, cotangent, doc_lengths,
    inward, inward_moment, inward_squares,
    outward, outward_moment, outward_squares,
    upward, upward_moment, upward_squares,
    downward, downward_moment, downward_squares,
    prenorm, prenorm_moment, prenorm_squares,
    subnorm, subnorm_moment, subnorm_squares,
):
    rows, seq_slots, width = hidden_in.shape
    quarter = cotangent.shape[1]
    group_slots = 2 * seq_slots
    row_slots = group_slots * lax.axis_size(ZX)
    half = inward.shape[2] // 2
    heads = half // HDIM
    units = 4 * half
    tokens = rows * group_slots
    share = rows * quarter
    zx = lax.axis_index(ZX)
    row_index = lax.axis_index(Z)
    yh = lax.axis_index(YH)
    core = lax.axis_index(C)
    ffn = lax.axis_index(FFN)
    me = lax.axis_index(EIGHT)
    low_side = yh == 0
    first_core = core == 0
    ids = jnp.stack([me, yh, core, zx]).astype(jnp.int32)

    def mine_theirs(array, axis):
        low = array.astype(BF16)
        mine = lax.dynamic_slice_in_dim(low, yh * half, half, axis)
        theirs = lax.dynamic_slice_in_dim(low, (1 - yh) * half, half, axis)
        return mine, theirs

    def in_order(own, other):
        return jnp.concatenate(
            [jnp.where(low_side, own, other), jnp.where(low_side, other, own)], axis=0
        )

    def both_halves(pairs):
        other = lax.ppermute(jnp.concatenate([t for _, t in pairs], axis=1), YH, SWAP)
        own = jnp.concatenate([m for m, _ in pairs], axis=1)
        return in_order(own, other)

    def rows_of(pair, order):
        return tuple(jnp.transpose(t, order).reshape(seq_slots, -1) for t in pair)

    in_pair = rows_of(mine_theirs(inward, 2), (0, 1, 2))
    out_pair = rows_of(mine_theirs(outward, 0), (1, 0))
    up_pair = rows_of(mine_theirs(upward, 2), (0, 1, 2))
    down_pair = rows_of(mine_theirs(downward, 1), (2, 0, 1))
    w_att = both_halves([in_pair, out_pair])
    w_att = lax.all_gather(w_att, ZX, axis=0, tiled=True)
    w_out = w_att[:, 3 * half :]
    w_mlp = both_halves([up_pair, down_pair])
    w_mlp = lax.all_gather(w_mlp, ZX, axis=0, tiled=True)
    w_up, w_down = w_mlp[:, :units], w_mlp[:, units:]

    doc_ends = jnp.cumsum(doc_lengths, axis=1)
    places = jnp.arange(row_slots, dtype=jnp.int32)
    my_ends = lax.dynamic_slice_in_dim(doc_ends, row_index, 1, 0)
    start = jnp.max(
        jnp.where(places[None, :] >= my_ends.reshape(-1, 1), my_ends.reshape(-1, 1), 0),
        axis=0,
        keepdims=True,
    )
    own_places = zx * group_slots + me * quarter + jnp.arange(quarter, dtype=jnp.int32)
    own_usable = (own_places[None, :] < doc_ends[:, -1:]).astype(F32).reshape(share, 1)

    half_slots = seq_slots // 2
    sent = lax.dynamic_slice_in_dim(hidden_in, core * half_slots, half_slots, 1)
    got_near = lax.ppermute(sent, YY, [(i, 3 - i) for i in range(4)])
    got_far = lax.ppermute(got_near, C, SWAP)
    own_hidden = lax.dynamic_slice_in_dim(hidden_in, ffn * quarter, quarter, 1)
    own_hidden = own_hidden.reshape(share, width)
    own_cot = cotangent.reshape(share, width)
    df_own = (own_usable * own_cot.astype(F32)).astype(BF16)
    df_parts = eight_parts(after(df_own, got_near))

    tables = jnp.asarray(rotation_tables(row_slots))
    near = lax.dynamic_slice_in_dim(tables, zx * group_slots, group_slots, 2)
    qkv, x_hat = local_call(
        project_kernel,
        "project",
        [
            shape((rows * heads, 3, HDIM, group_slots), BF16),
            shape((tokens, width), BF16),
        ],
        [ids, hidden_in, got_near, got_far, after(prenorm, *df_parts), near, w_att],
        [
            pltpu.VMEM((tokens, width), BF16),
            pltpu.VMEM((group_slots, width), BF16),
            pltpu.VMEM((tokens, half), F32),
        ],
        flops=2 * tokens * width * 3 * half,
        moved=8 * MIB,
        far=(0, 1),
    )
    sub = lax.dynamic_slice_in_dim(subnorm, yh * half, half, 2)
    gain_o, shift_o = sub[0, 0].reshape(half, 1), sub[1, 0].reshape(half, 1)
    gain_h, shift_h = sub[0, 1:].reshape(1, units), sub[1, 1:].reshape(1, units)
    (gains,) = local_call(
        gain_product_kernel,
        "gain_product",
        [shape((8, width))],
        [sub[0, 0].reshape(1, half), sub[1, 0].reshape(1, half), after(w_out, x_hat)],
    )
    gains = gains + lax.ppermute(gains, C, SWAP)
    gains = [gains] + [lax.ppermute(gains, YY, xor_pairs(4, k)) for k in (2, 1, 3)]
    qkv = after(each_to_all(qkv, ZX), *gains)
    o_head, o_low, top = attend(qkv, start)
    o = each_to_all(o_low, ZX)
    (x_turned,) = local_call(
        turn_kernel, "turn", [shape((width, tokens), BF16)], [ids, x_hat], moved=4 * MIB, far=(0,)
    )

    stat = shape((8, 8, tokens))
    pieces = [shape((tokens // 2, width)), shape((tokens // 2, width), BF16)]
    wide = [shape((tokens // 2, width + 128)), shape((tokens // 2, width + 128), BF16)]
    keep, send, sums_o = local_call(
        out_kernel,
        "out",
        wide + [shape((2, tokens))],
        [ids, o, gain_o, w_out],
        [
            pltpu.VMEM((tokens, half), BF16),
            pltpu.VMEM((tokens, 128), F32),
            pltpu.VMEM((tokens, half), BF16),
            pltpu.VMEM((tokens, 128), F32),
        ],
        flops=2 * tokens * width * half,
        moved=4 * MIB,
    )
    scattered = finish_scatter(keep, send, kernel=core_sum_stats_kernel)
    r1, bb_own = local_call(
        middle_kernel,
        "middle",
        [shape((share, width)), shape((share, width), BF16)],
        scattered + [own_hidden, own_usable, prenorm] + gains,
        moved=3 * MIB,
        far=(0,),
    )

    df, dhn = local_call(
        down_back_kernel,
        "down_back",
        [shape((tokens, width), BF16), shape((tokens, units))],
        [ids] + df_parts + [after(w_down, bb_own)],
        flops=2 * tokens * width * units,
        moved=10 * MIB,
        stay=range(1, 9),
        far=(0,),
    )
    bb_parts = eight_parts(bb_own, dhn)
    bb, h, slope, sums_h = local_call(
        up_kernel,
        "up",
        [shape((tokens, width), BF16), shape((tokens, units)), shape((tokens, units)), stat],
        [ids] + bb_parts + [w_up, dhn, gain_h, sums_o],
        flops=2 * tokens * width * units,
        moved=14 * MIB,
        stay=range(1, 9),
        far=(0,),
    )
    sums_h = each_to_all(sums_h, EIGHT)
    keep, send, hn, du, sub_h = local_call(
        inner_back_kernel,
        "inner_back",
        pieces + [shape((tokens, units), BF16)] * 2 + [shape((2, units))],
        [ids, h, slope, dhn, sums_h, gain_h, shift_h, w_up],
        [pltpu.VMEM((tokens, units), BF16)],
        flops=2 * tokens * width * units,
        moved=14 * MIB,
        far=(2, 3),
    )
    scattered, (g_mlp,) = finish_scatter(
        keep, send, lambda own: [mlp_grad(df, hn, bb, after(du, own))]
    )
    g_mlp = lax.psum_scatter(after(g_mlp, *scattered), ZX, scatter_dimension=0, tiled=True)
    dr1, dattn_own, pre_three = local_call(
        middle_back_kernel,
        "middle_back",
        [shape((share, width)), shape((share, width), BF16), shape((2, width))],
        scattered + [r1, own_cot, own_usable, prenorm],
        moved=4 * MIB,
        far=(0,),
    )
    keep, send = local_call(
        down_kernel,
        "down",
        pieces,
        [ids, hn, w_down],
        [pltpu.VMEM((tokens, units), BF16)],
        flops=2 * tokens * width * units,
        moved=8 * MIB,
    )
    dattn_parts = eight_parts(dattn_own, keep)

    (c,) = local_call(
        lambda *refs: normed_heads_kernel(*refs, width=width),
        "normed_heads",
        [shape((tokens, half), BF16)],
        [o, sums_h, gain_o, shift_o],
        far=(0,),
    )
    dattn, dc, back_o, sub_o = local_call(
        out_back_kernel,
        "out_back",
        [shape((tokens, width), BF16), shape((half, tokens)), stat, shape((2, half))],
        [ids] + dattn_parts + [w_out, o, sums_h, gain_o],
        [pltpu.VMEM((tokens, half), F32)],
        flops=2 * tokens * width * half,
        moved=6 * MIB,
        stay=range(1, 9),
        far=(0,),
    )
    g_out = out_grad(dattn, c)
    back_o = after(each_to_all(back_o, EIGHT), g_out)
    (do,) = local_call(
        lambda *refs: head_grad_kernel(*refs, width=width),
        "head_grad",
        [shape((rows * heads, HDIM, group_slots), BF16)],
        [dc, o, sums_h, back_o, gain_o],
        moved=MIB,
    )
    f_parts = core_scatter(keep, after(send, *dattn_parts))
    do = after(each_to_all(do, ZX), x_turned, f_parts[0])
    scattered = line_scatter(*f_parts)
    dqkv = attend_back(qkv, do, o_head, top, start, tables)
    dqkv = each_to_all(after(dqkv, *scattered), ZX)

    both = 4 * half
    line = [shape((count, both), BF16) for count in (272, 272, 144, 128, 272)]
    line += [shape((count, both), BF16) for count in (256, 256, 128, 128, 256)]
    *lines, dproj = local_call(
        in_grad_kernel,
        "in_grad",
        line + [shape((tokens, 3 * half), BF16)],
        [ids, dqkv, x_turned, w_att, prenorm, g_out, pre_three, sub_o, sub_h],
        [pltpu.VMEM((3 * half, tokens), BF16), pltpu.VMEM((2, width), F32)],
        flops=2 * tokens * width * 3 * half,
        moved=13 * MIB,
        far=range(10),
    )
    first, second = ring_crossing(lines)
    mlp_keep, mlp_give, squares_mlp = local_call(
        rest_kernel,
        "rest",
        [shape((seq_slots, 2 * units), BF16)] * 2 + [shape((8, 128))],
        [ids, after(g_mlp, dproj)],
        stay=(1,),
        far=(0,),
    )
    mlp_take = lax.ppermute(mlp_give, YH, SWAP)
    keep, send = local_call(
        in_back_kernel,
        "in_back",
        pieces,
        [ids, dproj, w_att],
        [pltpu.VMEM((tokens, 3 * half), BF16)],
        flops=2 * tokens * width * 3 * half,
        moved=7 * MIB,
    )
    da_parts = finish_scatter(keep, after(send, *first[1:], *second[1:], squares_mlp))
    piece = [shape((seq_slots + 16, both))] + [shape((seq_slots + 16, both), BF16)] * 3
    piece += [shape((seq_slots, both))] + [shape((seq_slots, both), BF16)] * 3
    lines = [*local_call(
        line_sum_kernel,
        "line_sum",
        piece,
        first + second,
        moved=6 * MIB,
    )]
    first, second = crossing(lines, Z, X)
    da_parts = da_parts[:1] + [after(part, *first[1:], *second[1:]) for part in da_parts[1:]]
    (own_grad,) = local_call(
        input_back_kernel,
        "input_back",
        [shape((share, width), BF16)],
        da_parts[:1] + [after(part, mlp_take) for part in da_parts[1:]] + [own_hidden, dr1, prenorm],
        moved=3 * MIB,
    )
    own_grad = own_grad.reshape(rows, quarter, width)
    line_grad = lax.ppermute(own_grad, YL, SWAP)
    grads = [own_grad, lax.ppermute(own_grad, C, SWAP), line_grad, lax.ppermute(line_grad, C, SWAP)]
    first_line = lax.axis_index(YL) == 0
    pairs = [
        jnp.concatenate([jnp.where(first_core, a, b), jnp.where(first_core, b, a)], axis=1)
        for a, b in (grads[:2], grads[2:])
    ]
    input_grad = jnp.concatenate(
        [jnp.where(first_line, *pairs), jnp.where(first_line, *pairs[::-1])], axis=1
    )

    grad_piece = shape((seq_slots + 16, 4 * half), BF16)
    att_keep, att_give, small = local_call(
        last_sum_kernel,
        "last_sum",
        [grad_piece, grad_piece, shape((8, 8, width), BF16)],
        [ids, *first, *second, squares_mlp],
        moved=MIB,
        far=(0,),
    )
    att_take = lax.ppermute(att_give, YH, SWAP)
    mlp_take = lax.ppermute(mlp_give, YH, SWAP)
    small = each_to_all(small, EIGHT)
    small_total, squares = local_call(
        group_total_kernel,
        "group_total",
        [shape((8, width)), shape((16, 8, 128))],
        [small],
        far=(0,),
    )
    squares = each_to_all(squares, ZX)
    hidden_out = local_call(
        result_kernel,
        "result",
        [shape((share, width), BF16)],
        scattered + [after(r1, small_total), own_usable],
        moved=3 * MIB,
        stay=range(5),
    )[0].reshape(rows, quarter, width)
    turns = ((1, 0, 2), (1, 0), (0, 1, 2), (0, 2, 1), (0, 1), (1, 0, 2))
    states = [
        (inward, inward_moment, inward_squares),
        (outward, outward_moment, outward_squares),
        (upward, upward_moment, upward_squares),
        (downward, downward_moment, downward_squares),
        (prenorm, prenorm_moment, prenorm_squares),
        (subnorm, subnorm_moment, subnorm_squares),
    ]
    *updated, norm = adam(
        ids,
        small_total,
        squares,
        [att_keep, att_take, mlp_keep, mlp_take],
        [tuple(jnp.transpose(a, turn) for a in state) for state, turn in zip(states, turns)],
    )
    updated = [jnp.transpose(a, turns[n // 3]) for n, a in enumerate(updated)]
    return (hidden_out, input_grad, *updated, norm.reshape(()))


def solution(mesh):
    finer = Mesh(mesh.devices.reshape(4, 4, 2, 2, 2), SEQ_FFN)
    matrices = (P(SEQ, None, FFN),) * 3 + (P(FFN, SEQ),) * 3
    matrices += (P(SEQ, None, FFN),) * 3 + (P(None, FFN, SEQ),) * 3
    norms = (P(),) * 3 + (P(None, None, FFN),) * 3
    return jax.shard_map(
        shards,
        mesh=finer,
        in_specs=(P(None, SEQ, None), P(None, SEQ_FFN, None), P(), *matrices, *norms),
        out_specs=(P(None, SEQ_FFN, None), P(None, SEQ, None), *matrices, *norms, P()),
        check_vma=False,
    )
```

```python
import math

import jax
import jax.numpy as jnp
import numpy as np
from jax import lax
from jax.experimental import pallas as pl
from jax.experimental.pallas import tpu as pltpu
from jax.sharding import Mesh
from jax.sharding import PartitionSpec as P

HDIM = 64
HALF = 32
FF = 8192
STEP = 10
Z, X, YH, YL, C = "seq_0", "seq_1", "seq_2", "ffn_0", "ffn_1"
FFN = (YL, C)
SEQ = (Z, X, YH)
SEQ_FFN = (Z, X, YH, YL, C)
ZX = (Z, X)
YY = (YH, YL)
EIGHT = (YH, YL, C)
TILE = 256

norm_eps = 1e-05
rope_base = 10000.0
xpos_base = 512.0
clip_limit = 1.0
beta_first = 0.9
beta_second = 0.95
adam_eps = 1e-08
decay_rate = 0.1
matrix_rate = 0.04
norm_rate = 0.6

F32 = jnp.float32
BF16 = jnp.bfloat16
SWAP = [(0, 1), (1, 0)]
MIB = 1024 * 1024


def xor_pairs(count, k):
    return [(i, i ^ k) for i in range(count)]


def dot(a, b, da, db):
    return lax.dot_general(a, b, (((da,), (db,)), ((), ())), preferred_element_type=F32)


def shape(dims, kind=F32):
    return jax.ShapeDtypeStruct(dims, kind)


def bytes_of(dims, kind):
    size = math.prod(dims[:-2]) * jnp.dtype(kind).itemsize
    tall = dims[-2] if len(dims) > 1 else 1
    return size * (-(-tall // 8) * 8) * (-(-dims[-1] // 128) * 128)


def in_hbm(out):
    return pltpu.HBM(out.shape, out.dtype)


def local_call(kernel, name, outs, ins, scratch=(), flops=0, moved=0, spare=4, far=(), stay=()):
    need = sum(bytes_of(a.shape, a.dtype) for a in (*ins, *outs))
    need += sum(bytes_of(s.shape, s.dtype) for s in scratch)
    scalar, vector = pltpu.SMEM, pltpu.VMEM
    return pl.pallas_call(
        kernel,
        out_shape=tuple(in_hbm(o) if n in far else o for n, o in enumerate(outs)),
        in_specs=[
            pl.BlockSpec(memory_space=scalar if a.dtype == jnp.int32 else vector) for a in ins
        ],
        out_specs=tuple(pl.BlockSpec(memory_space=vector) for _ in outs),
        scratch_shapes=list(scratch),
        compiler_params=pltpu.CompilerParams(vmem_limit_bytes=need + spare * MIB),
        cost_estimate=pl.CostEstimate(flops=flops, bytes_accessed=moved, transcendentals=0),
        name=name,
    )(*(pltpu.with_memory_space_constraint(a, pltpu.HBM) if n in stay else a for n, a in enumerate(ins)))


def turned(tile):
    return jnp.transpose(tile.astype(F32)).astype(BF16)


def forward_kernel(qkv_ref, start_ref, out_ref, low_ref, top_ref, q_s, k_s, v_s, s_s):
    blocks = q_s.shape[0]
    pieces = TILE // 128
    for i in range(blocks):
        for j in range(pieces):
            part = slice(j * 128, (j + 1) * 128)
            q_s[i, :, part] = qkv_ref[i * pieces + j, 0]
            k_s[i, part, :] = turned(qkv_ref[i * pieces + j, 1])
            v_s[i, :, part] = qkv_ref[i * pieces + j, 2]
    factor = math.log2(math.e) / math.sqrt(HDIM)
    key_line = lax.broadcasted_iota(jnp.int32, (TILE, TILE), 0)
    query_line = lax.broadcasted_iota(jnp.int32, (TILE, TILE), 1)
    for i in range(blocks):
        query = q_s[i]
        begin = start_ref[:, i * TILE : (i + 1) * TILE]
        peak = None
        for b in range(i + 1):
            s = dot(k_s[b], query, 1, 0) * factor
            keep = key_line >= begin - b * TILE
            if b == i:
                keep = keep & (key_line <= query_line)
            s = jnp.where(keep, s, -1e30)
            s_s[b] = s
            high = jnp.max(s, axis=0, keepdims=True)
            peak = high if peak is None else jnp.maximum(peak, high)
        total = jnp.zeros((1, TILE), F32)
        acc = jnp.zeros((HDIM, TILE), F32)
        for b in range(i + 1):
            e = jnp.exp2(s_s[b] - peak)
            total = total + jnp.sum(e, axis=0, keepdims=True)
            acc = acc + dot(v_s[b], e.astype(BF16), 1, 0)
        out = acc / total
        for j in range(pieces):
            out_ref[i * pieces + j] = out[:, j * 128 : (j + 1) * 128]
            low_ref[i * pieces + j] = out[:, j * 128 : (j + 1) * 128].astype(BF16)
        top_ref[:, i * TILE : (i + 1) * TILE] = peak + jnp.log2(total)


def backward_kernel(
    qkv_ref, do_ref, o_ref, top_ref, start_ref, rot_ref, out_ref,
    qt_s, kt_s, dot_s, q_s, k_s, v_s, do_s, dq_s, dk_s, dv_s,
):
    blocks = qt_s.shape[0]
    pieces = TILE // 128
    for i in range(blocks):
        for j in range(pieces):
            part = slice(j * 128, (j + 1) * 128)
            c = i * pieces + j
            qt_s[i, :, part] = qkv_ref[c, 0]
            kt_s[i, :, part] = qkv_ref[c, 1]
            dot_s[i, :, part] = do_ref[c]
            q_s[i, part, :] = turned(qkv_ref[c, 0])
            k_s[i, part, :] = turned(qkv_ref[c, 1])
            v_s[i, part, :] = turned(qkv_ref[c, 2])
            do_s[i, part, :] = turned(do_ref[c])
    scale = 1.0 / math.sqrt(HDIM)
    factor = math.log2(math.e) * scale
    key_line = lax.broadcasted_iota(jnp.int32, (TILE, TILE), 0)
    query_line = lax.broadcasted_iota(jnp.int32, (TILE, TILE), 1)
    for i in range(blocks):
        span = slice(i * TILE, (i + 1) * TILE)
        begin = start_ref[:, span]
        top = top_ref[:, span]
        delta = jnp.concatenate(
            [
                jnp.sum(
                    do_ref[i * pieces + j].astype(F32) * o_ref[i * pieces + j],
                    axis=0,
                    keepdims=True,
                )
                for j in range(pieces)
            ],
            axis=1,
        )
        dq = jnp.zeros((HDIM, TILE), F32)
        for b in range(i + 1):
            s = dot(k_s[b], qt_s[i], 1, 0) * factor
            keep = key_line >= begin - b * TILE
            if b == i:
                keep = keep & (key_line <= query_line)
            p = jnp.where(keep, jnp.exp2(s - top), 0.0)
            dp = dot(v_s[b], dot_s[i], 1, 0)
            ds = (p * (dp - delta)).astype(BF16)
            dq = dq + dot(kt_s[b], ds, 1, 0)
            dk = dot(ds, q_s[i], 1, 0)
            dv = dot(p.astype(BF16), do_s[i], 1, 0)
            if b == i:
                dk_s[b] = dk
                dv_s[b] = dv
            else:
                dk_s[b] += dk
                dv_s[b] += dv
        dq_s[i] = dq
    for i in range(blocks):
        span = slice(i * TILE, (i + 1) * TILE)
        dq = dq_s[i] * scale
        dk = jnp.transpose(dk_s[i]) * scale
        dv = jnp.transpose(dv_s[i])
        results = []
        for n, g in enumerate((dq, dk)):
            co, si = rot_ref[2 * n, :, span], rot_ref[2 * n + 1, :, span]
            front, back = g[:HALF], g[HALF:]
            results.append(
                jnp.concatenate([front * co + back * si, back * co - front * si], axis=0)
            )
        results.append(dv)
        for n, g in enumerate(results):
            for j in range(pieces):
                out_ref[i * pieces + j, n] = g[:, j * 128 : (j + 1) * 128].astype(BF16)


def attend(qkv, start):
    count = qkv.shape[0]
    blocks = count * 128 // TILE
    return pl.pallas_call(
        forward_kernel,
        out_shape=(
            pltpu.HBM((count, HDIM, 128), F32),
            pltpu.HBM((count, HDIM, 128), BF16),
            jax.ShapeDtypeStruct((1, count * 128), F32),
        ),
        scratch_shapes=[
            pltpu.VMEM((blocks, HDIM, TILE), BF16),
            pltpu.VMEM((blocks, TILE, HDIM), BF16),
            pltpu.VMEM((blocks, HDIM, TILE), BF16),
            pltpu.VMEM((blocks, TILE, TILE), F32),
        ],
        compiler_params=pltpu.CompilerParams(vmem_limit_bytes=20 * MIB),
        cost_estimate=pl.CostEstimate(
            flops=2000000000, bytes_accessed=4000000, transcendentals=2400000
        ),
        name="attend",
    )(qkv, start)


def attend_back(qkv, d_out, out, top, start, tables):
    count = qkv.shape[0]
    blocks = count * 128 // TILE
    wide = pltpu.VMEM((blocks, HDIM, TILE), BF16)
    tall = pltpu.VMEM((blocks, TILE, HDIM), BF16)
    return pl.pallas_call(
        backward_kernel,
        out_shape=pltpu.HBM((count, 3, HDIM, 128), BF16),
        scratch_shapes=[
            wide, wide, wide, tall, tall, tall, tall,
            pltpu.VMEM((blocks, HDIM, TILE), F32),
            pltpu.VMEM((blocks, TILE, HDIM), F32),
            pltpu.VMEM((blocks, TILE, HDIM), F32),
        ],
        compiler_params=pltpu.CompilerParams(vmem_limit_bytes=28 * MIB),
        cost_estimate=pl.CostEstimate(
            flops=6000000000, bytes_accessed=6000000, transcendentals=2400000
        ),
        name="attend_back",
    )(qkv, d_out, out, top, start, tables)


def rotation_tables(row_slots):
    index_half = np.arange(HALF, dtype=np.float64)
    places = np.arange(row_slots, dtype=np.float64) - row_slots // 2
    inverse = rope_base ** (-2.0 * index_half / HDIM)
    angles = inverse[:, None] * places[None, :]
    zeta = (2.0 * index_half + 0.4 * HDIM) / (1.4 * HDIM)
    stretch = zeta[:, None] ** (places[None, :] / xpos_base)
    cosine, sine = np.cos(angles), np.sin(angles)
    tables = [cosine * stretch, sine * stretch, cosine / stretch, sine / stretch]
    return np.stack(tables).astype(np.float32)


def moments(values):
    center = jnp.mean(values, axis=-1, keepdims=True)
    spread = jnp.mean(jnp.square(values - center), axis=-1, keepdims=True)
    inverse = lax.rsqrt(spread + norm_eps)
    return (values - center) * inverse, inverse


def norm_back(upstream, gain, normed, inverse):
    scaled = upstream * gain
    return inverse * (
        scaled
        - jnp.mean(scaled, axis=-1, keepdims=True)
        - normed * jnp.mean(scaled * normed, axis=-1, keepdims=True)
    )


def place_parts(parts, target, me):
    share = parts[0].shape[0]
    for k, part in enumerate(parts):
        target[pl.ds(pl.multiple_of((me ^ k) * share, share), share), :] = part[...]


def take_for_scatter(source, target, me):
    share = source.shape[0] // 8
    for side in range(2):
        for j in range(4):
            at = pl.multiple_of((me ^ (2 * j + side)) * share, share)
            target[pl.ds((side * 4 + j) * share, share), :] = source[pl.ds(at, share), :]


def scatter_product(left, right, keep_ref, send_ref, width=None):
    half = left.shape[0] // 2
    width = width or keep_ref.shape[1]
    step = 256

    def body(i, _):
        at = pl.ds(pl.multiple_of(i * step, step), step)
        product = dot(left[...], right[at, : left.shape[1]], 1, 1)
        keep_ref[:, at] = product[:half]
        send_ref[:, at] = product[half:].astype(BF16)
        return 0

    lax.fori_loop(0, width // step, body, 0)


def project_kernel(
    ids, here_ref, near_ref, far_ref, pre_ref, rot_ref, w_ref, qkv_ref, hat_ref, a_ref, x_s, y_s
):
    half, core = ids[1], ids[2]
    rows, slots, width = here_ref.shape
    other = (1 - half) * slots
    for r in range(rows):
        x_s[pl.ds(pl.multiple_of(half * slots, slots), slots), :] = here_ref[r]
        x_s[pl.ds(pl.multiple_of(other + core * 32, 32), 32), :] = near_ref[r]
        x_s[pl.ds(pl.multiple_of(other + (1 - core) * 32, 32), 32), :] = far_ref[r]
        normed, _ = moments(x_s[...].astype(F32))
        low = normed * pre_ref[0:1] + pre_ref[1:2]
        hat_ref[r * 2 * slots : (r + 1) * 2 * slots, :] = normed.astype(BF16)
        a_ref[r * 2 * slots : (r + 1) * 2 * slots, :] = low.astype(BF16)
    span = 2 * slots
    heads = y_s.shape[1] // HDIM
    for n in range(3):
        y_s[...] = dot(a_ref[...], w_ref[:, n * heads * HDIM : (n + 1) * heads * HDIM], 1, 0)
        for r in range(rows):
            for pair in range(heads // 2):
                t = jnp.transpose(
                    y_s[r * span : (r + 1) * span, pair * 128 : (pair + 1) * 128]
                )
                for e in range(2):
                    g = t[e * HDIM : (e + 1) * HDIM]
                    if n < 2:
                        co, si = rot_ref[2 * n], rot_ref[2 * n + 1]
                        front, back = g[:HALF], g[HALF:]
                        g = jnp.concatenate(
                            [front * co - back * si, front * si + back * co], axis=0
                        )
                    qkv_ref[r * heads + pair * 2 + e, n] = g.astype(BF16)


def inner_moments(sums_ref, width, row=0):
    sums = sums_ref[0]
    for k in range(1, 8):
        sums = sums + sums_ref[k]
    center = sums[row : row + 1] / width
    inverse = lax.rsqrt(sums[row + 1 : row + 2] / width - center * center + norm_eps)
    return sums, center, inverse


def high_low(value):
    high = value.astype(BF16).astype(F32)
    return [high, value - high]


def out_kernel(
    ids, o_ref, gain_ref, w_ref, keep_ref, send_ref, line_ref, c_s, sum_s, l_s, k_s
):
    count, _, span = o_ref.shape
    heads = count // 4
    width = w_ref.shape[0]
    half = keep_ref.shape[0]
    for r in range(4):
        o = jnp.concatenate([o_ref[r * heads + h] for h in range(heads)], axis=0).astype(F32)
        first = jnp.sum(o, axis=0, keepdims=True)
        second = jnp.sum(o * o, axis=0, keepdims=True)
        line_ref[0:1, r * span : (r + 1) * span] = first
        line_ref[1:2, r * span : (r + 1) * span] = second
        lines = [first, second, *high_low(first), *high_low(second)]
        lines.append(jnp.zeros((128 - len(lines), span), F32))
        sums = jnp.transpose(jnp.concatenate(lines, axis=0))
        c = jnp.transpose(o * gain_ref[...]).astype(BF16)
        for s in range(8):
            at = slice(s * 64 + r * 16, s * 64 + (r + 1) * 16)
            c_s[at, :] = c[s * 16 : (s + 1) * 16]
            sum_s[at, :] = sums[s * 16 : (s + 1) * 16]
    take_for_scatter(c_s, l_s, ids[0])
    take_for_scatter(sum_s, k_s, ids[0])
    scatter_product(l_s, w_ref, keep_ref, send_ref, width)
    keep_ref[:, width:] = k_s[:half]
    send_ref[:, width:] = k_s[half:].astype(BF16)


def normed_heads_kernel(o_ref, sums_ref, gain_ref, shift_ref, c_ref, *, width):
    count, _, span = o_ref.shape
    heads = count // 4
    _, center, inverse = inner_moments(sums_ref, width, 4)
    for r in range(4):
        at = slice(r * span, (r + 1) * span)
        o = jnp.concatenate([o_ref[r * heads + h] for h in range(heads)], axis=0).astype(F32)
        c = (o - center[:, at]) * inverse[:, at] * gain_ref[...] + shift_ref[...]
        c = jnp.transpose(c).astype(BF16)
        for s in range(8):
            c_ref[s * 64 + r * 16 : s * 64 + (r + 1) * 16, :] = c[s * 16 : (s + 1) * 16]


def gain_product_kernel(gain_ref, shift_ref, w_ref, out_ref):
    rows = [*high_low(gain_ref[...]), *high_low(shift_ref[...])]
    rows = jnp.concatenate(rows + [jnp.zeros((12, rows[0].shape[1]), F32)], axis=0).astype(BF16)
    product = dot(rows, w_ref[...], 1, 1)
    both = [product[0:1] + product[1:2], product[2:3] + product[3:4]]
    out_ref[...] = jnp.concatenate(both + [jnp.zeros((6, product.shape[1]), F32)], axis=0)


def two_sums(stats, other):
    first = stats[:, 0:1] + (other[:, 2:3] + other[:, 3:4])
    second = stats[:, 1:2] + (other[:, 4:5] + other[:, 5:6])
    return first, second


def core_sum_stats_kernel(keep_ref, got_ref, own_ref, one_ref, two_ref, three_ref):
    share = own_ref.shape[0]
    width = own_ref.shape[1] - 128
    both = keep_ref[:, :width] + got_ref[:, :width].astype(F32)
    first, second = two_sums(keep_ref[:, width:], got_ref[:, width:].astype(F32))
    lane = lax.broadcasted_iota(jnp.int32, (keep_ref.shape[0], 128), 1)
    stats = jnp.zeros(lane.shape, F32)
    for n, v in enumerate([first, second, *high_low(first), *high_low(second)]):
        stats = jnp.where(lane == n, v, stats)
    own_ref[:, :width] = both[:share]
    own_ref[:, width:] = stats[:share]
    for j, ref in ((1, one_ref), (2, two_ref), (3, three_ref)):
        ref[:, :width] = both[j * share : (j + 1) * share].astype(BF16)
        ref[:, width:] = stats[j * share : (j + 1) * share].astype(BF16)


def core_sum_kernel(keep_ref, got_ref, own_ref, one_ref, two_ref, three_ref):
    share = own_ref.shape[0]
    both = keep_ref[...] + got_ref[...].astype(F32)
    own_ref[...] = both[:share]
    for j, ref in ((1, one_ref), (2, two_ref), (3, three_ref)):
        ref[...] = both[j * share : (j + 1) * share].astype(BF16)


def summed(own_ref, refs):
    total = own_ref[...]
    for ref in refs:
        total = total + ref[...].astype(F32)
    return total


def middle_kernel(
    own_ref, one, two, three, x_ref, usable_ref, pre_ref, g_ref, g_one, g_two, g_three,
    r1_ref, bb_ref,
):
    width = r1_ref.shape[1]
    total = own_ref[...]
    product, stats = total[:, :width], total[:, width:]
    for ref in (one, two, three):
        product = product + ref[:, :width].astype(F32)
        first, second = two_sums(stats, ref[:, width:].astype(F32))
        lane = lax.broadcasted_iota(jnp.int32, stats.shape, 1)
        stats = jnp.where(lane == 0, first, jnp.where(lane == 1, second, 0.0))
    center = stats[:, 0:1] / width
    inverse = lax.rsqrt(stats[:, 1:2] / width - center * center + norm_eps)
    g = (g_ref[...] + g_one[...]) + (g_two[...] + g_three[...])
    attn = inverse * (product - center * g[0:1]) + g[1:2]
    r1 = x_ref[...].astype(F32) + usable_ref[...] * attn
    normed, _ = moments(r1)
    r1_ref[...] = r1
    bb_ref[...] = (normed * pre_ref[2:3] + pre_ref[3:4]).astype(BF16)


def result_kernel(own_ref, one, two, three, r1_ref, usable_ref, out_ref):
    f = summed(own_ref, (one, two, three))
    out_ref[...] = (r1_ref[...] + usable_ref[...] * f).astype(BF16)


def down_back_kernel(ids, *refs):
    parts, (w_ref, df_ref, dhn_ref) = refs[:8], refs[8:]
    place_parts(parts, df_ref, ids[0])

    def body(i, _):
        at = pl.ds(pl.multiple_of(i * 256, 256), 256)
        dhn_ref[:, at] = dot(df_ref[...], w_ref[:, at], 1, 0)
        return 0

    lax.fori_loop(0, dhn_ref.shape[1] // 256, body, 0)


def up_kernel(ids, *refs):
    parts, refs = refs[:8], refs[8:]
    w_ref, dhn_ref, gain_ref, o_ref, bb_ref, h_ref, u_ref, sums_ref = refs
    place_parts(parts, bb_ref, ids[0])
    tokens, units = h_ref.shape
    step = 256

    def body(i, carry):
        at = pl.ds(pl.multiple_of(i * step, step), step)
        u = dot(bb_ref[...], w_ref[:, at], 1, 0)
        cdf = 0.5 * (1.0 + lax.erf(u * (1.0 / math.sqrt(2.0))))
        h = u * cdf
        h_ref[:, at] = h
        u_ref[:, at] = u
        scaled = dhn_ref[:, at] * gain_ref[:, at]
        terms = (h, h * h, scaled, scaled * h)
        return tuple(c + jnp.sum(t, axis=1, keepdims=True) for c, t in zip(carry, terms))

    zero = jnp.zeros((tokens, 1), F32)
    sums = lax.fori_loop(0, units // step, body, (zero,) * 4)
    lane = lax.broadcasted_iota(jnp.int32, (tokens, 128), 1)
    wide = jnp.zeros((tokens, 128), F32)
    for n, s in enumerate(sums):
        wide = jnp.where(lane == n, s, wide)
    line = jnp.transpose(wide)
    line = jnp.concatenate([line[:4], o_ref[...], line[6:8]], axis=0)
    for k in range(8):
        sums_ref[k] = line


def slope_kernel(h_ref, u_ref, dhn_ref, gain_ref, first_ref, slope_ref, last_ref):
    def body(i, _):
        at = pl.ds(pl.multiple_of(i * 256, 256), 256)
        u = u_ref[:, at]
        slope = 0.5 * (1.0 + lax.erf(u * (1.0 / math.sqrt(2.0)))) + u * (
            jnp.exp(-0.5 * u * u) * (1.0 / math.sqrt(2.0 * math.pi))
        )
        first_ref[:, at] = dhn_ref[:, at] * gain_ref[:, at] * slope
        slope_ref[:, at] = slope
        last_ref[:, at] = h_ref[:, at] * slope
        return 0

    lax.fori_loop(0, u_ref.shape[1] // 256, body, 0)


def inner_columns(sums_ref):
    sums, center, inverse = inner_moments(sums_ref, FF)
    mean_scaled = sums[2:3] / FF
    mean_both = inverse * (sums[3:4] / FF - center * mean_scaled)
    by_slope = inverse * (inverse * mean_both * center - mean_scaled)
    by_last = inverse * inverse * mean_both
    rows = jnp.concatenate([center, inverse, by_slope, by_last, sums[4:8]], axis=0)
    columns = jnp.transpose(jnp.concatenate([rows] * 16, axis=0))
    return tuple(columns[:, n : n + 1] for n in range(4))


def inner_back_kernel(
    ids, first_ref, slope_ref, last_ref, sums_ref, w_ref, keep_ref, send_ref, du_ref, l_s
):
    _, inverse, by_slope, by_last = inner_columns(sums_ref)

    def body(i, _):
        at = pl.ds(pl.multiple_of(i * 256, 256), 256)
        du = inverse * first_ref[:, at] + by_slope * slope_ref[:, at] - by_last * last_ref[:, at]
        du_ref[:, at] = du.astype(BF16)
        return 0

    lax.fori_loop(0, du_ref.shape[1] // 256, body, 0)
    take_for_scatter(du_ref, l_s, ids[0])
    scatter_product(l_s, w_ref, keep_ref, send_ref)


def inner_norm_kernel(h_ref, dhn_ref, sums_ref, gain_ref, shift_ref, hn_ref, sub_ref):
    center, inverse, _, _ = inner_columns(sums_ref)

    def body(i, _):
        at = pl.ds(pl.multiple_of(i * 256, 256), 256)
        hat = (h_ref[:, at] - center) * inverse
        dhn = dhn_ref[:, at]
        hn_ref[:, at] = (hat * gain_ref[:, at] + shift_ref[:, at]).astype(BF16)
        sub_ref[0:1, at] = jnp.sum(dhn * hat, axis=0, keepdims=True)
        sub_ref[1:2, at] = jnp.sum(dhn, axis=0, keepdims=True)
        return 0

    lax.fori_loop(0, h_ref.shape[1] // 256, body, 0)


def down_kernel(ids, hn_ref, w_ref, keep_ref, send_ref, l_s):
    take_for_scatter(hn_ref, l_s, ids[0])
    scatter_product(l_s, w_ref, keep_ref, send_ref)


def mlp_grad_kernel(df_ref, hn_ref, bb_ref, du_ref, out_ref):
    units = hn_ref.shape[1]
    out_ref[:, :units] = dot(jnp.transpose(bb_ref[...]), du_ref[...], 1, 0).astype(BF16)
    out_ref[:, units:] = dot(jnp.transpose(df_ref[...]), hn_ref[...], 1, 0).astype(BF16)


def mlp_grad(df, hn, bb, du):
    tokens, width = df.shape
    units = hn.shape[1]
    step = 256
    narrow = pl.BlockSpec((tokens, step), lambda i: (0, i))
    whole = pl.BlockSpec((tokens, units), lambda i: (0, 0))
    return pl.pallas_call(
        mlp_grad_kernel,
        grid=(width // step,),
        out_shape=pltpu.HBM((width, 2 * units), BF16),
        in_specs=[narrow, whole, narrow, whole],
        out_specs=pl.BlockSpec((step, 2 * units), lambda i: (i, 0)),
        compiler_params=pltpu.CompilerParams(vmem_limit_bytes=20 * MIB),
        cost_estimate=pl.CostEstimate(
            flops=4 * tokens * width * units, bytes_accessed=14 * MIB, transcendentals=0
        ),
        name="mlp_grad",
    )(df, hn, bb, du)


def middle_back_kernel(
    own_ref, one, two, three, r1_ref, cot_ref, usable_ref, pre_ref, dr1_ref, dattn_ref, grad_ref
):
    dbb = summed(own_ref, (one, two, three))
    hat, inverse = moments(r1_ref[...])
    dr1 = cot_ref[...].astype(F32) + norm_back(dbb, pre_ref[2:3], hat, inverse)
    dr1_ref[...] = dr1
    dattn_ref[...] = (usable_ref[...] * dr1).astype(BF16)
    grad_ref[0:1] = jnp.sum(dbb * hat, axis=0, keepdims=True)
    grad_ref[1:2] = jnp.sum(dbb, axis=0, keepdims=True)


def out_back_kernel(ids, *refs):
    parts, refs = refs[:8], refs[8:]
    w_ref, o_ref, sums_ref, gain_ref, dattn_ref, dc_ref, out_ref, sub_ref, y_s = refs
    place_parts(parts, dattn_ref, ids[0])
    y_s[...] = dot(dattn_ref[...], w_ref[...], 1, 0)
    count, _, span = o_ref.shape
    heads = count // 4
    _, center, inverse = inner_moments(sums_ref, dattn_ref.shape[1], 4)
    gain_grad, shift_grad, lines = 0.0, 0.0, []
    for r in range(4):
        at = slice(r * span, (r + 1) * span)
        dc = jnp.concatenate(
            [y_s[s * 64 + r * 16 : s * 64 + (r + 1) * 16, :] for s in range(8)], axis=0
        )
        dc = jnp.transpose(dc)
        dc_ref[:, at] = dc
        o = jnp.concatenate([o_ref[r * heads + h] for h in range(heads)], axis=0).astype(F32)
        hat = (o - center[:, at]) * inverse[:, at]
        gain_grad = gain_grad + jnp.sum(dc * hat, axis=1, keepdims=True)
        shift_grad = shift_grad + jnp.sum(dc, axis=1, keepdims=True)
        scaled = dc * gain_ref[...]
        lines.append(
            jnp.concatenate(
                [
                    jnp.sum(scaled, axis=0, keepdims=True),
                    jnp.sum(scaled * hat, axis=0, keepdims=True),
                    jnp.zeros((6, span), F32),
                ],
                axis=0,
            )
        )
    line = jnp.concatenate(lines, axis=1)
    for k in range(8):
        out_ref[k] = line
    sub_ref[...] = jnp.concatenate(
        [
            jnp.transpose(jnp.broadcast_to(g, (g.shape[0], 128)))[0:1]
            for g in (gain_grad, shift_grad)
        ],
        axis=0,
    )


def head_grad_kernel(dc_ref, o_ref, sums_ref, back_ref, gain_ref, out_ref, *, width):
    count, _, span = o_ref.shape
    heads = count // 4
    _, center, inverse = inner_moments(sums_ref, width, 4)
    back = back_ref[0]
    for k in range(1, 8):
        back = back + back_ref[k]
    for r in range(4):
        at = slice(r * span, (r + 1) * span)
        first, second = back[0:1, at] / width, back[1:2, at] / width
        for h in range(heads):
            part = slice(h * HDIM, (h + 1) * HDIM)
            hat = (o_ref[r * heads + h].astype(F32) - center[:, at]) * inverse[:, at]
            scaled = dc_ref[part, at] * gain_ref[part]
            out_ref[r * heads + h] = (
                inverse[:, at] * (scaled - first - hat * second)
            ).astype(BF16)


def out_grad_kernel(dattn_ref, c_ref, out_ref):
    out_ref[...] = dot(jnp.transpose(dattn_ref[...]), c_ref[...], 1, 0).astype(BF16)


def out_grad(dattn, c):
    tokens, width = dattn.shape
    units = c.shape[1]
    step = 512
    return pl.pallas_call(
        out_grad_kernel,
        grid=(width // step,),
        out_shape=pltpu.HBM((width, units), BF16),
        in_specs=[
            pl.BlockSpec((tokens, step), lambda i: (0, i)),
            pl.BlockSpec((tokens, units), lambda i: (0, 0)),
        ],
        out_specs=pl.BlockSpec((step, units), lambda i: (i, 0)),
        compiler_params=pltpu.CompilerParams(vmem_limit_bytes=16 * MIB),
        cost_estimate=pl.CostEstimate(
            flops=2 * tokens * width * units, bytes_accessed=4 * MIB, transcendentals=0
        ),
        name="out_grad",
    )(dattn, c)


def ring_block(group, i, j):
    return (((group >> 2) + i) & 3) * 4 + ((group + j) & 3)


def turn_kernel(ids, a_ref, out_ref):
    for r in range(16):
        at = pl.ds(pl.multiple_of(ring_block(ids[3], r // 4, r % 4) * 128, 128), 128)
        to = (r % 4) * 4 + r // 4
        out_ref[to * 128 : (to + 1) * 128, :] = jnp.transpose(a_ref[:, at])


def column(row):
    return jnp.transpose(jnp.broadcast_to(row, (128, row.shape[1])))[:, 0:1]


def row_of(col):
    return jnp.transpose(jnp.broadcast_to(col, (col.shape[0], 128)))[0:1]


def in_grad_kernel(
    ids, dqkv_ref, xt_ref, w_ref, pre_ref, out_ref, three_ref, o_ref, h_ref, *refs
):
    lines, (tokens_ref, d_s, one_s) = refs[:10], refs[10:]

    def put(side, place, other, columns, value):
        refs = lines[5 * side : 5 * side + 5]
        if place == 2:
            ref, row = refs[2 + other // 2], (other % 2) * 64
        else:
            ref, row = refs[(0, 1, None, 4)[place]], other * 64
        ref[row : row + 64, columns] = value

    count = dqkv_ref.shape[0]
    heads = count // 4
    units = d_s.shape[0]
    for r in range(4):
        for n in range(3):
            for h in range(heads):
                base = (n * heads + h) * HDIM
                d_s[base : base + HDIM, r * 128 : (r + 1) * 128] = dqkv_ref[r * heads + h, n]
    sums = []
    for n in range(0, units, 128):
        total = jnp.zeros((1, 128), F32)
        for r in range(4):
            t = jnp.transpose(d_s[n : n + 128, r * 128 : (r + 1) * 128].astype(F32))
            total = total + jnp.sum(t, axis=0, keepdims=True)
            t = t.astype(BF16)
            for s in range(8):
                tokens_ref[s * 64 + r * 16 : s * 64 + (r + 1) * 16, n : n + 128] = t[
                    s * 16 : (s + 1) * 16
                ]
        sums.append(total)
    sums = jnp.concatenate(sums, axis=1)
    for j in range(4):
        products = dot(xt_ref[j * 512 : (j + 1) * 512, :], d_s[...], 1, 1)
        for i in range(4):
            at = pl.ds(pl.multiple_of(ring_block(ids[3], i, j) * 128, 128), 128)
            product = products[i * 128 : (i + 1) * 128]
            gradient = product * column(pre_ref[0:1, at]) + column(pre_ref[1:2, at]) * sums
            gradient = gradient.astype(BF16)
            outward = out_ref[at, :]
            for columns, value in ((slice(units), gradient), (slice(units, None), outward)):
                put(0, j, i, columns, value[:64])
                put(1, i, j, columns, value[64:])
            w = w_ref[at, :units].astype(F32)
            one_s[0:1, at] = row_of(jnp.sum(w * product, axis=1, keepdims=True))
            one_s[1:2, at] = row_of(jnp.sum(w * sums, axis=1, keepdims=True))
    width = lines[0].shape[1]
    half = o_ref.shape[1]
    small = []
    for ref in (one_s, three_ref):
        for n in range(2):
            small += [ref[n : n + 1, :width], ref[n : n + 1, width:]]
    for n in range(2):
        first = [o_ref[n : n + 1], h_ref[n : n + 1, : width - half]]
        last = [h_ref[n : n + 1, width - half :], jnp.zeros((1, width - half), F32)]
        small += [jnp.concatenate(first, axis=1), jnp.concatenate(last, axis=1)]
    small.append(jnp.zeros((16 - len(small), width), F32))
    small = jnp.concatenate(small, axis=0).astype(BF16)
    for ref in (lines[0], lines[1], lines[2], lines[4]):
        ref[ref.shape[0] - 16 :, :] = small


def in_back_kernel(ids, d_ref, w_ref, keep_ref, send_ref, l_s):
    take_for_scatter(d_ref, l_s, ids[0])
    scatter_product(l_s, w_ref, keep_ref, send_ref)


def summed_low(refs):
    total = refs[0][...].astype(F32)
    for ref in refs[1:]:
        total = total + ref[...].astype(F32)
    return total


def ring_sum_kernel(*refs):
    ins, outs = refs[:8], refs[8:]
    for side in range(2):
        on, back, got_on, got_back = ins[4 * side : 4 * side + 4]
        out_on, out_back = outs[2 * side : 2 * side + 2]
        rows = got_back.shape[0]
        out_on[:rows, :] = (on[:rows].astype(F32) + got_on[:rows].astype(F32)).astype(BF16)
        out_on[rows : 2 * rows, :] = on[rows : 2 * rows]
        out_back[:rows, :] = back[:rows]
        both = back[rows : 2 * rows].astype(F32) + got_back[...].astype(F32)
        out_back[rows : 2 * rows, :] = both.astype(BF16)
        if got_on.shape[0] > rows:
            small = on[2 * rows :].astype(F32) + got_on[rows:].astype(F32)
            out_on[2 * rows :, :] = small.astype(BF16)
            out_back[2 * rows :, :] = back[2 * rows :]


def line_sum_kernel(*refs):
    first, second, outs = refs[:3], refs[3:6], refs[6:]
    total = summed_low(first)
    small = total[256:272]
    outs[0][0:64, :] = total[0:64]
    outs[0][64:80, :] = small
    for k in (1, 2, 3):
        outs[k][0:64, :] = total[k * 64 : (k + 1) * 64].astype(BF16)
        outs[k][64:80, :] = small.astype(BF16)
    total = summed_low(second)
    outs[4][...] = total[0:64]
    for k in (1, 2, 3):
        outs[4 + k][...] = total[k * 64 : (k + 1) * 64].astype(BF16)


def last_sum_kernel(ids, *refs):
    ins, (mlp_ref, keep_ref, give_ref, out_ref) = refs[:8], refs[8:]
    width = keep_ref.shape[1]
    low = ids[1] == 0
    second = summed_low(ins[4:])
    slots = second.shape[0]
    total = summed_low(ins[:4])
    first, small = total[:slots], total[slots:]
    keep_ref[:slots, :] = jnp.where(low, first, second).astype(BF16)
    give_ref[:slots, :] = jnp.where(low, second, first).astype(BF16)
    keep_ref[slots:, :] = small.astype(BF16)
    give_ref[slots:, :] = small.astype(BF16)
    squares = whole_sum(first * first + second * second) + mlp_ref[0:1, 0:1]

    def joined(begin):
        return jnp.concatenate([small[begin : begin + 1], small[begin + 1 : begin + 2]], axis=1)

    sub = jnp.concatenate([joined(8), joined(10)], axis=0)
    lane = lax.broadcasted_iota(jnp.int32, (4, 2 * width), 1)
    scalars = jnp.zeros(lane.shape, F32)
    for n, term in enumerate([*high_low(squares), *high_low(whole_sum(sub * sub))]):
        scalars = jnp.where(lane // 128 == n, term, scalars)
    lines = jnp.concatenate([joined(2 * n) for n in range(4)] + [scalars], axis=0).astype(BF16)
    for k in range(out_ref.shape[0]):
        out_ref[k] = lines


def group_total_kernel(small_ref, total_ref, out_ref):
    total = small_ref[0].astype(F32)
    for k in range(1, small_ref.shape[0]):
        total = total + small_ref[k].astype(F32)
    total_ref[...] = total
    squares = total[4:5, 0:128] + total[4:5, 128:256]
    for k in range(out_ref.shape[0]):
        out_ref[k] = jnp.broadcast_to(squares, out_ref.shape[1:])


def input_back_kernel(own_ref, one, two, three, x_ref, dr1_ref, pre_ref, out_ref):
    da = summed(own_ref, (one, two, three))
    hat, inverse = moments(x_ref[...].astype(F32))
    out_ref[...] = (dr1_ref[...] + norm_back(da, pre_ref[0:1], hat, inverse)).astype(BF16)


def whole_sum(values):
    return jnp.sum(jnp.sum(values, axis=1, keepdims=True), axis=0, keepdims=True)


def rest_kernel(ids, g_ref, keep_ref, give_ref, sum_ref):
    slots = keep_ref.shape[0]
    half = ids[1]
    keep_ref[...] = g_ref[pl.ds(pl.multiple_of(half * slots, slots), slots), :]
    give_ref[...] = g_ref[pl.ds(pl.multiple_of((1 - half) * slots, slots), slots), :]
    total = jnp.zeros((1, 1), F32)
    for k in range(g_ref.shape[0] // 32):
        g = g_ref[k * 32 : (k + 1) * 32, :].astype(F32)
        total = total + whole_sum(g * g)
    sum_ref[...] = jnp.broadcast_to(total, sum_ref.shape)


def adam_step(weight, moment, squares, gradient, factor, step_rate, decay_weight):
    clipped = gradient * factor
    moment_new = beta_first * moment + (1.0 - beta_first) * clipped
    squares_new = beta_second * squares + (1.0 - beta_second) * clipped * clipped
    moment_hat = moment_new * (1.0 / (1.0 - beta_first**STEP))
    squares_hat = squares_new * (1.0 / (1.0 - beta_second**STEP))
    updated = weight - step_rate * (
        moment_hat / (jnp.sqrt(squares_hat) + adam_eps) + decay_weight * weight
    )
    return updated, moment_new, squares_new


def adam_kernel(
    ids, small_ref, norm_part, sub_own, sub_take, att_keep, att_take, mlp_keep, mlp_take, *refs
):
    states, outs, norm_out = refs[:18], refs[18:36], refs[36]
    low = ids[1] == 0
    squares = norm_part[0, 0:1, 0:1]
    for k in range(1, norm_part.shape[0]):
        squares = squares + norm_part[k, 0:1, 0:1]
    pre = small_ref[0:4]
    squares = squares + small_ref[4:5, 256:257] + small_ref[4:5, 384:385] + whole_sum(pre * pre)
    norm = jnp.sqrt(squares)
    factor = jnp.minimum(1.0, clip_limit / (norm + 1e-06))
    half = att_keep.shape[1] // 4

    def pair(mine, theirs, at):
        mine = mine[:, at * half : (at + 1) * half].astype(F32)
        theirs = theirs[:, at * half : (at + 1) * half].astype(F32)
        return jnp.concatenate(
            [jnp.where(low, mine, theirs), jnp.where(low, theirs, mine)], axis=1
        )

    def step(which, index, gradient, rate, decay):
        state = [states[3 * which + n][index] for n in range(3)]
        for n, value in enumerate(adam_step(*state, gradient, factor, rate, decay)):
            outs[3 * which + n][index] = value

    everything = slice(None)
    for k in range(3):
        step(0, (k,), pair(att_keep, att_take, k), matrix_rate, decay_rate)
    step(1, (everything,), pair(att_keep, att_take, 3), matrix_rate, decay_rate)
    for b in range(4):
        step(2, (everything, b), pair(mlp_keep, mlp_take, b), matrix_rate, decay_rate)
        step(3, (b,), pair(mlp_keep, mlp_take, 4 + b), matrix_rate, decay_rate)

    @pl.when(pl.program_id(0) == 0)
    def _():
        step(4, (everything,), pre, norm_rate, 0.0)
        for b in range(5):
            row, at = (0, b) if b < 4 else (1, 0)
            both = pair(sub_own, sub_take, at)
            both = jnp.concatenate([both[8 + row : 9 + row], both[10 + row : 11 + row]], axis=0)
            step(5, (b,), both, norm_rate, 0.0)
        norm_out[...] = jnp.broadcast_to(norm, norm_out.shape)


def adam(ids, small, norm_part, gradients, states):
    flat = [a for state in states for a in state]
    step = 32

    def whole(a):
        return pl.BlockSpec(a.shape, lambda i, nd=a.ndim: (0,) * nd)

    def blocks(which, a):
        if which > 3:
            return whole(a)
        dim = (1, 0, 0, 1)[which]
        block = tuple(step if n == dim else d for n, d in enumerate(a.shape))
        return pl.BlockSpec(
            block, lambda i, nd=a.ndim, dim=dim: tuple(i if n == dim else 0 for n in range(nd))
        )

    specs = [blocks(n // 3, a) for n, a in enumerate(flat)]
    rows = [pl.BlockSpec((step, g.shape[1]), lambda i: (i, 0)) for g in gradients]
    a_rows = gradients[2].shape[0] // 16
    norm = shape((1, 1))
    return pl.pallas_call(
        adam_kernel,
        grid=(gradients[2].shape[0] // step,),
        out_shape=tuple(shape(a.shape) for a in flat) + (norm,),
        in_specs=[
            pl.BlockSpec(memory_space=pltpu.SMEM),
            whole(small),
            whole(norm_part),
            *(pl.BlockSpec((16, a.shape[1]), lambda i: (a_rows, 0)) for a in gradients[:2]),
            *rows,
            *specs,
        ],
        out_specs=tuple(specs) + (whole(norm),),
        compiler_params=pltpu.CompilerParams(vmem_limit_bytes=56 * MIB),
        cost_estimate=pl.CostEstimate(flops=0, bytes_accessed=12 * MIB, transcendentals=0),
        name="adam",
    )(ids, small, norm_part, *gradients[:2], *gradients, *flat)


def eight_parts(own, *meanwhile):
    lines = [lax.ppermute(own, YY, xor_pairs(4, k)) for k in (1, 2, 3)]
    if meanwhile:
        lines = [after(line, *meanwhile) for line in lines]
    lines = [own] + lines
    parts = []
    for line in lines:
        parts += [line, lax.ppermute(line, C, SWAP)]
    return parts


def core_scatter(keep, send, kernel=core_sum_kernel):
    share, width = keep.shape[0] // 4, keep.shape[1]
    got = lax.ppermute(send, C, SWAP)
    return local_call(
        kernel,
        "core_sum",
        [shape((share, width))] + [shape((share, width), BF16)] * 3,
        [keep, got],
        moved=5 * MIB,
    )


def line_scatter(own, *sent):
    return [own] + [lax.ppermute(s, YY, xor_pairs(4, k)) for k, s in zip((1, 2, 3), sent)]


def finish_scatter(keep, send, work=None, kernel=core_sum_kernel):
    own, *sent = core_scatter(keep, send, kernel)
    lines = line_scatter(own, *sent)
    if work is None:
        return lines
    done = work(own)
    return lines[:1] + [after(line, *done) for line in lines[1:]], done


def ring_pairs(k):
    return [(i, (i + k) % 4) for i in range(4)]


def crossing(lines, first_axis, second_axis):
    first, second = list(lines[:4]), list(lines[4:])
    for k in (2, 1, 3):
        first[k] = lax.ppermute(first[k], first_axis, ring_pairs(k))
        second[k] = lax.ppermute(second[k], second_axis, ring_pairs(k))
    return first, second


def ring_crossing(lines):
    sides = [(lines[:5], X), (lines[5:], Z)]
    ins = []
    for (_, on, two_on, two_back, back), axis in sides:
        ins += [on, back]
        ins += [lax.ppermute(two_on, axis, ring_pairs(1)), lax.ppermute(two_back, axis, ring_pairs(3))]
    outs = [shape(ins[n].shape, BF16) for n in (0, 1, 4, 5)]
    sums = local_call(ring_sum_kernel, "ring_sum", outs, ins, moved=5 * MIB)
    return [
        [side[0], lax.ppermute(on, axis, ring_pairs(1)), lax.ppermute(back, axis, ring_pairs(3))]
        for (side, axis), on, back in zip(sides, sums[::2], sums[1::2])
    ]


def each_to_all(copies, axis):
    return lax.all_to_all(copies, axis, split_axis=0, concat_axis=0, tiled=True)


def after(value, *others):
    return lax.optimization_barrier((value, *others))[0]


def shards(
    hidden_in, cotangent, doc_lengths,
    inward, inward_moment, inward_squares,
    outward, outward_moment, outward_squares,
    upward, upward_moment, upward_squares,
    downward, downward_moment, downward_squares,
    prenorm, prenorm_moment, prenorm_squares,
    subnorm, subnorm_moment, subnorm_squares,
):
    rows, seq_slots, width = hidden_in.shape
    quarter = cotangent.shape[1]
    group_slots = 2 * seq_slots
    row_slots = group_slots * lax.axis_size(ZX)
    half = inward.shape[2] // 2
    heads = half // HDIM
    units = 4 * half
    tokens = rows * group_slots
    share = rows * quarter
    zx = lax.axis_index(ZX)
    row_index = lax.axis_index(Z)
    yh = lax.axis_index(YH)
    core = lax.axis_index(C)
    ffn = lax.axis_index(FFN)
    me = lax.axis_index(EIGHT)
    low_side = yh == 0
    first_core = core == 0
    ids = jnp.stack([me, yh, core, zx]).astype(jnp.int32)

    def mine_theirs(array, axis):
        low = array.astype(BF16)
        mine = lax.dynamic_slice_in_dim(low, yh * half, half, axis)
        theirs = lax.dynamic_slice_in_dim(low, (1 - yh) * half, half, axis)
        return mine, theirs

    def in_order(own, other):
        return jnp.concatenate(
            [jnp.where(low_side, own, other), jnp.where(low_side, other, own)], axis=0
        )

    def both_halves(pairs):
        other = lax.ppermute(jnp.concatenate([t for _, t in pairs], axis=1), YH, SWAP)
        own = jnp.concatenate([m for m, _ in pairs], axis=1)
        return in_order(own, other)

    def rows_of(pair, order):
        return tuple(jnp.transpose(t, order).reshape(seq_slots, -1) for t in pair)

    in_pair = rows_of(mine_theirs(inward, 2), (0, 1, 2))
    out_pair = rows_of(mine_theirs(outward, 0), (1, 0))
    up_pair = rows_of(mine_theirs(upward, 2), (0, 1, 2))
    down_pair = rows_of(mine_theirs(downward, 1), (2, 0, 1))
    w_att = both_halves([in_pair, out_pair])
    w_att = lax.all_gather(w_att, ZX, axis=0, tiled=True)
    w_out = w_att[:, 3 * half :]
    w_mlp = both_halves([up_pair, down_pair])
    w_mlp = lax.all_gather(w_mlp, ZX, axis=0, tiled=True)
    w_up, w_down = w_mlp[:, :units], w_mlp[:, units:]

    doc_ends = jnp.cumsum(doc_lengths, axis=1)
    places = jnp.arange(row_slots, dtype=jnp.int32)
    my_ends = lax.dynamic_slice_in_dim(doc_ends, row_index, 1, 0)
    start = jnp.max(
        jnp.where(places[None, :] >= my_ends.reshape(-1, 1), my_ends.reshape(-1, 1), 0),
        axis=0,
        keepdims=True,
    )
    own_places = zx * group_slots + me * quarter + jnp.arange(quarter, dtype=jnp.int32)
    own_usable = (own_places[None, :] < doc_ends[:, -1:]).astype(F32).reshape(share, 1)

    half_slots = seq_slots // 2
    sent = lax.dynamic_slice_in_dim(hidden_in, core * half_slots, half_slots, 1)
    got_near = lax.ppermute(sent, YY, [(i, 3 - i) for i in range(4)])
    got_far = lax.ppermute(got_near, C, SWAP)
    own_hidden = lax.dynamic_slice_in_dim(hidden_in, ffn * quarter, quarter, 1)
    own_hidden = own_hidden.reshape(share, width)
    own_cot = cotangent.reshape(share, width)
    df_own = (own_usable * own_cot.astype(F32)).astype(BF16)
    df_parts = eight_parts(after(df_own, got_near))

    tables = jnp.asarray(rotation_tables(row_slots))
    near = lax.dynamic_slice_in_dim(tables, zx * group_slots, group_slots, 2)
    qkv, x_hat = local_call(
        project_kernel,
        "project",
        [
            shape((rows * heads, 3, HDIM, group_slots), BF16),
            shape((tokens, width), BF16),
        ],
        [ids, hidden_in, got_near, got_far, after(prenorm, *df_parts), near, w_att],
        [
            pltpu.VMEM((tokens, width), BF16),
            pltpu.VMEM((group_slots, width), BF16),
            pltpu.VMEM((tokens, half), F32),
        ],
        flops=2 * tokens * width * 3 * half,
        moved=8 * MIB,
        far=(0, 1),
    )
    sub = lax.dynamic_slice_in_dim(subnorm, yh * half, half, 2)
    gain_o, shift_o = sub[0, 0].reshape(half, 1), sub[1, 0].reshape(half, 1)
    gain_h, shift_h = sub[0, 1:].reshape(1, units), sub[1, 1:].reshape(1, units)
    (gains,) = local_call(
        gain_product_kernel,
        "gain_product",
        [shape((8, width))],
        [sub[0, 0].reshape(1, half), sub[1, 0].reshape(1, half), after(w_out, x_hat)],
    )
    gains = gains + lax.ppermute(gains, C, SWAP)
    gains = [gains] + [lax.ppermute(gains, YY, xor_pairs(4, k)) for k in (2, 1, 3)]
    qkv = after(each_to_all(qkv, ZX), *gains)
    o_head, o_low, top = attend(qkv, start)
    o = each_to_all(o_low, ZX)
    (x_turned,) = local_call(
        turn_kernel, "turn", [shape((width, tokens), BF16)], [ids, x_hat], moved=4 * MIB, far=(0,)
    )

    stat = shape((8, 8, tokens))
    pieces = [shape((tokens // 2, width)), shape((tokens // 2, width), BF16)]
    wide = [shape((tokens // 2, width + 128)), shape((tokens // 2, width + 128), BF16)]
    keep, send, sums_o = local_call(
        out_kernel,
        "out",
        wide + [shape((2, tokens))],
        [ids, o, gain_o, w_out],
        [
            pltpu.VMEM((tokens, half), BF16),
            pltpu.VMEM((tokens, 128), F32),
            pltpu.VMEM((tokens, half), BF16),
            pltpu.VMEM((tokens, 128), F32),
        ],
        flops=2 * tokens * width * half,
        moved=4 * MIB,
    )
    scattered = finish_scatter(keep, send, kernel=core_sum_stats_kernel)
    r1, bb_own = local_call(
        middle_kernel,
        "middle",
        [shape((share, width)), shape((share, width), BF16)],
        scattered + [own_hidden, own_usable, prenorm] + gains,
        moved=3 * MIB,
        far=(0,),
    )

    df, dhn = local_call(
        down_back_kernel,
        "down_back",
        [shape((tokens, width), BF16), shape((tokens, units))],
        [ids] + df_parts + [after(w_down, bb_own)],
        flops=2 * tokens * width * units,
        moved=10 * MIB,
        stay=range(1, 9),
        far=(0,),
    )
    bb_parts = eight_parts(bb_own, dhn)
    bb, h, u, sums_h = local_call(
        up_kernel,
        "up",
        [shape((tokens, width), BF16), shape((tokens, units)), shape((tokens, units)), stat],
        [ids] + bb_parts + [w_up, dhn, gain_h, sums_o],
        flops=2 * tokens * width * units,
        moved=14 * MIB,
        stay=range(1, 9),
        far=(0,),
    )
    sums_h = each_to_all(sums_h, EIGHT)
    table = shape((tokens, units))
    terms = local_call(slope_kernel, "slopes", [table] * 3, [h, u, dhn, gain_h], moved=12 * MIB)
    keep, send, du = local_call(
        inner_back_kernel,
        "inner_back",
        pieces + [shape((tokens, units), BF16)],
        [ids, *terms, sums_h, w_up],
        [pltpu.VMEM((tokens, units), BF16)],
        flops=2 * tokens * width * units,
        moved=14 * MIB,
        far=(2,),
    )

    def feed_forward_grad(own):
        hn, sub_h = local_call(
            inner_norm_kernel,
            "inner_norm",
            [shape((tokens, units), BF16), shape((2, units))],
            [after(h, own), dhn, sums_h, gain_h, shift_h],
            moved=5 * MIB,
            far=(0,),
        )
        return [mlp_grad(df, hn, bb, after(du, own)), hn, sub_h]

    scattered, (g_mlp, hn, sub_h) = finish_scatter(keep, send, feed_forward_grad)
    g_mlp = lax.psum_scatter(after(g_mlp, *scattered), ZX, scatter_dimension=0, tiled=True)
    dr1, dattn_own, pre_three = local_call(
        middle_back_kernel,
        "middle_back",
        [shape((share, width)), shape((share, width), BF16), shape((2, width))],
        scattered + [r1, own_cot, own_usable, prenorm],
        moved=4 * MIB,
        far=(0,),
    )
    keep, send = local_call(
        down_kernel,
        "down",
        pieces,
        [ids, hn, w_down],
        [pltpu.VMEM((tokens, units), BF16)],
        flops=2 * tokens * width * units,
        moved=8 * MIB,
    )
    dattn_parts = eight_parts(dattn_own, keep)

    (c,) = local_call(
        lambda *refs: normed_heads_kernel(*refs, width=width),
        "normed_heads",
        [shape((tokens, half), BF16)],
        [o, sums_h, gain_o, shift_o],
        far=(0,),
    )
    dattn, dc, back_o, sub_o = local_call(
        out_back_kernel,
        "out_back",
        [shape((tokens, width), BF16), shape((half, tokens)), stat, shape((2, half))],
        [ids] + dattn_parts + [w_out, o, sums_h, gain_o],
        [pltpu.VMEM((tokens, half), F32)],
        flops=2 * tokens * width * half,
        moved=6 * MIB,
        stay=range(1, 9),
        far=(0,),
    )
    g_out = out_grad(dattn, c)
    back_o = after(each_to_all(back_o, EIGHT), g_out)
    (do,) = local_call(
        lambda *refs: head_grad_kernel(*refs, width=width),
        "head_grad",
        [shape((rows * heads, HDIM, group_slots), BF16)],
        [dc, o, sums_h, back_o, gain_o],
        moved=MIB,
    )
    f_parts = core_scatter(keep, after(send, *dattn_parts))
    do = after(each_to_all(do, ZX), x_turned, f_parts[0])
    scattered = line_scatter(*f_parts)
    dqkv = attend_back(qkv, do, o_head, top, start, tables)
    dqkv = each_to_all(after(dqkv, *scattered), ZX)

    both = 4 * half
    line = [shape((count, both), BF16) for count in (272, 272, 144, 128, 272)]
    line += [shape((count, both), BF16) for count in (256, 256, 128, 128, 256)]
    *lines, dproj = local_call(
        in_grad_kernel,
        "in_grad",
        line + [shape((tokens, 3 * half), BF16)],
        [ids, dqkv, x_turned, w_att, prenorm, g_out, pre_three, sub_o, sub_h],
        [pltpu.VMEM((3 * half, tokens), BF16), pltpu.VMEM((2, width), F32)],
        flops=2 * tokens * width * 3 * half,
        moved=13 * MIB,
        far=range(10),
    )
    first, second = ring_crossing(lines)
    mlp_keep, mlp_give, squares_mlp = local_call(
        rest_kernel,
        "rest",
        [shape((seq_slots, 2 * units), BF16)] * 2 + [shape((8, 128))],
        [ids, after(g_mlp, dproj)],
        stay=(1,),
        far=(0,),
    )
    mlp_take = lax.ppermute(mlp_give, YH, SWAP)
    keep, send = local_call(
        in_back_kernel,
        "in_back",
        pieces,
        [ids, dproj, w_att],
        [pltpu.VMEM((tokens, 3 * half), BF16)],
        flops=2 * tokens * width * 3 * half,
        moved=7 * MIB,
    )
    da_parts = finish_scatter(keep, after(send, *first[1:], *second[1:], squares_mlp))
    piece = [shape((seq_slots + 16, both))] + [shape((seq_slots + 16, both), BF16)] * 3
    piece += [shape((seq_slots, both))] + [shape((seq_slots, both), BF16)] * 3
    lines = [*local_call(
        line_sum_kernel,
        "line_sum",
        piece,
        first + second,
        moved=6 * MIB,
    )]
    first, second = crossing(lines, Z, X)
    da_parts = da_parts[:1] + [after(part, *first[1:], *second[1:]) for part in da_parts[1:]]
    (own_grad,) = local_call(
        input_back_kernel,
        "input_back",
        [shape((share, width), BF16)],
        da_parts[:1] + [after(part, mlp_take) for part in da_parts[1:]] + [own_hidden, dr1, prenorm],
        moved=3 * MIB,
    )
    own_grad = own_grad.reshape(rows, quarter, width)
    line_grad = lax.ppermute(own_grad, YL, SWAP)
    grads = [own_grad, lax.ppermute(own_grad, C, SWAP), line_grad, lax.ppermute(line_grad, C, SWAP)]
    first_line = lax.axis_index(YL) == 0
    pairs = [
        jnp.concatenate([jnp.where(first_core, a, b), jnp.where(first_core, b, a)], axis=1)
        for a, b in (grads[:2], grads[2:])
    ]
    input_grad = jnp.concatenate(
        [jnp.where(first_line, *pairs), jnp.where(first_line, *pairs[::-1])], axis=1
    )

    grad_piece = shape((seq_slots + 16, 4 * half), BF16)
    att_keep, att_give, small = local_call(
        last_sum_kernel,
        "last_sum",
        [grad_piece, grad_piece, shape((8, 8, width), BF16)],
        [ids, *first, *second, squares_mlp],
        moved=MIB,
        far=(0,),
    )
    att_take = lax.ppermute(att_give, YH, SWAP)
    mlp_take = lax.ppermute(mlp_give, YH, SWAP)
    small = each_to_all(small, EIGHT)
    small_total, squares = local_call(
        group_total_kernel,
        "group_total",
        [shape((8, width)), shape((16, 8, 128))],
        [small],
        far=(0,),
    )
    squares = each_to_all(squares, ZX)
    hidden_out = local_call(
        result_kernel,
        "result",
        [shape((share, width), BF16)],
        scattered + [after(r1, small_total), own_usable],
        moved=3 * MIB,
        stay=range(5),
    )[0].reshape(rows, quarter, width)
    turns = ((1, 0, 2), (1, 0), (0, 1, 2), (0, 2, 1), (0, 1), (1, 0, 2))
    states = [
        (inward, inward_moment, inward_squares),
        (outward, outward_moment, outward_squares),
        (upward, upward_moment, upward_squares),
        (downward, downward_moment, downward_squares),
        (prenorm, prenorm_moment, prenorm_squares),
        (subnorm, subnorm_moment, subnorm_squares),
    ]
    *updated, norm = adam(
        ids,
        small_total,
        squares,
        [att_keep, att_take, mlp_keep, mlp_take],
        [tuple(jnp.transpose(a, turn) for a in state) for state, turn in zip(states, turns)],
    )
    updated = [jnp.transpose(a, turns[n // 3]) for n, a in enumerate(updated)]
    return (hidden_out, input_grad, *updated, norm.reshape(()))


def solution(mesh):
    finer = Mesh(mesh.devices.reshape(4, 4, 2, 2, 2), SEQ_FFN)
    matrices = (P(SEQ, None, FFN),) * 3 + (P(FFN, SEQ),) * 3
    matrices += (P(SEQ, None, FFN),) * 3 + (P(None, FFN, SEQ),) * 3
    norms = (P(),) * 3 + (P(None, None, FFN),) * 3
    return jax.shard_map(
        shards,
        mesh=finer,
        in_specs=(P(None, SEQ, None), P(None, SEQ_FFN, None), P(), *matrices, *norms),
        out_specs=(P(None, SEQ_FFN, None), P(None, SEQ, None), *matrices, *norms, P()),
        check_vma=False,
    )
```
